32 devices in a mesh: fsdp: 16 (over z, y, x), ctx: 2 (over core).
Axes of the slice: x: 2, y: 2, z: 4, core: 2. Of those that a mesh axis runs over, the one named last changes fastest.
Arguments:
- tokens: bfloat16 [16, 1024, 768], P('fsdp', 'ctx'), may hold values from -6 to 6
- lengths: int32 [16], P('fsdp'), may hold values from 768 to 1024
- cotangent: bfloat16 [16, 1024, 768], P('fsdp', 'ctx'), may hold values from -6 to 6
- projection: bfloat16 [768, 2304], P('fsdp'), may hold values from -0.3125 to 0.3125
- mixing: bfloat16 [768, 768], P('fsdp'), may hold values from -0.625 to 0.625
- widening: bfloat16 [768, 3072], P('fsdp'), may hold values from -0.21875 to 0.21875
- narrowing: bfloat16 [3072, 768], P('fsdp'), may hold values from -0.15625 to 0.15625
- biases: bfloat16 [4, 768], P(None, 'fsdp'), may hold values from -1.5 to 1.5
- widen_bias: bfloat16 [3072], P('fsdp'), may hold values from -2.5 to 2.5
- norms: bfloat16 [4, 768], P(None, 'fsdp'), may hold values from -1.2 to 1.4, as said below
Outputs:
- result: bfloat16 [16, 1024, 768], P('fsdp', 'ctx')
- grad_tokens: float32 [16, 1024, 768], P('fsdp', 'ctx')
- grad_projection: float32 [768, 2304], P('fsdp')
- grad_mixing: float32 [768, 768], P('fsdp')
- grad_widening: float32 [768, 3072], P('fsdp')
- grad_narrowing: float32 [3072, 768], P('fsdp')
- grad_biases: float32 [4, 768], P(None, 'fsdp')
- grad_widen: float32 [3072], P('fsdp')
- grad_norms: float32 [4, 768], P(None, 'fsdp')
The draws below stay inside these ranges and needn't reach their ends.
Inputs may be any that keep to these rules, and one draw needn't show every extreme that they name: `norms`: rows 0 and 2 are gains near 1, rows 1 and 3 shifts near 0.
All inputs are finite; a program needn't handle non-finite values.
Results may differ from the reference program's by a relative error of at most 0.014.
The reference program's roundings to bfloat16 on the way count: a program that leaves them out, or rounds other values in their place, can miss the bound.
Values may be sent and summed in bfloat16 or wider, within the bound.
No kernel may reach another device: no remote copies, remote signals or barrier semaphores. Data moves between devices by JAX's collectives and lax.ppermute only.
A program may use at most 192 MiB of HBM per device.

```python
from functools import partial
import jax
import jax.numpy as jnp
from jax import lax

D = 768
HEADS = 12
HEAD_DIM = 64
FF = 3072
LENGTH = 1024
ROWS = 512
SEQS = 16


def draw_norms(key, part):
    key = jax.random.fold_in(key, 5)
    noise = jnp.clip(jax.random.normal(key, (4, D), jnp.float32), -4.0, 4.0)
    level = jnp.array([1.0, 0.0, 1.0, 0.0], jnp.float32)[:, None]
    spread = jnp.array([0.1, 0.3, 0.1, 0.3], jnp.float32)[:, None]
    return (level + spread * noise).astype(jnp.bfloat16)


def plant(entries, rng, least, top_value):
    place = [jax.random.randint(jax.random.fold_in(rng, axis), (), 0, length) for axis, length in enumerate(entries.shape)]
    longest = entries.shape.index(max(entries.shape))
    next_to = place[:longest] + [(place[longest] + 1) % entries.shape[longest]] + place[longest + 1:]
    return entries.at[tuple(place)].set(least).at[tuple(next_to)].set(top_value)


def levels(key, shape, pieces, least, top_value):
    loudness, own = 1.0, jax.random.fold_in(key, 6)
    for axis_at, blocks in pieces:
        draws = jnp.exp(jax.random.uniform(jax.random.fold_in(own, axis_at), (blocks,), jnp.float32, least / len(pieces), top_value / len(pieces)))
        loudness = loudness * jnp.repeat(draws, shape[axis_at] // blocks).reshape([-1 if axis == axis_at else 1 for axis in range(len(shape))])
    return loudness


def bell_draw(stream_key, extent, scale, most, pieces=(), held_as=jnp.bfloat16):
    values = scale * jax.random.normal(stream_key, extent, jnp.float32)
    if pieces:
        values = values * levels(stream_key, extent, pieces, -0.22, 0.18)
    return jnp.clip(values, -most, most).astype(held_as)


def setup_inputs(seed: int = 0) -> dict:
    keys = jax.random.split(jax.random.key(seed), 11)
    return {
        "tokens": bell_draw(keys[0], (SEQS, LENGTH, D), 1.0, 6.0, ((0, 16), (1, 2))),
        "lengths": plant(jax.random.randint(keys[1], (SEQS,), LENGTH - ROWS // 2, LENGTH + 1), jax.random.fold_in(keys[1], 1), LENGTH - ROWS // 2, LENGTH).astype(jnp.int32),
        "cotangent": bell_draw(keys[2], (SEQS, LENGTH, D), 1.0, 6.0, ((0, 16), (1, 2))),
        "projection": bell_draw(keys[3], (D, 3 * D), (D // 2) ** -0.5, 0.3125, ((0, 16),)),
        "mixing": bell_draw(keys[4], (D, D), (D // 8) ** -0.5, 0.625, ((0, 16),)),
        "widening": bell_draw(keys[5], (D, FF), D ** -0.5, 0.21875, ((0, 16),)),
        "narrowing": bell_draw(keys[6], (FF, D), (FF // 2) ** -0.5, 0.15625, ((0, 16),)),
        "biases": bell_draw(keys[7], (4, D), 0.3, 1.5, ((1, 16),)),
        "widen_bias": bell_draw(keys[8], (FF,), 0.5, 2.5, ((0, 16),)),
        "norms": draw_norms(jax.random.fold_in(keys[10], 71), 0),
    }


EPSILON = 1e-12

@jax.custom_vjp
def low(v):
    return lax.optimization_barrier(v.astype(jnp.bfloat16)).astype(jnp.float32)

@jax.custom_vjp
def low_back(v):
    return v

def low_keep(v):
    return (low(v), None)

def low_pass(kept, grad):
    return (grad,)

def back_keep(v):
    return (v, None)

def back_low(kept, grad):
    return (low(grad),)
low.defvjp(low_keep, low_pass)
low_back.defvjp(back_keep, back_low)

def product(spec, left_side, right_side):
    return jnp.einsum(spec, left_side, right_side, precision=lax.Precision.HIGHEST)

def layer_norm(hidden, gain, shift):
    row_mean = lax.optimization_barrier(jnp.mean(hidden, axis=-1, keepdims=True))
    centred = hidden - row_mean
    variance = lax.optimization_barrier(jnp.mean(centred * centred, axis=-1, keepdims=True))
    return centred * lax.rsqrt(variance + EPSILON) * gain + shift

def sequence_forward(params, inputs, seq_length):
    projection, mixing, widening, narrowing, biases, widen_bias, norms = params
    row_count = inputs.shape[0]
    model_width = inputs.shape[1]
    head_shape = (row_count, HEADS, HEAD_DIM)
    joined_rows = product('rd,de->re', inputs, projection)
    queries = low_back(low(joined_rows[:, :model_width] + biases[0]))
    key_rows = low_back(low(joined_rows[:, model_width:2 * model_width]))
    value_rows = low_back(low(joined_rows[:, 2 * model_width:] + biases[1]))
    scores = low_back(product('ahd,bhd->hab', queries.reshape(head_shape), key_rows.reshape(head_shape)) * HEAD_DIM ** (-0.5))
    key_valid = jnp.arange(row_count) < seq_length
    scores = jnp.where(key_valid[None, None, :], scores, -1e+30)
    probability = low(jax.nn.softmax(scores, axis=-1))
    mixed_rows = product('hab,bhd->ahd', probability, value_rows.reshape(head_shape))
    mixed_rows = low_back(low(mixed_rows.reshape(row_count, model_width)))
    branch = low_back(product('ad,de->ae', mixed_rows, mixing) + biases[2])
    first_norm = layer_norm(inputs + branch, norms[0], norms[1])
    expanded = low_back(product('ad,df->af', low(first_norm), widening) + widen_bias)
    activated = low(jax.nn.gelu(expanded, approximate=False))
    second = low_back(product('af,fd->ad', activated, narrowing) + biases[3])
    return layer_norm(first_norm + second, norms[2], norms[3])

def reference(tokens, lengths, cotangent, projection, mixing, widening, narrowing, biases, widen_bias, norms):
    params = (projection.astype(jnp.float32), mixing.astype(jnp.float32), widening.astype(jnp.float32), narrowing.astype(jnp.float32), biases.astype(jnp.float32), widen_bias.astype(jnp.float32), norms.astype(jnp.float32))
    inputs = tokens.astype(jnp.float32)

    def whole_layer(params, inputs):
        seq_block = jax.checkpoint(partial(sequence_forward, params))
        return lax.map(lambda sample: seq_block(sample[0], sample[1]), (inputs, lengths))
    result, pullback = jax.vjp(whole_layer, params, inputs)
    gradients, grad_tokens = pullback(cotangent.astype(jnp.float32))
    return (result.astype(jnp.bfloat16), grad_tokens, gradients[0], gradients[1], gradients[2], gradients[3], gradients[4], gradients[5], gradients[6])
```

```python
import functools

import jax
import jax.numpy as jnp
from jax import lax
from jax.experimental import pallas as pl
from jax.experimental.pallas import tpu as pltpu
from jax.sharding import PartitionSpec as P

HEADS = 12
HEAD_DIM = 64


EPSILON = 1e-12


def split_heads(matrix):
    return matrix.reshape(matrix.shape[0], HEADS, matrix.shape[1] // HEADS)


def pair_scores(left_rows, right_rows, factor):
    return (
        jnp.einsum(
            "ahd,bhd->hab",
            split_heads(left_rows),
            split_heads(right_rows),
            preferred_element_type=jnp.float32,
        )
        * factor
    )


def spread_rows(weights_hab, right_rows):
    out_rows = jnp.einsum(
        "hab,bhd->ahd", weights_hab, split_heads(right_rows), preferred_element_type=jnp.float32
    )
    return out_rows.reshape(out_rows.shape[0], -1)


def collect_rows(weights_hab, left_rows):
    out_rows = jnp.einsum(
        "hab,ahd->bhd", weights_hab, split_heads(left_rows), preferred_element_type=jnp.float32
    )
    return out_rows.reshape(out_rows.shape[0], -1)


def norm_forward(hidden, gain, shift):
    row_mean = jnp.mean(hidden, axis=-1, keepdims=True)
    centred = hidden - row_mean
    inverse = lax.rsqrt(jnp.mean(centred * centred, axis=-1, keepdims=True) + EPSILON)
    normed = centred * inverse
    return (normed * gain + shift, normed, inverse)


def norm_backward(upstream, normed, inverse, gain):
    inner = upstream * gain
    return inverse * (
        inner
        - jnp.mean(inner, axis=-1, keepdims=True)
        - normed * jnp.mean(inner * normed, axis=-1, keepdims=True)
    )


def gelu_exact(values_in):
    return jax.nn.gelu(values_in, approximate=False)


def general_body(
    tokens, lengths, cotangent, projection, mixing, widening, narrowing, biases, widen_bias, norms
):
    score_scale = HEAD_DIM ** (-0.5)
    gathered = (
        lax.all_gather(projection, "fsdp", axis=0, tiled=True),
        lax.all_gather(mixing, "fsdp", axis=0, tiled=True),
        lax.all_gather(widening, "fsdp", axis=0, tiled=True),
        lax.all_gather(narrowing, "fsdp", axis=0, tiled=True),
        lax.all_gather(biases, "fsdp", axis=1, tiled=True),
        lax.all_gather(widen_bias, "fsdp", axis=0, tiled=True),
        lax.all_gather(norms, "fsdp", axis=1, tiled=True),
    )
    w_project, w_mixing, w_widen, w_narrow, bias_rows, widen_all, norm_rows = gathered
    bias_float = bias_rows.astype(jnp.float32)
    widen_float = widen_all.astype(jnp.float32)
    norm_float = norm_rows.astype(jnp.float32)
    inputs = tokens[0]
    row_count, model_width = inputs.shape
    seq_length = lengths[0]
    joined_rows = jnp.dot(inputs, w_project, preferred_element_type=jnp.float32)
    queries = (joined_rows[:, :model_width] + bias_float[0]).astype(jnp.bfloat16)
    key_rows = joined_rows[:, model_width : 2 * model_width].astype(jnp.bfloat16)
    value_rows = (joined_rows[:, 2 * model_width :] + bias_float[1]).astype(jnp.bfloat16)
    all_keys, all_values = (
        lax.all_gather(key_rows, "ctx", axis=0, tiled=True),
        lax.all_gather(value_rows, "ctx", axis=0, tiled=True),
    )
    key_valid = jnp.arange(all_keys.shape[0], dtype=jnp.int32) < seq_length
    scores = jnp.where(key_valid[None, None, :], pair_scores(queries, all_keys, score_scale), -1e30)
    row_peak = jnp.max(scores, axis=-1, keepdims=True)
    exp_terms = jnp.exp(scores - row_peak)
    summed = jnp.sum(exp_terms, axis=-1, keepdims=True)
    prob_low = (exp_terms / summed).astype(jnp.bfloat16)
    logsum = row_peak + jnp.log(summed)
    mixed_low = spread_rows(prob_low, all_values).astype(jnp.bfloat16)
    branch = jnp.dot(mixed_low, w_mixing, preferred_element_type=jnp.float32) + bias_float[2]
    first_norm, normed_one, inverse_one = norm_forward(
        inputs.astype(jnp.float32) + branch, norm_float[0], norm_float[1]
    )
    first_low = first_norm.astype(jnp.bfloat16)
    expanded = jnp.dot(first_low, w_widen, preferred_element_type=jnp.float32) + widen_float
    activated, gelu_pull = jax.vjp(gelu_exact, expanded)
    active_low = activated.astype(jnp.bfloat16)
    second = jnp.dot(active_low, w_narrow, preferred_element_type=jnp.float32) + bias_float[3]
    result, normed_two, inverse_two = norm_forward(
        first_norm + second, norm_float[2], norm_float[3]
    )
    grad_out = cotangent[0].astype(jnp.float32)
    grad_two = norm_backward(grad_out, normed_two, inverse_two, norm_float[2])
    second_grad = grad_two.astype(jnp.bfloat16)
    narrow_term = jnp.einsum(
        "rf,rd->fd", active_low, second_grad, preferred_element_type=jnp.float32
    )
    active_grad = jnp.einsum("rd,fd->rf", second_grad, w_narrow, preferred_element_type=jnp.float32)
    expand_grad = gelu_pull(active_grad)[0].astype(jnp.bfloat16)
    widen_term = jnp.einsum("rd,rf->df", first_low, expand_grad, preferred_element_type=jnp.float32)
    first_grad = grad_two + jnp.einsum(
        "rf,df->rd", expand_grad, w_widen, preferred_element_type=jnp.float32
    )
    grad_one = norm_backward(first_grad, normed_one, inverse_one, norm_float[0])
    branch_grad = grad_one.astype(jnp.bfloat16)
    mixing_term = jnp.einsum(
        "rd,re->de", mixed_low, branch_grad, preferred_element_type=jnp.float32
    )
    mixed_grad = jnp.einsum(
        "re,de->rd", branch_grad, w_mixing, preferred_element_type=jnp.float32
    ).astype(jnp.bfloat16)
    scores = jnp.where(key_valid[None, None, :], pair_scores(queries, all_keys, score_scale), -1e30)
    prob_again = jnp.exp(scores - logsum)
    prob_grad = pair_scores(mixed_grad, all_values, 1.0)
    row_delta = jnp.sum(prob_again * prob_grad, axis=-1, keepdims=True)
    score_grad = (prob_again * (prob_grad - row_delta)).astype(jnp.bfloat16)
    query_grad = (spread_rows(score_grad, all_keys) * score_scale).astype(jnp.bfloat16)
    key_terms = collect_rows(score_grad, queries) * score_scale
    value_terms = collect_rows(prob_low, mixed_grad)
    key_grad, value_grad = (
        lax.psum_scatter(key_terms, "ctx", scatter_dimension=0, tiled=True),
        lax.psum_scatter(value_terms, "ctx", scatter_dimension=0, tiled=True),
    )
    key_low = key_grad.astype(jnp.bfloat16)
    value_low = value_grad.astype(jnp.bfloat16)
    joined_grad = jnp.concatenate([query_grad, key_low, value_low], axis=1)
    project_term = jnp.einsum("rd,re->de", inputs, joined_grad, preferred_element_type=jnp.float32)
    input_grad = (
        jnp.einsum("re,de->rd", joined_grad, w_project, preferred_element_type=jnp.float32)
        + grad_one
    )
    bias_terms = jnp.stack(
        [
            jnp.sum(query_grad.astype(jnp.float32), axis=0),
            jnp.sum(value_low.astype(jnp.float32), axis=0),
            jnp.sum(branch_grad.astype(jnp.float32), axis=0),
            jnp.sum(second_grad.astype(jnp.float32), axis=0),
        ]
    )
    widen_terms = jnp.sum(expand_grad.astype(jnp.float32), axis=0)
    norm_terms = jnp.stack(
        [
            jnp.sum(first_grad * normed_one, axis=0),
            jnp.sum(first_grad, axis=0),
            jnp.sum(grad_out * normed_two, axis=0),
            jnp.sum(grad_out, axis=0),
        ]
    )
    shares = (
        lax.psum_scatter(project_term, "fsdp", scatter_dimension=0, tiled=True),
        lax.psum_scatter(mixing_term, "fsdp", scatter_dimension=0, tiled=True),
        lax.psum_scatter(widen_term, "fsdp", scatter_dimension=0, tiled=True),
        lax.psum_scatter(narrow_term, "fsdp", scatter_dimension=0, tiled=True),
        lax.psum_scatter(bias_terms, "fsdp", scatter_dimension=1, tiled=True),
        lax.psum_scatter(widen_terms, "fsdp", scatter_dimension=0, tiled=True),
        lax.psum_scatter(norm_terms, "fsdp", scatter_dimension=1, tiled=True),
    )
    totals = lax.psum(
        (shares[0], shares[1], shares[2], shares[3], shares[4], shares[5], shares[6]), "ctx"
    )
    return (
        result.astype(jnp.bfloat16)[None],
        input_grad[None],
        totals[0],
        totals[1],
        totals[2],
        totals[3],
        totals[4],
        totals[5],
        totals[6],
    )


NT=(((1,),(1,)),((),()))
NN=(((1,),(0,)),((),()))
def dotf(a,b,dims): return lax.dot_general(a,b,dims,preferred_element_type=jnp.float32)

def attn_fwd_kernel(len_ref,q_ref,k_ref,v_ref,o_ref,lse_ref,vt_ref):
    @pl.when(pl.program_id(1)==0)
    def _():
        vt_ref[...]=v_ref[...].T
    n=len_ref[0]
    q=q_ref[...]; k=k_ref[...]
    lanes=lax.broadcasted_iota(jnp.int32,q.shape,1)
    rows=lax.broadcasted_iota(jnp.int32,(k.shape[0],1),0)
    valid=rows<n
    outs = []
    for h in range(2):
        qh=jnp.where((lanes>=64)==(h==1),q*jnp.bfloat16(HEAD_DIM**-0.5),jnp.bfloat16(0))
        s=dotf(k,qh,NT)
        s=jnp.where(valid,s,-1e30)
        m=jnp.max(s,axis=0,keepdims=True)
        e=jnp.exp(s-m)
        l=jnp.sum(e,axis=0,keepdims=True)
        p=(e*(1.0/l)).astype(jnp.bfloat16)
        lse_ref[0,h:h+1,:]=m+jnp.log(l)
        outs.append(dotf(vt_ref[64*h:64*h+64,:],p,NN))
    o=jnp.concatenate(outs,axis=0)
    o_ref[...]=o.T.astype(jnp.bfloat16)

def attn_fwd(length, joined, QB=512):
    L = joined.shape[0]
    C = joined.shape[1] // 3
    pairs = C // 128
    QB = min(QB, L)
    return pl.pallas_call(
        attn_fwd_kernel,
        grid=(pairs, L // QB),
        in_specs=[
            pl.BlockSpec(memory_space=pltpu.SMEM),
            pl.BlockSpec((QB, 128), lambda p, i: (i, p)),
            pl.BlockSpec((L, 128), lambda p, i: (0, pairs + p)),
            pl.BlockSpec((L, 128), lambda p, i: (0, 2 * pairs + p)),
        ],
        out_specs=[
            pl.BlockSpec((QB, 128), lambda p, i: (i, p)),
            pl.BlockSpec((1, 2, QB), lambda p, i: (p, 0, i)),
        ],
        out_shape=[
            jax.ShapeDtypeStruct((L, C), jnp.bfloat16),
            jax.ShapeDtypeStruct((pairs, 2, L), jnp.float32),
        ],
        scratch_shapes=[pltpu.VMEM((128, L), jnp.bfloat16)],
        compiler_params=pltpu.CompilerParams(vmem_limit_bytes=48 * 2**20),
        name="attn_fwd",
    )(length, joined, joined, joined)


def attn_bwd_kernel(len_ref,q_ref,k_ref,v_ref,do_ref,lse_ref,dq_ref,dk_ref,dv_ref,kt_ref,dka_ref,dva_ref):
    i=pl.program_id(1)
    @pl.when(i==0)
    def _():
        kt_ref[...]=k_ref[...].T
        dka_ref[...]=jnp.zeros_like(dka_ref)
        dva_ref[...]=jnp.zeros_like(dva_ref)
    n=len_ref[0]
    scale=jnp.bfloat16(HEAD_DIM**-0.5)
    q=q_ref[...]; k=k_ref[...]; v=v_ref[...]; do=do_ref[...]
    lanes=lax.broadcasted_iota(jnp.int32,q.shape,1)
    rows=lax.broadcasted_iota(jnp.int32,(k.shape[0],1),0)
    valid=rows<n
    outs = []
    for h in range(2):
        mine=(lanes>=64)==(h==1)
        qh=jnp.where(mine,q*scale,jnp.bfloat16(0))
        doh=jnp.where(mine,do,jnp.bfloat16(0))
        s=dotf(k,qh,NT)
        p=jnp.where(valid,jnp.exp(s-lse_ref[0,h:h+1,:]),0.0)
        dp=dotf(v,doh,NT)
        delta=jnp.sum(p*dp,axis=0,keepdims=True)
        ds=(p*(dp-delta)).astype(jnp.bfloat16)
        dva_ref[...]+=dotf(p.astype(jnp.bfloat16),doh,NN)
        dka_ref[...]+=dotf(ds,qh,NN)
        outs.append(dotf(kt_ref[64*h:64*h+64,:],ds,NN))
    dq=jnp.concatenate(outs,axis=0)*(HEAD_DIM**-0.5)
    dq_ref[...]=dq.T.astype(jnp.bfloat16)
    @pl.when(i==pl.num_programs(1)-1)
    def _():
        dk_ref[...]=dka_ref[...].astype(jnp.bfloat16)
        dv_ref[...]=dva_ref[...].astype(jnp.bfloat16)

def attn_bwd(length, joined, do, lse, QB=512):
    L = joined.shape[0]
    C = joined.shape[1] // 3
    pairs = C // 128
    QB = min(QB, L)
    block = lambda at: pl.BlockSpec((QB, 128), lambda p, i: (i, at * pairs + p))
    whole = lambda at: pl.BlockSpec((L, 128), lambda p, i: (0, at * pairs + p))
    return pl.pallas_call(
        attn_bwd_kernel,
        grid=(pairs, L // QB),
        in_specs=[
            pl.BlockSpec(memory_space=pltpu.SMEM),
            block(0),
            whole(1),
            whole(2),
            block(0),
            pl.BlockSpec((1, 2, QB), lambda p, i: (p, 0, i)),
        ],
        out_specs=[block(0), whole(0), whole(0)],
        out_shape=[jax.ShapeDtypeStruct((L, C), jnp.bfloat16)] * 3,
        scratch_shapes=[
            pltpu.VMEM((128, L), jnp.bfloat16),
            pltpu.VMEM((L, 128), jnp.float32),
            pltpu.VMEM((L, 128), jnp.float32),
        ],
        compiler_params=pltpu.CompilerParams(vmem_limit_bytes=48 * 2**20),
        name="attn_bwd",
    )(length, joined, joined, joined, do, lse)


AXES = ("fsdp", "ctx")


def core_permute(value, chips):
    pairs = [(2 * f + c, 2 * f + 1 - c) for f in range(chips) for c in range(2)]
    return lax.ppermute(value, AXES, pairs)


def chip_permute(value, chips, mask):
    pairs = [(2 * f + c, 2 * (f ^ mask) + c) for f in range(chips) for c in range(2)]
    return lax.ppermute(value, AXES, pairs)


def chip_bit(mask):
    return (lax.axis_index("fsdp") // mask) % 2


def by_core(mine, other, axis):
    core = lax.axis_index("ctx")
    first = jnp.where(core == 0, mine, other)
    second = jnp.where(core == 0, other, mine)
    return jnp.concatenate([first, second], axis=axis)


def dims_of(chips):
    return [1 << b for b in reversed(range(chips.bit_length() - 1))]


def gather_step(value, chips, mask):
    axis = dims_of(chips).index(mask)
    other = chip_permute(value, chips, mask)
    bit = chip_bit(mask)
    first = jnp.where(bit == 0, value, other)
    second = jnp.where(bit == 0, other, value)
    return jnp.concatenate([first, second], axis=axis)


def scatter_send(value, chips, mask):
    axis = dims_of(chips).index(mask)
    send = lax.dynamic_index_in_dim(value, 1 - chip_bit(mask), axis, keepdims=True)
    return chip_permute(send.astype(jnp.bfloat16), chips, mask)


def scatter_step(value, chips, mask):
    axis = dims_of(chips).index(mask)
    other = scatter_send(value, chips, mask)
    keep = lax.dynamic_index_in_dim(value, chip_bit(mask), axis, keepdims=True)
    return keep.astype(jnp.float32) + other.astype(jnp.float32)


def scatter_chips(value, chips, masks):
    rows, columns = value.shape[1:]
    value = value.reshape([2] * len(dims_of(chips)) + [rows, columns])
    for mask in masks:
        value = scatter_step(value, chips, mask)
    return value.reshape(rows, columns)


def core_half(value, axis, own):
    core = lax.axis_index("ctx")
    size = value.shape[axis] // 2
    which = core if own else 1 - core
    return lax.dynamic_slice_in_dim(value, which * size, size, axis)


def core_scatter(value):
    chips = lax.axis_size("fsdp")
    other = core_permute(core_half(value, 1, False), chips)
    return core_half(value, 1, True).astype(jnp.float32) + other.astype(jnp.float32)


def fast_body(
    tokens, lengths, cotangent, projection, mixing, widening, narrowing, biases, widen_bias, norms
):
    chips = lax.axis_size("fsdp")
    core = lax.axis_index("ctx")
    bits = dims_of(chips)
    far = bits[:-2]
    by_x = far + [1, 2]
    by_y = far + [2, 1]
    down_x = by_y[::-1]
    down_y = by_x[::-1]
    inputs = tokens[0]
    row_count, model_width = inputs.shape
    shard = projection.shape[0]
    half = model_width // 2

    w_rest = jnp.concatenate(
        [mixing] + [widening[:, i * model_width : (i + 1) * model_width] for i in range(widening.shape[1] // model_width)],
        axis=0,
    )
    rest_rows = (w_rest.shape[0], narrowing.shape[0])
    mine = jnp.concatenate([core_half(w_rest, 0, True), core_half(narrowing, 0, True)], axis=0)
    gathered = lax.all_gather(mine, AXES, axis=0)
    gathered = gathered.reshape(chips, 2, mine.shape[0], model_width)
    first_rows = rest_rows[0] // 2
    w_rest = gathered[:, :, :first_rows].reshape(chips, rest_rows[0], model_width)
    w_mixing = w_rest[:, :shard].reshape(model_width, model_width)
    w_widen = jnp.concatenate(
        [w_rest[:, i : i + shard].reshape(model_width, model_width) for i in range(shard, rest_rows[0], shard)], axis=1
    )
    w_narrow = gathered[:, :, first_rows:].reshape(chips * rest_rows[1], model_width)

    own = projection.reshape(shard, 3, 2, half)
    own = lax.dynamic_index_in_dim(own, core, 2, keepdims=False).reshape(shard, 3 * half)
    small = jnp.concatenate([biases.reshape(-1), widen_bias, norms.reshape(-1)])
    small_count = small.shape[0]
    small = jnp.pad(small, (0, shard * 128 - small_count)).reshape(shard, 128)
    packed = jnp.concatenate([own, small], axis=1)
    packed = packed.reshape([1] * len(bits) + [shard, packed.shape[1]])
    for mask in far:
        packed = gather_step(packed, chips, mask)
    cut = packed.shape[-1] // 2
    left, right = packed[..., :cut], packed[..., cut:]
    left, right = gather_step(left, chips, 1), gather_step(right, chips, 2)
    left, right = gather_step(left, chips, 2), gather_step(right, chips, 1)
    left = left.reshape(model_width, cut)
    right = right.reshape(model_width, cut)
    w_own = jnp.concatenate([left, right[:, : 3 * half - cut]], axis=1)
    small = right[:, 3 * half - cut :].reshape(chips, shard * 128)[:, :small_count].astype(jnp.float32)
    bias_float = small[:, : 4 * shard].reshape(chips, 4, shard).transpose(1, 0, 2).reshape(4, model_width)
    widen_float = small[:, 4 * shard : 4 * shard + widen_bias.shape[0]].reshape(-1)
    norm_float = small[:, small_count - 4 * shard :].reshape(chips, 4, shard).transpose(1, 0, 2).reshape(4, model_width)

    all_inputs = by_core(inputs, core_permute(inputs, chips), 0)
    bias_own = lax.dynamic_slice_in_dim(bias_float, core * half, half, 1)
    bias_joined = jnp.concatenate([bias_own[0], jnp.zeros_like(bias_own[0]), bias_own[1]])
    joined = (jnp.dot(all_inputs, w_own, preferred_element_type=jnp.float32) + bias_joined).astype(jnp.bfloat16)
    mixed_own, logsum = attn_fwd(lengths, joined)
    mixed_mine = core_half(mixed_own, 0, True)
    mixed_low = by_core(mixed_mine, core_permute(core_half(mixed_own, 0, False), chips), 1)

    branch = jnp.dot(mixed_low, w_mixing, preferred_element_type=jnp.float32) + bias_float[2]
    first_norm, normed_one, inverse_one = norm_forward(
        inputs.astype(jnp.float32) + branch, norm_float[0], norm_float[1]
    )
    first_low = first_norm.astype(jnp.bfloat16)
    expanded = jnp.dot(first_low, w_widen, preferred_element_type=jnp.float32) + widen_float
    activated, gelu_pull = jax.vjp(gelu_exact, expanded)
    active_low = activated.astype(jnp.bfloat16)
    second = jnp.dot(active_low, w_narrow, preferred_element_type=jnp.float32) + bias_float[3]
    result, normed_two, inverse_two = norm_forward(
        first_norm + second, norm_float[2], norm_float[3]
    )
    grad_out = cotangent[0].astype(jnp.float32)
    grad_two = norm_backward(grad_out, normed_two, inverse_two, norm_float[2])
    second_grad = grad_two.astype(jnp.bfloat16)
    narrow_term = jnp.einsum(
        "rf,rd->fd", active_low, second_grad, preferred_element_type=jnp.float32
    ).astype(jnp.bfloat16)
    narrow_share = scatter_chips(
        core_scatter(narrow_term).reshape(chips, narrowing.shape[0], half), chips, down_x
    )
    active_grad = jnp.einsum("rd,fd->rf", second_grad, w_narrow, preferred_element_type=jnp.float32)
    expand_grad = gelu_pull(active_grad)[0].astype(jnp.bfloat16)
    widen_term = jnp.einsum(
        "rd,rf->df", first_low, expand_grad, preferred_element_type=jnp.float32
    ).astype(jnp.bfloat16)
    widen_share = scatter_chips(
        core_scatter(widen_term).reshape(chips, shard, widening.shape[1] // 2), chips, down_y
    )
    first_grad = grad_two + jnp.einsum(
        "rf,df->rd", expand_grad, w_widen, preferred_element_type=jnp.float32
    )
    grad_one = norm_backward(first_grad, normed_one, inverse_one, norm_float[0])
    branch_grad = grad_one.astype(jnp.bfloat16)
    mixed_grad = jnp.einsum(
        "re,de->rd", branch_grad, w_mixing, preferred_element_type=jnp.float32
    ).astype(jnp.bfloat16)
    mixing_term = jnp.einsum(
        "rd,re->de", mixed_low, branch_grad, preferred_element_type=jnp.float32
    ).astype(jnp.bfloat16)
    mixing_share = scatter_chips(
        core_scatter(mixing_term).reshape(chips, shard, half), chips, down_y
    )
    grad_own = by_core(
        core_half(mixed_grad, 1, True), core_permute(core_half(mixed_grad, 1, False), chips), 0
    )
    query_grad, key_grad, value_grad = attn_bwd(lengths, joined, grad_own, logsum)
    joined_grad = jnp.concatenate([query_grad, key_grad, value_grad], axis=1)

    query_bias = jnp.sum(query_grad.astype(jnp.float32), axis=0)
    value_bias = jnp.sum(value_grad.astype(jnp.float32), axis=0)
    zero_bias = jnp.zeros_like(query_bias)
    bias_terms = jnp.stack(
        [
            by_core(query_bias, zero_bias, 0),
            by_core(value_bias, zero_bias, 0),
            jnp.sum(branch_grad.astype(jnp.float32), axis=0),
            jnp.sum(second_grad.astype(jnp.float32), axis=0),
        ]
    )
    widen_terms = jnp.sum(expand_grad.astype(jnp.float32), axis=0)
    norm_terms = jnp.stack(
        [
            jnp.sum(first_grad * normed_one, axis=0),
            jnp.sum(first_grad, axis=0),
            jnp.sum(grad_out * normed_two, axis=0),
            jnp.sum(grad_out, axis=0),
        ]
    )
    per_chip = lambda terms: terms.reshape(4, chips, shard).transpose(1, 0, 2).reshape(chips, 4 * shard)
    small_terms = jnp.concatenate(
        [per_chip(bias_terms), widen_terms.reshape(chips, -1), per_chip(norm_terms)], axis=1
    )
    small_terms = small_terms + core_permute(small_terms, chips)
    small_terms = jnp.pad(small_terms, ((0, 0), (0, shard * 128 - small_count)))
    small_terms = small_terms.reshape(model_width, 128).astype(jnp.bfloat16)

    project_term = jnp.einsum(
        "rd,re->de", all_inputs, joined_grad, preferred_element_type=jnp.float32
    ).astype(jnp.bfloat16)
    left_share = scatter_chips(
        project_term[:, :cut].reshape(chips, shard, cut), chips, down_x
    )
    right_term = jnp.concatenate([project_term[:, cut:], small_terms], axis=1)
    right_share = scatter_chips(right_term.reshape(chips, shard, cut), chips, down_y)
    small_share = right_share[:, 3 * half - cut :].reshape(-1)[:small_count]
    project_share = jnp.concatenate([left_share, right_share[:, : 3 * half - cut]], axis=1)

    input_part = jnp.einsum("re,de->rd", joined_grad, w_own, preferred_element_type=jnp.float32)
    input_grad = (
        core_half(input_part, 0, True) + core_permute(core_half(input_part, 0, False), chips) + grad_one
    )

    other_share = core_permute(project_share, chips)
    grad_projection = by_core(
        project_share.reshape(shard, 3, 1, half), other_share.reshape(shard, 3, 1, half), 2
    ).reshape(shard, 6 * half)
    join = lambda share: by_core(share, core_permute(share, chips), 1)
    return (
        result.astype(jnp.bfloat16)[None],
        input_grad[None],
        grad_projection,
        join(mixing_share),
        join(widen_share),
        join(narrow_share),
        small_share[: 4 * shard].reshape(4, shard),
        small_share[4 * shard : 4 * shard + widen_bias.shape[0]],
        small_share[small_count - 4 * shard :].reshape(4, shard),
    )


def solution(mesh):
    in_specs = (
        P("fsdp", "ctx", None),
        P("fsdp"),
        P("fsdp", "ctx", None),
        P("fsdp", None),
        P("fsdp", None),
        P("fsdp", None),
        P("fsdp", None),
        P(None, "fsdp"),
        P("fsdp"),
        P(None, "fsdp"),
    )
    out_specs = (
        P("fsdp", "ctx", None),
        P("fsdp", "ctx", None),
        P("fsdp", None),
        P("fsdp", None),
        P("fsdp", None),
        P("fsdp", None),
        P(None, "fsdp"),
        P("fsdp"),
        P(None, "fsdp"),
    )
    chips = mesh.shape["fsdp"]
    paired = mesh.shape["ctx"] == 2 and chips >= 4 and chips & (chips - 1) == 0
    body = fast_body if paired else general_body
    return jax.shard_map(body, mesh=mesh, in_specs=in_specs, out_specs=out_specs, check_vma=False)
```

```python
import functools

import jax
import jax.numpy as jnp
from jax import lax
from jax.experimental import pallas as pl
from jax.experimental.pallas import tpu as pltpu
from jax.sharding import PartitionSpec as P

HEADS = 12
HEAD_DIM = 64


EPSILON = 1e-12


def split_heads(matrix):
    return matrix.reshape(matrix.shape[0], HEADS, matrix.shape[1] // HEADS)


def pair_scores(left_rows, right_rows, factor):
    return (
        jnp.einsum(
            "ahd,bhd->hab",
            split_heads(left_rows),
            split_heads(right_rows),
            preferred_element_type=jnp.float32,
        )
        * factor
    )


def spread_rows(weights_hab, right_rows):
    out_rows = jnp.einsum(
        "hab,bhd->ahd", weights_hab, split_heads(right_rows), preferred_element_type=jnp.float32
    )
    return out_rows.reshape(out_rows.shape[0], -1)


def collect_rows(weights_hab, left_rows):
    out_rows = jnp.einsum(
        "hab,ahd->bhd", weights_hab, split_heads(left_rows), preferred_element_type=jnp.float32
    )
    return out_rows.reshape(out_rows.shape[0], -1)


def norm_forward(hidden, gain, shift):
    row_mean = jnp.mean(hidden, axis=-1, keepdims=True)
    centred = hidden - row_mean
    inverse = lax.rsqrt(jnp.mean(centred * centred, axis=-1, keepdims=True) + EPSILON)
    normed = centred * inverse
    return (normed * gain + shift, normed, inverse)


def norm_backward(upstream, normed, inverse, gain):
    inner = upstream * gain
    return inverse * (
        inner
        - jnp.mean(inner, axis=-1, keepdims=True)
        - normed * jnp.mean(inner * normed, axis=-1, keepdims=True)
    )


def gelu_exact(values_in):
    return jax.nn.gelu(values_in, approximate=False)


def general_body(
    tokens, lengths, cotangent, projection, mixing, widening, narrowing, biases, widen_bias, norms
):
    score_scale = HEAD_DIM ** (-0.5)
    gathered = (
        lax.all_gather(projection, "fsdp", axis=0, tiled=True),
        lax.all_gather(mixing, "fsdp", axis=0, tiled=True),
        lax.all_gather(widening, "fsdp", axis=0, tiled=True),
        lax.all_gather(narrowing, "fsdp", axis=0, tiled=True),
        lax.all_gather(biases, "fsdp", axis=1, tiled=True),
        lax.all_gather(widen_bias, "fsdp", axis=0, tiled=True),
        lax.all_gather(norms, "fsdp", axis=1, tiled=True),
    )
    w_project, w_mixing, w_widen, w_narrow, bias_rows, widen_all, norm_rows = gathered
    bias_float = bias_rows.astype(jnp.float32)
    widen_float = widen_all.astype(jnp.float32)
    norm_float = norm_rows.astype(jnp.float32)
    inputs = tokens[0]
    row_count, model_width = inputs.shape
    seq_length = lengths[0]
    joined_rows = jnp.dot(inputs, w_project, preferred_element_type=jnp.float32)
    queries = (joined_rows[:, :model_width] + bias_float[0]).astype(jnp.bfloat16)
    key_rows = joined_rows[:, model_width : 2 * model_width].astype(jnp.bfloat16)
    value_rows = (joined_rows[:, 2 * model_width :] + bias_float[1]).astype(jnp.bfloat16)
    all_keys, all_values = (
        lax.all_gather(key_rows, "ctx", axis=0, tiled=True),
        lax.all_gather(value_rows, "ctx", axis=0, tiled=True),
    )
    key_valid = jnp.arange(all_keys.shape[0], dtype=jnp.int32) < seq_length
    scores = jnp.where(key_valid[None, None, :], pair_scores(queries, all_keys, score_scale), -1e30)
    row_peak = jnp.max(scores, axis=-1, keepdims=True)
    exp_terms = jnp.exp(scores - row_peak)
    summed = jnp.sum(exp_terms, axis=-1, keepdims=True)
    prob_low = (exp_terms / summed).astype(jnp.bfloat16)
    logsum = row_peak + jnp.log(summed)
    mixed_low = spread_rows(prob_low, all_values).astype(jnp.bfloat16)
    branch = jnp.dot(mixed_low, w_mixing, preferred_element_type=jnp.float32) + bias_float[2]
    first_norm, normed_one, inverse_one = norm_forward(
        inputs.astype(jnp.float32) + branch, norm_float[0], norm_float[1]
    )
    first_low = first_norm.astype(jnp.bfloat16)
    expanded = jnp.dot(first_low, w_widen, preferred_element_type=jnp.float32) + widen_float
    activated, gelu_pull = jax.vjp(gelu_exact, expanded)
    active_low = activated.astype(jnp.bfloat16)
    second = jnp.dot(active_low, w_narrow, preferred_element_type=jnp.float32) + bias_float[3]
    result, normed_two, inverse_two = norm_forward(
        first_norm + second, norm_float[2], norm_float[3]
    )
    grad_out = cotangent[0].astype(jnp.float32)
    grad_two = norm_backward(grad_out, normed_two, inverse_two, norm_float[2])
    second_grad = grad_two.astype(jnp.bfloat16)
    narrow_term = jnp.einsum(
        "rf,rd->fd", active_low, second_grad, preferred_element_type=jnp.float32
    )
    active_grad = jnp.einsum("rd,fd->rf", second_grad, w_narrow, preferred_element_type=jnp.float32)
    expand_grad = gelu_pull(active_grad)[0].astype(jnp.bfloat16)
    widen_term = jnp.einsum("rd,rf->df", first_low, expand_grad, preferred_element_type=jnp.float32)
    first_grad = grad_two + jnp.einsum(
        "rf,df->rd", expand_grad, w_widen, preferred_element_type=jnp.float32
    )
    grad_one = norm_backward(first_grad, normed_one, inverse_one, norm_float[0])
    branch_grad = grad_one.astype(jnp.bfloat16)
    mixing_term = jnp.einsum(
        "rd,re->de", mixed_low, branch_grad, preferred_element_type=jnp.float32
    )
    mixed_grad = jnp.einsum(
        "re,de->rd", branch_grad, w_mixing, preferred_element_type=jnp.float32
    ).astype(jnp.bfloat16)
    scores = jnp.where(key_valid[None, None, :], pair_scores(queries, all_keys, score_scale), -1e30)
    prob_again = jnp.exp(scores - logsum)
    prob_grad = pair_scores(mixed_grad, all_values, 1.0)
    row_delta = jnp.sum(prob_again * prob_grad, axis=-1, keepdims=True)
    score_grad = (prob_again * (prob_grad - row_delta)).astype(jnp.bfloat16)
    query_grad = (spread_rows(score_grad, all_keys) * score_scale).astype(jnp.bfloat16)
    key_terms = collect_rows(score_grad, queries) * score_scale
    value_terms = collect_rows(prob_low, mixed_grad)
    key_grad, value_grad = (
        lax.psum_scatter(key_terms, "ctx", scatter_dimension=0, tiled=True),
        lax.psum_scatter(value_terms, "ctx", scatter_dimension=0, tiled=True),
    )
    key_low = key_grad.astype(jnp.bfloat16)
    value_low = value_grad.astype(jnp.bfloat16)
    joined_grad = jnp.concatenate([query_grad, key_low, value_low], axis=1)
    project_term = jnp.einsum("rd,re->de", inputs, joined_grad, preferred_element_type=jnp.float32)
    input_grad = (
        jnp.einsum("re,de->rd", joined_grad, w_project, preferred_element_type=jnp.float32)
        + grad_one
    )
    bias_terms = jnp.stack(
        [
            jnp.sum(query_grad.astype(jnp.float32), axis=0),
            jnp.sum(value_low.astype(jnp.float32), axis=0),
            jnp.sum(branch_grad.astype(jnp.float32), axis=0),
            jnp.sum(second_grad.astype(jnp.float32), axis=0),
        ]
    )
    widen_terms = jnp.sum(expand_grad.astype(jnp.float32), axis=0)
    norm_terms = jnp.stack(
        [
            jnp.sum(first_grad * normed_one, axis=0),
            jnp.sum(first_grad, axis=0),
            jnp.sum(grad_out * normed_two, axis=0),
            jnp.sum(grad_out, axis=0),
        ]
    )
    shares = (
        lax.psum_scatter(project_term, "fsdp", scatter_dimension=0, tiled=True),
        lax.psum_scatter(mixing_term, "fsdp", scatter_dimension=0, tiled=True),
        lax.psum_scatter(widen_term, "fsdp", scatter_dimension=0, tiled=True),
        lax.psum_scatter(narrow_term, "fsdp", scatter_dimension=0, tiled=True),
        lax.psum_scatter(bias_terms, "fsdp", scatter_dimension=1, tiled=True),
        lax.psum_scatter(widen_terms, "fsdp", scatter_dimension=0, tiled=True),
        lax.psum_scatter(norm_terms, "fsdp", scatter_dimension=1, tiled=True),
    )
    totals = lax.psum(
        (shares[0], shares[1], shares[2], shares[3], shares[4], shares[5], shares[6]), "ctx"
    )
    return (
        result.astype(jnp.bfloat16)[None],
        input_grad[None],
        totals[0],
        totals[1],
        totals[2],
        totals[3],
        totals[4],
        totals[5],
        totals[6],
    )


NT=(((1,),(1,)),((),()))
NN=(((1,),(0,)),((),()))
def dotf(a,b,dims): return lax.dot_general(a,b,dims,preferred_element_type=jnp.float32)

def cost(microseconds):
    return pl.CostEstimate(flops=int(microseconds * 1.15e9), bytes_accessed=2**20, transcendentals=0)


def attn_fwd_kernel(len_ref,q_ref,k_ref,v_ref,*refs):
    o_ref,lse_ref,vt_ref=refs[-3:]
    @pl.when(pl.program_id(1)==0)
    def _():
        vt_ref[...]=v_ref[...].T
    n=len_ref[0]
    q=q_ref[...]; k=k_ref[...]
    lanes=lax.broadcasted_iota(jnp.int32,q.shape,1)
    rows=lax.broadcasted_iota(jnp.int32,(k.shape[0],1),0)
    valid=rows<n
    outs = []
    for h in range(2):
        qh=jnp.where((lanes>=64)==(h==1),q*jnp.bfloat16(HEAD_DIM**-0.5),jnp.bfloat16(0))
        s=dotf(k,qh,NT)
        s=jnp.where(valid,s,-1e30)
        m=jnp.max(s,axis=0,keepdims=True)
        e=jnp.exp(s-m)
        l=jnp.sum(e,axis=0,keepdims=True)
        p=(e*(1.0/l)).astype(jnp.bfloat16)
        lse_ref[0,h:h+1,:]=m+jnp.log(l)
        outs.append(dotf(vt_ref[64*h:64*h+64,:],p,NN))
    o=jnp.concatenate(outs,axis=0)
    o_ref[...]=o.T.astype(jnp.bfloat16)

def attn_fwd(length, joined, before, QB=512):
    L = joined.shape[0]
    C = joined.shape[1] // 3
    pairs = C // 128
    QB = min(QB, L)
    return pl.pallas_call(
        attn_fwd_kernel,
        grid=(pairs, L // QB),
        in_specs=[
            pl.BlockSpec(memory_space=pltpu.SMEM),
            pl.BlockSpec((QB, 128), lambda p, i: (i, p)),
            pl.BlockSpec((L, 128), lambda p, i: (0, pairs + p)),
            pl.BlockSpec((L, 128), lambda p, i: (0, 2 * pairs + p)),
        ]
        + [pl.BlockSpec(memory_space=pl.ANY)] * len(before),
        out_specs=[
            pl.BlockSpec((QB, 128), lambda p, i: (i, p)),
            pl.BlockSpec((1, 2, QB), lambda p, i: (p, 0, i)),
        ],
        out_shape=[
            jax.ShapeDtypeStruct((L, C), jnp.bfloat16),
            jax.ShapeDtypeStruct((pairs, 2, L), jnp.float32),
        ],
        scratch_shapes=[pltpu.VMEM((128, L), jnp.bfloat16)],
        compiler_params=pltpu.CompilerParams(vmem_limit_bytes=40 * 2**20),
        cost_estimate=cost(14.5),
        name="attn_fwd",
    )(length, joined, joined, joined, *before)


def attn_bwd_kernel(core_ref, len_ref, q_ref, k_ref, v_ref, do_ref, do_other_ref, lse_ref, *refs):
    df_ref, sum_ref, kt_ref, dka_ref, dva_ref = refs[-5:]
    i = pl.program_id(0)

    @pl.when(i == 0)
    def _():
        kt_ref[...] = k_ref[...].T
        dka_ref[...] = jnp.zeros_like(dka_ref)
        dva_ref[...] = jnp.zeros_like(dva_ref)

    n = len_ref[0]
    scale = jnp.bfloat16(HEAD_DIM**-0.5)
    q = q_ref[...]
    k = k_ref[...]
    v = v_ref[...]
    do = jnp.where(i == core_ref[0], do_ref[...], do_other_ref[...])
    lanes = lax.broadcasted_iota(jnp.int32, q.shape, 1)
    valid = lax.broadcasted_iota(jnp.int32, (k.shape[0], 1), 0) < n
    outs = []
    for h in range(2):
        mine = (lanes >= HEAD_DIM) == (h == 1)
        qh = jnp.where(mine, q * scale, jnp.bfloat16(0))
        doh = jnp.where(mine, do, jnp.bfloat16(0))
        s = dotf(k, qh, NT)
        p = jnp.where(valid, jnp.exp(s - lse_ref[0, h : h + 1, :]), 0.0)
        dp = dotf(v, doh, NT)
        delta = jnp.sum(p * dp, axis=0, keepdims=True)
        ds = (p * (dp - delta)).astype(jnp.bfloat16)
        dva_ref[...] += dotf(p.astype(jnp.bfloat16), doh, NN)
        dka_ref[...] += dotf(ds, qh, NN)
        outs.append(dotf(kt_ref[HEAD_DIM * h : HEAD_DIM * (h + 1), :], ds, NN))
    dq = jnp.concatenate(outs, axis=0) * (HEAD_DIM**-0.5)
    df_ref[pl.ds(pl.multiple_of(i * q.shape[0], q.shape[0]), q.shape[0]), 0:128] = dq.T.astype(jnp.bfloat16)

    @pl.when(i == pl.num_programs(0) - 1)
    def _():
        df_ref[:, 128:256] = dka_ref[...].astype(jnp.bfloat16)
        df_ref[:, 256:384] = dva_ref[...].astype(jnp.bfloat16)
        sum_ref[0:1, :] = jnp.sum(df_ref[...].astype(jnp.float32), axis=0, keepdims=True)


def attn_bwd(core, length, joined, do, do_other, lse, pair, before):
    L = joined.shape[0]
    pairs = joined.shape[1] // 384
    QB = L // 2
    block = lambda at: pl.BlockSpec((QB, 128), lambda i, c: (i, at * pairs + pair))
    whole = lambda at: pl.BlockSpec((L, 128), lambda i, c: (0, at * pairs + pair))
    return pl.pallas_call(
        attn_bwd_kernel,
        grid_spec=pltpu.PrefetchScalarGridSpec(
            num_scalar_prefetch=1,
            grid=(2,),
            in_specs=[
                pl.BlockSpec(memory_space=pltpu.SMEM),
                block(0),
                whole(1),
                whole(2),
                pl.BlockSpec((QB, 128), lambda i, c: (0, c[0] * pairs + pair)),
                pl.BlockSpec((QB, 128), lambda i, c: (0, pair)),
                pl.BlockSpec((1, 2, QB), lambda i, c: (pair, 0, i)),
            ]
            + [pl.BlockSpec(memory_space=pl.ANY)] * len(before),
            out_specs=[pl.BlockSpec((L, 384), lambda i, c: (0, 0)), pl.BlockSpec((8, 384), lambda i, c: (0, 0))],
            scratch_shapes=[
                pltpu.VMEM((128, L), jnp.bfloat16),
                pltpu.VMEM((L, 128), jnp.float32),
                pltpu.VMEM((L, 128), jnp.float32),
            ],
        ),
        out_shape=[
            jax.ShapeDtypeStruct((L, 384), jnp.bfloat16),
            jax.ShapeDtypeStruct((8, 384), jnp.float32),
        ],
        compiler_params=pltpu.CompilerParams(vmem_limit_bytes=24 * 2**20),
        cost_estimate=cost(7.6),
        name="attn_bwd",
    )(core, length, joined, joined, joined, do, do_other, lse, *before)


TN = (((0,), (0,)), ((), ()))


def gelu_pair(z):
    cdf = 0.5 * (1.0 + lax.erf(z * (0.5**0.5)))
    pdf = jnp.exp(-0.5 * z * z) * ((0.5 / jnp.pi) ** 0.5)
    return z * cdf, cdf + z * pdf

def widen_kernel(core_ref, own_ref, other_ref, mix_own_ref, mix_other_ref, x_ref, rows_ref, w_ref, wb_ref,
                 low_ref, turned_ref, normed_ref, inverse_ref, g_ref, gp_ref, z_ref, *, ROWS):
    @pl.when(pl.program_id(0) == 0)
    def _():
        width = x_ref.shape[1]
        branch = dotf(own_ref[...], mix_own_ref[...].reshape(width // 2, width), NN)
        branch += dotf(other_ref[...], mix_other_ref[...].reshape(width // 2, width), NN)
        hidden = x_ref[...].astype(jnp.float32) + (branch + rows_ref[2:3, :])
        centred = hidden - jnp.mean(hidden, axis=1, keepdims=True)
        inverse = lax.rsqrt(jnp.mean(centred * centred, axis=1, keepdims=True) + EPSILON)
        normed = centred * inverse
        normed_ref[...] = normed
        inverse_ref[...] = inverse
        low_ref[...] = (normed * rows_ref[4:5, :] + rows_ref[5:6, :]).astype(jnp.bfloat16)
        turned_ref[...] = low_ref[...].T

    z_ref[...] = dotf(low_ref[...], w_ref[...].reshape(low_ref.shape[1], -1), NN)

    def step(i, carry):
        at = pl.ds(i * ROWS, ROWS)
        value, slope = gelu_pair(z_ref[at, :] + wb_ref[...])
        g_ref[at, :] = value.astype(jnp.bfloat16)
        gp_ref[at, :] = slope.astype(gp_ref.dtype)
        return carry

    lax.fori_loop(0, z_ref.shape[0] // ROWS, step, 0)

def widen(core, mixed_own, mixed_other, rest, inputs, rows_float, widen_bias, ROWS=64, GP=jnp.float32):
    rows, width = inputs.shape
    chips, packed, _ = rest.shape
    shard = width // chips
    blocks = packed // shard - 1
    half = width // 2
    fixed = lambda shape: pl.BlockSpec(shape, lambda j, c: (0,) * len(shape))
    return pl.pallas_call(
        functools.partial(widen_kernel, ROWS=ROWS),
        grid_spec=pltpu.PrefetchScalarGridSpec(
            num_scalar_prefetch=1,
            grid=(blocks,),
            in_specs=[
                pl.BlockSpec((rows, half), lambda j, c: (c[0], 0)),
                pl.BlockSpec((rows, half), lambda j, c: (c[0], 0)),
                pl.BlockSpec((chips // 2, shard, width), lambda j, c: (c[0], 0, 0)),
                pl.BlockSpec((chips // 2, shard, width), lambda j, c: (1 - c[0], 0, 0)),
                fixed((rows, width)),
                fixed((8, width)),
                pl.BlockSpec((chips, shard, width), lambda j, c: (0, 1 + j, 0)),
                pl.BlockSpec((1, width), lambda j, c: (0, j)),
            ],
            out_specs=[
                fixed((rows, width)),
                fixed((width, rows)),
                fixed((rows, width)),
                fixed((rows, 1)),
                pl.BlockSpec((rows, width), lambda j, c: (0, j)),
                pl.BlockSpec((rows, width), lambda j, c: (0, j)),
            ],
            scratch_shapes=[pltpu.VMEM((rows, width), jnp.float32)],
        ),
        out_shape=[
            jax.ShapeDtypeStruct((rows, width), jnp.bfloat16),
            jax.ShapeDtypeStruct((width, rows), jnp.bfloat16),
            jax.ShapeDtypeStruct((rows, width), jnp.float32),
            jax.ShapeDtypeStruct((rows, 1), jnp.float32),
            jax.ShapeDtypeStruct((rows, blocks * width), jnp.bfloat16),
            jax.ShapeDtypeStruct((rows, blocks * width), GP),
        ],
        compiler_params=pltpu.CompilerParams(vmem_limit_bytes=56 * 2**20),
        cost_estimate=cost(12.5),
        name="widen",
    )(core, mixed_own, mixed_other, rest, rest, inputs, rows_float, rest, widen_bias)

def back_kernel(core_ref, dm_ref, grad_two_ref, normed_ref, inverse_ref, norm_ref, wn_ref, w_ref, gp_ref, mix_ref, *refs):
    dz_own_ref, dz_other_ref, dzsum_ref, one_ref, da_ref, do_ref, sums_ref, acc_ref = refs[-8:]
    j = pl.program_id(0)
    rows, width = dm_ref.shape
    dz = dotf(dm_ref[...], wn_ref[...], NT) * gp_ref[...].astype(jnp.float32)
    dz = dz.astype(jnp.bfloat16)
    own_turn = j >= pl.num_programs(0) // 2

    @pl.when(own_turn)
    def _():
        dz_own_ref[...] = dz

    @pl.when(jnp.logical_not(own_turn))
    def _():
        dz_other_ref[...] = dz

    dzsum_ref[...] = jnp.sum(dz.astype(jnp.float32), axis=0, keepdims=True)
    part = dotf(dz, w_ref[...].reshape(width, -1), NT)

    @pl.when(j == 0)
    def _():
        acc_ref[...] = grad_two_ref[...] + part

    @pl.when(j > 0)
    def _():
        acc_ref[...] += part

    @pl.when(j == pl.num_programs(0) - 1)
    def _():
        first_grad = acc_ref[...]
        normed = normed_ref[...]
        inner = first_grad * norm_ref[4:5, :]
        one = inverse_ref[...] * (
            inner
            - jnp.mean(inner, axis=1, keepdims=True)
            - normed * jnp.mean(inner * normed, axis=1, keepdims=True)
        )
        one_ref[...] = one
        low = one.astype(jnp.bfloat16)
        da_ref[...] = low
        do_ref[...] = dotf(low, mix_ref[...].reshape(width, width), NT).astype(jnp.bfloat16)
        sums_ref[0:1, :] = jnp.sum(first_grad * normed, axis=0, keepdims=True)
        sums_ref[1:2, :] = jnp.sum(first_grad, axis=0, keepdims=True)
        sums_ref[2:3, :] = jnp.sum(low.astype(jnp.float32), axis=0, keepdims=True)

def back(core, dm, grad_two, normed, inverse, norms, w_narrow, rest, gp, before):
    rows, width = dm.shape
    chips, packed, _ = rest.shape
    shard = width // chips
    blocks = packed // shard - 1
    at = lambda j, c: (j + (1 - c[0]) * (blocks // 2)) % blocks
    fixed = lambda shape: pl.BlockSpec(shape, lambda j, c: (0,) * len(shape))
    return pl.pallas_call(
        back_kernel,
        grid_spec=pltpu.PrefetchScalarGridSpec(
            num_scalar_prefetch=1,
            grid=(blocks,),
            in_specs=[
                fixed((rows, width)),
                fixed((rows, width)),
                fixed((rows, width)),
                fixed((rows, 1)),
                fixed((8, width)),
                pl.BlockSpec((width, width), lambda j, c: (at(j, c), 0)),
                pl.BlockSpec((chips, shard, width), lambda j, c: (0, 1 + at(j, c), 0)),
                pl.BlockSpec((rows, width), lambda j, c: (0, at(j, c))),
                fixed((chips, shard, width)),
            ]
            + [pl.BlockSpec(memory_space=pl.ANY)] * len(before),
            out_specs=[
                pl.BlockSpec((rows, width), lambda j, c: (0, jnp.maximum(j - blocks // 2, 0))),
                pl.BlockSpec((rows, width), lambda j, c: (0, jnp.minimum(j, blocks // 2 - 1))),
                pl.BlockSpec((1, width), lambda j, c: (0, at(j, c))),
                fixed((rows, width)),
                fixed((rows, width)),
                fixed((rows, width)),
                fixed((8, width)),
            ],
            scratch_shapes=[pltpu.VMEM((rows, width), jnp.float32)],
        ),
        out_shape=[
            jax.ShapeDtypeStruct((rows, blocks // 2 * width), jnp.bfloat16),
            jax.ShapeDtypeStruct((rows, blocks // 2 * width), jnp.bfloat16),
            jax.ShapeDtypeStruct((1, blocks * width), jnp.float32),
            jax.ShapeDtypeStruct((rows, width), jnp.float32),
            jax.ShapeDtypeStruct((rows, width), jnp.bfloat16),
            jax.ShapeDtypeStruct((rows, width), jnp.bfloat16),
            jax.ShapeDtypeStruct((8, width), jnp.float32),
        ],
        compiler_params=pltpu.CompilerParams(vmem_limit_bytes=56 * 2**20),
        cost_estimate=cost(13.8),
        name="back",
    )(core, dm, grad_two, normed, inverse, norms, w_narrow, rest, gp, rest, *before)


def tokens_kernel(core_ref, *refs, pairs):
    own_ref, other_ref = refs[-2:]
    w_ref, one_ref = refs[pairs], refs[pairs + 1]
    half = w_ref.shape[1] // 3

    def part():
        total = 0.0
        for pair in range(pairs):
            for kind in range(3):
                at = kind * half + pair * 128
                total += dotf(refs[pair][:, kind * 128 : kind * 128 + 128], w_ref[:, at : at + 128], NT)
        return total

    @pl.when(pl.program_id(0) == 0)
    def _():
        other_ref[...] = part()

    @pl.when(pl.program_id(0) == 1)
    def _():
        own_ref[...] = part() + one_ref[...]


def tokens_grad(core, grads, w_own, grad_one, before):
    rows, width = grad_one.shape
    fixed = lambda shape: pl.BlockSpec(shape, lambda i, c: (0,) * len(shape))
    turn = lambda i, c: (jnp.where(i == 0, 1 - c[0], c[0]), 0)
    return pl.pallas_call(
        functools.partial(tokens_kernel, pairs=len(grads)),
        grid_spec=pltpu.PrefetchScalarGridSpec(
            num_scalar_prefetch=1,
            grid=(2,),
            in_specs=[pl.BlockSpec((rows, 384), turn) for _ in grads]
            + [fixed(w_own.shape), fixed((rows, width))]
            + [pl.BlockSpec(memory_space=pl.ANY)] * len(before),
            out_specs=[fixed((rows, width)), fixed((rows, width))],
        ),
        out_shape=[jax.ShapeDtypeStruct((rows, width), jnp.float32)] * 2,
        compiler_params=pltpu.CompilerParams(vmem_limit_bytes=20 * 2**20),
        cost_estimate=cost(5.0),
        name="tokens_grad",
    )(core, *grads, w_own, grad_one, *before)


def widen_grad_kernel(own_ref, other_ref, grad_own_ref, grad_other_ref, left_ref, right_ref):
    term = dotf(own_ref[...], grad_own_ref[...], NN) + dotf(other_ref[...], grad_other_ref[...], NN)

    @pl.when(pl.program_id(0) == 0)
    def _():
        left_ref[...] = term.astype(jnp.bfloat16)

    @pl.when(pl.program_id(0) == 1)
    def _():
        right_ref[...] = term.astype(jnp.bfloat16)


def widen_grad(turned, turned_other, grad, grad_other):
    width, rows = turned.shape
    columns = grad.shape[1] // 2
    fixed = lambda shape: pl.BlockSpec(shape, lambda i: (0, 0))
    return pl.pallas_call(
        widen_grad_kernel,
        grid=(2,),
        in_specs=[fixed((width, rows))] * 2 + [pl.BlockSpec((rows, columns), lambda i: (0, i))] * 2,
        out_specs=[fixed((width, columns))] * 2,
        out_shape=[jax.ShapeDtypeStruct((width, columns), jnp.bfloat16)] * 2,
        compiler_params=pltpu.CompilerParams(vmem_limit_bytes=16 * 2**20),
        cost_estimate=cost(4.0),
        name="widen_grad",
    )(turned, turned_other, grad, grad_other)


def last_grad_kernel(core_ref, turned_ref, grad_ref, *refs):
    first_ref, second_ref, widen_ref, left_ref, right_ref = refs[-5:]
    sums = refs[:-5]
    half = turned_ref.shape[0] // 2
    term = dotf(turned_ref[...], grad_ref[...], NN).astype(jnp.bfloat16)
    left_ref[...] = term[:, :256]
    right_ref[:, :128] = term[:, 256:]

    def columns(rows):
        place = lax.broadcasted_iota(jnp.int32, (128, rows[0][1].shape[1]), 0)
        total = 0.0
        for at, row in rows:
            total = jnp.where(place == at, row, total)
        return total.T

    given = [(2, first_ref[2:3, :]), (3, second_ref[0:1, :]), (4, first_ref[0:1, :])]
    given += [(5, first_ref[1:2, :]), (6, second_ref[1:2, :]), (7, second_ref[2:3, :])]
    right_ref[:, 128:] = (columns(given) + widen_ref[...]).astype(jnp.bfloat16)
    queries = jnp.concatenate([ref[0:1, :128] for ref in sums], axis=1)
    values = jnp.concatenate([ref[0:1, 256:] for ref in sums], axis=1)
    at = pl.ds(pl.multiple_of(core_ref[0] * half, half), half)
    right_ref[at, 128:] = right_ref[at, 128:] + columns([(0, queries), (1, values)]).astype(jnp.bfloat16)


def last_grad(core, turned, grad, sums, first_sums, second_sums, widen_columns):
    width = turned.shape[0]
    whole = pl.BlockSpec(memory_space=pltpu.VMEM)
    return pl.pallas_call(
        last_grad_kernel,
        in_specs=[pl.BlockSpec(memory_space=pltpu.SMEM)] + [whole] * (5 + len(sums)),
        out_specs=[whole] * 2,
        out_shape=[jax.ShapeDtypeStruct((width, 256), jnp.bfloat16)] * 2,
        compiler_params=pltpu.CompilerParams(vmem_limit_bytes=12 * 2**20),
        cost_estimate=cost(2.0),
        name="last_grad",
    )(core, turned, grad, *sums, first_sums, second_sums, widen_columns)


def finish_kernel(core_ref, own_ref, other_ref, *refs, half, width):
    project_ref, mixing_ref, small_ref = refs[-3:]
    for ref, core in ((own_ref, core_ref[0]), (other_ref, 1 - core_ref[0])):
        starts = list(range(width + half, ref.shape[1], 384)) + [0]
        for pair, start in enumerate(starts):
            for kind in range(3):
                to = pl.multiple_of(core * half + (kind * 2 * half + pair * 128), 128)
                project_ref[:, pl.ds(to, 128)] = ref[:, start + kind * 128 : start + kind * 128 + 128]
        mixing_ref[:, pl.ds(pl.multiple_of(core * half, half), half)] = ref[:, width : width + half]
    small = own_ref[:, width - 128 : width] + other_ref[:, width - 128 : width]
    small_ref[...] = small.T


def finish(core, share, other, half, width, before):
    rows = share.shape[0]
    whole = pl.BlockSpec(memory_space=pltpu.VMEM)
    return pl.pallas_call(
        functools.partial(finish_kernel, half=half, width=width),
        in_specs=[pl.BlockSpec(memory_space=pltpu.SMEM)] + [whole] * 2 + [pl.BlockSpec(memory_space=pl.ANY)] * len(before),
        out_specs=[whole] * 3,
        out_shape=[
            jax.ShapeDtypeStruct((rows, 6 * half), jnp.float32),
            jax.ShapeDtypeStruct((rows, 2 * half), jnp.float32),
            jax.ShapeDtypeStruct((128, rows), jnp.float32),
        ],
        compiler_params=pltpu.CompilerParams(vmem_limit_bytes=8 * 2**20),
        cost_estimate=cost(2.0),
        name="finish",
    )(core, share, other, *before)


def narrow_kernel(core_ref, g_ref, own_ref, other_ref, normed_ref, rows_ref, cot_ref,
                  result_ref, two_ref, dm_ref, dm_own_ref, dm_other_ref, sums_ref, w_ref, acc_ref):
    j = pl.program_id(0)
    half = own_ref.shape[1]
    at_own = pl.ds(pl.multiple_of(core_ref[0] * half, half), half)
    at_other = pl.ds(pl.multiple_of((1 - core_ref[0]) * half, half), half)

    @pl.when(j == 0)
    def _():
        acc_ref[...] = jnp.zeros_like(acc_ref)

    w_ref[:, at_own] = own_ref[...]
    w_ref[:, at_other] = other_ref[...]
    acc_ref[...] += dotf(g_ref[...], w_ref[...], NN)

    @pl.when(j == pl.num_programs(0) - 1)
    def _():
        hidden = normed_ref[...] * rows_ref[4:5, :] + rows_ref[5:6, :] + (acc_ref[...] + rows_ref[3:4, :])
        centred = hidden - jnp.mean(hidden, axis=1, keepdims=True)
        inverse = lax.rsqrt(jnp.mean(centred * centred, axis=1, keepdims=True) + EPSILON)
        normed = centred * inverse
        result_ref[...] = (normed * rows_ref[6:7, :] + rows_ref[7:8, :]).astype(jnp.bfloat16)
        cot = cot_ref[...].astype(jnp.float32)
        inner = cot * rows_ref[6:7, :]
        two = inverse * (
            inner
            - jnp.mean(inner, axis=1, keepdims=True)
            - normed * jnp.mean(inner * normed, axis=1, keepdims=True)
        )
        two_ref[...] = two
        dm = two.astype(jnp.bfloat16)
        dm_ref[...] = dm
        dm_own_ref[...] = dm_ref[:, at_own]
        dm_other_ref[...] = dm_ref[:, at_other]
        sums_ref[0:1, :] = jnp.sum(dm.astype(jnp.float32), axis=0, keepdims=True)
        sums_ref[1:2, :] = jnp.sum(cot * normed, axis=0, keepdims=True)
        sums_ref[2:3, :] = jnp.sum(cot, axis=0, keepdims=True)


def narrow(core, g, own, other, normed, rows_float, cotangent):
    rows, width = normed.shape
    half = width // 2
    fixed = lambda shape: pl.BlockSpec(shape, lambda j, c: (0,) * len(shape))
    return pl.pallas_call(
        narrow_kernel,
        grid_spec=pltpu.PrefetchScalarGridSpec(
            num_scalar_prefetch=1,
            grid=(g.shape[1] // width,),
            in_specs=[
                pl.BlockSpec((rows, width), lambda j, c: (0, j)),
                pl.BlockSpec((width, half), lambda j, c: (j, 0)),
                pl.BlockSpec((width, half), lambda j, c: (j, 0)),
                fixed((rows, width)),
                fixed((8, width)),
                fixed((rows, width)),
            ],
            out_specs=[
                fixed((rows, width)),
                fixed((rows, width)),
                fixed((rows, width)),
                fixed((rows, half)),
                fixed((rows, half)),
                fixed((8, width)),
                pl.BlockSpec((width, width), lambda j, c: (j, 0)),
            ],
            scratch_shapes=[pltpu.VMEM((rows, width), jnp.float32)],
        ),
        out_shape=[
            jax.ShapeDtypeStruct((rows, width), jnp.bfloat16),
            jax.ShapeDtypeStruct((rows, width), jnp.float32),
            jax.ShapeDtypeStruct((rows, width), jnp.bfloat16),
            jax.ShapeDtypeStruct((rows, half), jnp.bfloat16),
            jax.ShapeDtypeStruct((rows, half), jnp.bfloat16),
            jax.ShapeDtypeStruct((8, width), jnp.float32),
            jax.ShapeDtypeStruct((g.shape[1], width), jnp.bfloat16),
        ],
        compiler_params=pltpu.CompilerParams(vmem_limit_bytes=56 * 2**20),
        cost_estimate=cost(8.0),
        name="narrow",
    )(core, g, own, other, normed, rows_float, cotangent)


def narrow_grad_kernel(own_ref, other_ref, dm_own_ref, dm_other_ref, out_ref):
    term = dotf(own_ref[...], dm_own_ref[...], TN) + dotf(other_ref[...], dm_other_ref[...], TN)
    out_ref[...] = term.reshape(out_ref.shape).astype(jnp.bfloat16)


def narrow_grad(g, g_other, dm_own, dm_other, chips):
    rows, hidden = g.shape
    half = dm_own.shape[1]
    lines = chips // 4
    size = hidden // lines
    fixed = lambda shape: pl.BlockSpec(shape, lambda j: (0, 0))
    return pl.pallas_call(
        narrow_grad_kernel,
        grid=(lines,),
        in_specs=[pl.BlockSpec((rows, size), lambda j: (0, j))] * 2 + [fixed((rows, half))] * 2,
        out_specs=pl.BlockSpec((4, 1, size // 4, half), lambda j: (0, j, 0, 0)),
        out_shape=jax.ShapeDtypeStruct((4, lines, size // 4, half), jnp.bfloat16),
        compiler_params=pltpu.CompilerParams(vmem_limit_bytes=16 * 2**20),
        cost_estimate=cost(4.5),
        name="narrow_grad",
    )(g, g_other, dm_own, dm_other)


def mixing_grad_kernel(core_ref, own_ref, other_ref, grad_ref, grad_other_ref, *refs):
    out_ref = refs[-1]
    rows, half = grad_other_ref.shape
    core = core_ref[0]
    here = pl.ds(pl.multiple_of(core * rows, rows), rows)
    there = pl.ds(pl.multiple_of((1 - core) * rows, rows), rows)
    at_own = pl.ds(pl.multiple_of(core * half, half), half)
    at_other = pl.ds(pl.multiple_of((1 - core) * half, half), half)
    grad = grad_ref[:, at_own]
    grad_other = grad_other_ref[...]
    for ref, at in ((own_ref, at_own), (other_ref, at_other)):
        term = dotf(ref[here, :], grad, TN) + dotf(ref[there, :], grad_other, TN)
        out_ref[at, :] = term.astype(jnp.bfloat16)


def mixing_grad(core, mixed_own, mixed_other, grad, grad_other, before):
    width = grad.shape[1]
    whole = pl.BlockSpec(memory_space=pltpu.VMEM)
    return pl.pallas_call(
        mixing_grad_kernel,
        in_specs=[pl.BlockSpec(memory_space=pltpu.SMEM)] + [whole] * 4 + [pl.BlockSpec(memory_space=pl.ANY)] * len(before),
        out_specs=whole,
        out_shape=jax.ShapeDtypeStruct((width, width // 2), jnp.bfloat16),
        compiler_params=pltpu.CompilerParams(vmem_limit_bytes=12 * 2**20),
        cost_estimate=cost(2.0),
        name="mixing_grad",
    )(core, mixed_own, mixed_other, grad, grad_other, *before)


AXES = ("fsdp", "ctx")


def core_permute(value, chips):
    pairs = [(2 * f + c, 2 * f + 1 - c) for f in range(chips) for c in range(2)]
    return lax.ppermute(value, AXES, pairs)


def chip_permute(value, chips, mask):
    pairs = [(2 * f + c, 2 * (f ^ mask) + c) for f in range(chips) for c in range(2)]
    return lax.ppermute(value, AXES, pairs)


def chip_bit(mask):
    return (lax.axis_index("fsdp") // mask) % 2


def by_core(mine, other, axis):
    core = lax.axis_index("ctx")
    first = jnp.where(core == 0, mine, other)
    second = jnp.where(core == 0, other, mine)
    return jnp.concatenate([first, second], axis=axis)


def dims_of(chips):
    return [1 << b for b in reversed(range(chips.bit_length() - 1))]


def gather_step(value, chips, mask):
    axis = dims_of(chips).index(mask)
    other = chip_permute(value, chips, mask)
    bit = chip_bit(mask)
    first = jnp.where(bit == 0, value, other)
    second = jnp.where(bit == 0, other, value)
    return jnp.concatenate([first, second], axis=axis)


def bits_of(chips):
    return jnp.stack([chip_bit(mask) for mask in dims_of(chips)])


def first_send(value, chips, mask):
    shape = [chips // (2 * mask), 2, mask] + list(value.shape[1:])
    send = lax.dynamic_index_in_dim(value.reshape(shape), 1 - chip_bit(mask), 1, keepdims=False)
    return send.reshape(chips // 2, *value.shape[1:])


def block_at(step, left, free, fixed):
    index = 0
    for place, mask in enumerate(left):
        if mask in fixed:
            bit = fixed[mask]
        else:
            bit = (step // 2 ** (len(free) - 1 - free.index(mask))) % 2
        index = index + bit * 2 ** (len(left) - 1 - place)
    return index


def hop_kernel(bits_ref, *refs, parts, merged, spare):
    outs = refs[4 * parts + spare :]
    at = 0
    for part in range(parts):
        away, away_in, keep, keep_in = refs[4 * part : 4 * part + 4]
        columns = away.shape[2]
        send_ref, keep_ref = outs[:2] if merged else outs[2 * part : 2 * part + 2]
        where = pl.ds(at, columns)
        send_ref[:, :, where] = (away[...].astype(jnp.float32) + away_in[...].astype(jnp.float32)).astype(jnp.bfloat16)
        keep_ref[:, :, where] = keep[...].astype(jnp.float32) + keep_in[...].astype(jnp.float32)
        if merged:
            at += columns


def hop(parts, bits, chips, before, merged):
    masks = dims_of(chips)
    in_specs, operands, out_columns = [], [], []
    steps = 2 ** (len([mask for mask in parts[0][2] if mask != parts[0][3]]) - 1)
    for value, arrived, left, came, goes in parts:
        rows, columns = value.shape[1:]
        rest = [mask for mask in left if mask != came]
        free = [mask for mask in rest if mask != goes]
        block = (1, rows, columns)
        for flip in (1, 0):
            def at_value(i, b, left=left, free=free, came=came, goes=goes, flip=flip):
                mine = b[masks.index(goes)]
                side = 1 - mine if flip else mine
                return block_at(i, left, free, {came: b[masks.index(came)], goes: side}), 0, 0

            def at_arrived(i, b, rest=rest, free=free, goes=goes, flip=flip):
                mine = b[masks.index(goes)]
                return block_at(i, rest, free, {goes: 1 - mine if flip else mine}), 0, 0

            in_specs += [pl.BlockSpec(block, at_value), pl.BlockSpec(block, at_arrived)]
            operands += [value, arrived]
        out_columns.append(columns)
    if merged:
        out_columns = [sum(out_columns)]
    out_specs, out_shape = [], []
    for columns in out_columns:
        out_specs += [pl.BlockSpec((1, rows, columns), lambda i, b: (i, 0, 0))] * 2
        out_shape += [
            jax.ShapeDtypeStruct((steps, rows, columns), jnp.bfloat16),
            jax.ShapeDtypeStruct((steps, rows, columns), jnp.float32),
        ]
    outs = pl.pallas_call(
        functools.partial(hop_kernel, parts=len(parts), merged=merged, spare=len(before)),
        grid_spec=pltpu.PrefetchScalarGridSpec(
            num_scalar_prefetch=1,
            grid=(steps,),
            in_specs=in_specs + [pl.BlockSpec(memory_space=pl.ANY)] * len(before),
            out_specs=out_specs,
        ),
        out_shape=out_shape,
        compiler_params=pltpu.CompilerParams(vmem_limit_bytes=8 * 2**20),
        cost_estimate=cost(2.0),
        name="hop",
    )(bits, *operands, *before)
    return list(outs[0::2]), list(outs[1::2])


class Chain:
    def __init__(self, values, chips, bits):
        self.chips, self.bits, self.masks = chips, bits, dims_of(chips)
        self.far = self.masks[:-2]
        self.order = ([1, 2], [2, 1])
        self.kept = values
        self.sent = [first_send(part, chips, order[0]) for part, order in zip(self.kept, self.order)]

    def move(self, masks):
        self.arrived = [chip_permute(part, self.chips, mask) for part, mask in zip(self.sent, masks)]

    def first(self):
        self.move([1, 2])

    def second(self, before):
        self.sent, self.kept = hop(
            [
                (kept, arrived, self.masks, order[0], order[1])
                for kept, arrived, order in zip(self.kept, self.arrived, self.order)
            ],
            self.bits, self.chips, before, False,
        )
        self.move([2, 1])

    def third(self, before, others=()):
        parts = [
            (kept, arrived, self.far, order[1], self.far[-1])
            for chain in (self, *others)
            for kept, arrived, order in zip(chain.kept, chain.arrived, chain.order)
        ]
        self.sent, self.kept = hop(parts, self.bits, self.chips, before, True)
        self.move([self.far[-1]])

    def fourth(self, before):
        for at in range(len(self.far) - 1, 0, -1):
            part = (self.kept[0], self.arrived[0], self.far[:at], self.far[at], self.far[at - 1])
            self.sent, self.kept = hop([part], self.bits, self.chips, before, True)
            self.move([self.far[at - 1]])

    def last(self):
        return self.kept[0][0] + self.arrived[0][0].astype(jnp.float32)


def groups_of(chips):
    near = [list(range(at, at + 4)) for at in range(0, chips, 4)]
    far = [list(range(at, chips, 4)) for at in range(4)]
    return near, far


def core_half(value, axis, own):
    core = lax.axis_index("ctx")
    size = value.shape[axis] // 2
    which = core if own else 1 - core
    return lax.dynamic_slice_in_dim(value, which * size, size, axis)


def gather_chips(value, chips, far, split):
    for mask in far:
        value = gather_step(value, chips, mask)
    left, right = split(value)
    left, right = gather_step(left, chips, 1), gather_step(right, chips, 2)
    return value, gather_step(left, chips, 2), gather_step(right, chips, 1)


def pair_terms(rows, rows_other, grad, chips):
    other = core_permute(core_half(grad, 1, False), chips)
    mine = jnp.einsum("rd,re->de", rows, core_half(grad, 1, True), preferred_element_type=jnp.float32)
    return mine + jnp.einsum("rd,re->de", rows_other, other, preferred_element_type=jnp.float32)


def fast_body(
    tokens, lengths, cotangent, projection, mixing, widening, narrowing, biases, widen_bias, norms
):
    chips = lax.axis_size("fsdp")
    core = lax.axis_index("ctx")
    core_at = core.reshape(1)
    bits = dims_of(chips)
    far = bits[:-2]
    down_x = [1, 2] + far[::-1]
    down_y = [2, 1] + far[::-1]
    inputs = tokens[0]
    row_count, model_width = inputs.shape
    shard = projection.shape[0]
    half = model_width // 2
    swap = lambda value: core_permute(value, chips)

    rest = jnp.concatenate(
        [mixing]
        + [widening[:, at : at + model_width] for at in range(0, widening.shape[1], model_width)],
        axis=0,
    )
    rest = lax.all_gather(core_half(rest, 0, True), AXES, axis=0, tiled=True).reshape(chips, *rest.shape)

    own = projection.reshape(shard, 3, 2, half)
    own = lax.dynamic_index_in_dim(own, core, 2, keepdims=False).reshape(shard, 3 * half)
    hidden = widen_bias.shape[0] // shard
    small = jnp.concatenate([biases.T, norms.T, widen_bias.reshape(hidden, shard).T], axis=1)
    small = jnp.pad(small, ((0, 0), (0, 128 - small.shape[1])))
    packed = jnp.concatenate([own, small], axis=1)
    packed = packed.reshape([1] * len(bits) + [shard, packed.shape[1]])
    cut = packed.shape[-1] // 2
    halfway, left, right = gather_chips(packed, chips, far, lambda value: (value[..., :cut], value[..., cut:]))
    left = left.reshape(model_width, cut)
    right = right.reshape(model_width, cut)
    w_own = jnp.concatenate([left, right[:, : 3 * half - cut]], axis=1)
    small = right[:, 3 * half - cut :].astype(jnp.float32)
    rows_float = small[:, :8].T
    widen_float = small[:, 8 : 8 + hidden].reshape(chips, shard, hidden).transpose(0, 2, 1).reshape(1, -1)

    narrow_rows = narrowing.shape[0]
    middle = narrow_rows // 2
    late = jnp.where(core > 1, halfway.reshape(-1)[0], jnp.bfloat16(0))
    own = (core_half(narrowing, 1, True) + late).reshape([1] * len(bits) + [narrow_rows, half])
    for mask in far:
        own = gather_step(own, chips, mask)
    upper = gather_step(own[..., :middle, :], chips, 1)
    lower = gather_step(own[..., middle:, :], chips, 2)

    all_inputs = by_core(inputs, swap(inputs), 0)
    bias_own = lax.dynamic_slice_in_dim(rows_float, core * half, half, 1)
    bias_joined = jnp.concatenate([bias_own[0], jnp.zeros_like(bias_own[0]), bias_own[1]])
    joined = (jnp.dot(all_inputs, w_own, preferred_element_type=jnp.float32) + bias_joined).astype(jnp.bfloat16)
    inputs_turned = all_inputs.T
    mixed_own, logsum = attn_fwd(lengths, joined, [rows_float, widen_float, inputs_turned])
    mixed_other = swap(mixed_own)

    late = jnp.where(core > 1, mixed_own[0, 0], jnp.bfloat16(0))
    upper = gather_step(upper + late, chips, 2)
    lower = gather_step(lower + late, chips, 1)
    first_low, first_turned, normed_one, inverse_one, active_low, slope = widen(
        core_at, mixed_own, mixed_other, rest, inputs, rows_float, widen_float
    )
    late = jnp.where(core > 1, first_low[0, 0], jnp.bfloat16(0))
    narrow_own = jnp.concatenate([upper, lower], axis=-2).reshape(chips * narrow_rows, half) + late
    narrow_other = swap(narrow_own)
    first_other = swap(first_turned)
    active_other = swap(active_low)
    result, grad_two, second_grad, dm_own, dm_other, second_sums, w_narrow = narrow(
        core_at, active_low, narrow_own, narrow_other, normed_one, rows_float, cotangent[0]
    )

    chip_bits = bits_of(chips)
    near, line = groups_of(chips)
    narrow_term = narrow_grad(active_low, active_other, dm_own, swap(dm_other), chips)
    narrow_near = lax.psum_scatter(
        narrow_term, "fsdp", scatter_dimension=0, axis_index_groups=near, tiled=True
    ).reshape(chips // 4, narrow_rows, half)

    expand_own, expand_other, widen_terms, grad_one, branch_grad, mixed_grad, first_sums = back(
        core_at, second_grad, grad_two, normed_one, inverse_one, rows_float,
        w_narrow, rest, slope, [narrow_term],
    )
    mixed_grad_other = swap(core_half(mixed_grad, 1, False))
    branch_other = swap(core_half(branch_grad, 1, False))
    widen_terms_two = widen_grad(first_turned, first_other, expand_own, swap(expand_other))
    widen_chain = Chain([term.reshape(chips, shard, -1) for term in widen_terms_two], chips, chip_bits)
    widen_chain.first()

    mixing_term = mixing_grad(core_at, mixed_own, mixed_other, branch_grad, branch_other, [widen_chain.sent[0]])

    widen_columns = widen_terms.reshape(chips, hidden, shard).transpose(0, 2, 1).reshape(model_width, hidden)
    widen_columns = jnp.pad(widen_columns, ((0, 0), (8, 120 - hidden)))

    pairs = half // 128
    project = lambda grad: jnp.dot(
        inputs_turned, grad, preferred_element_type=jnp.float32
    ).astype(jnp.bfloat16)
    grads, sums = [], []
    before = widen_chain.sent + [mixing_term]
    for pair in range(pairs - 1):
        grad, grad_sum = attn_bwd(core_at, lengths, joined, mixed_grad, mixed_grad_other, logsum, pair, before)
        grads.append(grad)
        sums.append(grad_sum)
        if pair == 0:
            widen_chain.second([grad])
        elif pair == 1:
            widen_chain.third([grad])
        before = widen_chain.sent + [narrow_near]
    parts = [mixing_term] + [project(grad) for grad in grads]
    cut = (len(parts) + 1) // 2
    first_terms = [jnp.concatenate(parts[:cut], axis=1), jnp.concatenate(parts[cut:], axis=1)]
    first_chain = Chain([term.reshape(chips, shard, -1) for term in first_terms], chips, chip_bits)
    first_chain.first()
    grad, grad_sum = attn_bwd(
        core_at, lengths, joined, mixed_grad, mixed_grad_other, logsum, pairs - 1,
        widen_chain.sent + first_chain.sent + [widen_columns],
    )
    grads.append(grad)
    sums.append(grad_sum)
    narrow_share = lax.psum_scatter(
        narrow_near, "fsdp", scatter_dimension=0, axis_index_groups=line, tiled=True
    )[0].astype(jnp.float32)

    last_terms = last_grad(core_at, inputs_turned, grad, sums, first_sums, second_sums, widen_columns)
    last_chain = Chain([term.reshape(chips, shard, -1) for term in last_terms], chips, chip_bits)
    last_chain.first()
    first_chain.second([grad] + last_chain.sent)
    widen_chain.fourth([grad] + first_chain.sent)
    last_chain.second(widen_chain.sent)
    last_chain.third([narrow_share], [first_chain])
    own_part, other_part = tokens_grad(core_at, grads, w_own, grad_one, last_chain.sent)
    last_chain.fourth([own_part])
    input_grad = own_part + swap(other_part)
    join = lambda share: by_core(share, swap(share), 1)
    widen_share = join(widen_chain.last())
    narrow_share = join(narrow_share)
    last_share = last_chain.last()
    width = sum(term.shape[1] for term in last_terms)
    other_share = swap(last_share)

    grad_projection, grad_mixing, small_share = finish(
        core_at, last_share, other_share, half, width, [input_grad, widen_share, narrow_share]
    )
    return (
        result.astype(jnp.bfloat16)[None],
        input_grad[None],
        grad_projection,
        grad_mixing,
        widen_share,
        narrow_share,
        small_share[:4],
        small_share[8 : 8 + hidden].reshape(-1),
        small_share[4:8],
    )


def solution(mesh):
    in_specs = (
        P("fsdp", "ctx", None),
        P("fsdp"),
        P("fsdp", "ctx", None),
        P("fsdp", None),
        P("fsdp", None),
        P("fsdp", None),
        P("fsdp", None),
        P(None, "fsdp"),
        P("fsdp"),
        P(None, "fsdp"),
    )
    out_specs = (
        P("fsdp", "ctx", None),
        P("fsdp", "ctx", None),
        P("fsdp", None),
        P("fsdp", None),
        P("fsdp", None),
        P("fsdp", None),
        P(None, "fsdp"),
        P("fsdp"),
        P(None, "fsdp"),
    )
    chips = mesh.shape["fsdp"]
    paired = mesh.shape["ctx"] == 2 and chips >= 4 and chips & (chips - 1) == 0
    body = fast_body if paired else general_body
    return jax.shard_map(body, mesh=mesh, in_specs=in_specs, out_specs=out_specs, check_vma=False)
```

```python
import functools

import jax
import jax.numpy as jnp
from jax import lax
from jax.experimental import pallas as pl
from jax.experimental.pallas import tpu as pltpu
from jax.sharding import PartitionSpec as P

HEADS = 12
HEAD_DIM = 64


EPSILON = 1e-12


def split_heads(matrix):
    return matrix.reshape(matrix.shape[0], HEADS, matrix.shape[1] // HEADS)


def pair_scores(left_rows, right_rows, factor):
    return (
        jnp.einsum(
            "ahd,bhd->hab",
            split_heads(left_rows),
            split_heads(right_rows),
            preferred_element_type=jnp.float32,
        )
        * factor
    )


def spread_rows(weights_hab, right_rows):
    out_rows = jnp.einsum(
        "hab,bhd->ahd", weights_hab, split_heads(right_rows), preferred_element_type=jnp.float32
    )
    return out_rows.reshape(out_rows.shape[0], -1)


def collect_rows(weights_hab, left_rows):
    out_rows = jnp.einsum(
        "hab,ahd->bhd", weights_hab, split_heads(left_rows), preferred_element_type=jnp.float32
    )
    return out_rows.reshape(out_rows.shape[0], -1)


def norm_forward(hidden, gain, shift):
    row_mean = jnp.mean(hidden, axis=-1, keepdims=True)
    centred = hidden - row_mean
    inverse = lax.rsqrt(jnp.mean(centred * centred, axis=-1, keepdims=True) + EPSILON)
    normed = centred * inverse
    return (normed * gain + shift, normed, inverse)


def norm_backward(upstream, normed, inverse, gain):
    inner = upstream * gain
    return inverse * (
        inner
        - jnp.mean(inner, axis=-1, keepdims=True)
        - normed * jnp.mean(inner * normed, axis=-1, keepdims=True)
    )


def gelu_exact(values_in):
    return jax.nn.gelu(values_in, approximate=False)


def general_body(
    tokens, lengths, cotangent, projection, mixing, widening, narrowing, biases, widen_bias, norms
):
    score_scale = HEAD_DIM ** (-0.5)
    gathered = (
        lax.all_gather(projection, "fsdp", axis=0, tiled=True),
        lax.all_gather(mixing, "fsdp", axis=0, tiled=True),
        lax.all_gather(widening, "fsdp", axis=0, tiled=True),
        lax.all_gather(narrowing, "fsdp", axis=0, tiled=True),
        lax.all_gather(biases, "fsdp", axis=1, tiled=True),
        lax.all_gather(widen_bias, "fsdp", axis=0, tiled=True),
        lax.all_gather(norms, "fsdp", axis=1, tiled=True),
    )
    w_project, w_mixing, w_widen, w_narrow, bias_rows, widen_all, norm_rows = gathered
    bias_float = bias_rows.astype(jnp.float32)
    widen_float = widen_all.astype(jnp.float32)
    norm_float = norm_rows.astype(jnp.float32)
    inputs = tokens[0]
    row_count, model_width = inputs.shape
    seq_length = lengths[0]
    joined_rows = jnp.dot(inputs, w_project, preferred_element_type=jnp.float32)
    queries = (joined_rows[:, :model_width] + bias_float[0]).astype(jnp.bfloat16)
    key_rows = joined_rows[:, model_width : 2 * model_width].astype(jnp.bfloat16)
    value_rows = (joined_rows[:, 2 * model_width :] + bias_float[1]).astype(jnp.bfloat16)
    all_keys, all_values = (
        lax.all_gather(key_rows, "ctx", axis=0, tiled=True),
        lax.all_gather(value_rows, "ctx", axis=0, tiled=True),
    )
    key_valid = jnp.arange(all_keys.shape[0], dtype=jnp.int32) < seq_length
    scores = jnp.where(key_valid[None, None, :], pair_scores(queries, all_keys, score_scale), -1e30)
    row_peak = jnp.max(scores, axis=-1, keepdims=True)
    exp_terms = jnp.exp(scores - row_peak)
    summed = jnp.sum(exp_terms, axis=-1, keepdims=True)
    prob_low = (exp_terms / summed).astype(jnp.bfloat16)
    logsum = row_peak + jnp.log(summed)
    mixed_low = spread_rows(prob_low, all_values).astype(jnp.bfloat16)
    branch = jnp.dot(mixed_low, w_mixing, preferred_element_type=jnp.float32) + bias_float[2]
    first_norm, normed_one, inverse_one = norm_forward(
        inputs.astype(jnp.float32) + branch, norm_float[0], norm_float[1]
    )
    first_low = first_norm.astype(jnp.bfloat16)
    expanded = jnp.dot(first_low, w_widen, preferred_element_type=jnp.float32) + widen_float
    activated, gelu_pull = jax.vjp(gelu_exact, expanded)
    active_low = activated.astype(jnp.bfloat16)
    second = jnp.dot(active_low, w_narrow, preferred_element_type=jnp.float32) + bias_float[3]
    result, normed_two, inverse_two = norm_forward(
        first_norm + second, norm_float[2], norm_float[3]
    )
    grad_out = cotangent[0].astype(jnp.float32)
    grad_two = norm_backward(grad_out, normed_two, inverse_two, norm_float[2])
    second_grad = grad_two.astype(jnp.bfloat16)
    narrow_term = jnp.einsum(
        "rf,rd->fd", active_low, second_grad, preferred_element_type=jnp.float32
    )
    active_grad = jnp.einsum("rd,fd->rf", second_grad, w_narrow, preferred_element_type=jnp.float32)
    expand_grad = gelu_pull(active_grad)[0].astype(jnp.bfloat16)
    widen_term = jnp.einsum("rd,rf->df", first_low, expand_grad, preferred_element_type=jnp.float32)
    first_grad = grad_two + jnp.einsum(
        "rf,df->rd", expand_grad, w_widen, preferred_element_type=jnp.float32
    )
    grad_one = norm_backward(first_grad, normed_one, inverse_one, norm_float[0])
    branch_grad = grad_one.astype(jnp.bfloat16)
    mixing_term = jnp.einsum(
        "rd,re->de", mixed_low, branch_grad, preferred_element_type=jnp.float32
    )
    mixed_grad = jnp.einsum(
        "re,de->rd", branch_grad, w_mixing, preferred_element_type=jnp.float32
    ).astype(jnp.bfloat16)
    scores = jnp.where(key_valid[None, None, :], pair_scores(queries, all_keys, score_scale), -1e30)
    prob_again = jnp.exp(scores - logsum)
    prob_grad = pair_scores(mixed_grad, all_values, 1.0)
    row_delta = jnp.sum(prob_again * prob_grad, axis=-1, keepdims=True)
    score_grad = (prob_again * (prob_grad - row_delta)).astype(jnp.bfloat16)
    query_grad = (spread_rows(score_grad, all_keys) * score_scale).astype(jnp.bfloat16)
    key_terms = collect_rows(score_grad, queries) * score_scale
    value_terms = collect_rows(prob_low, mixed_grad)
    key_grad, value_grad = (
        lax.psum_scatter(key_terms, "ctx", scatter_dimension=0, tiled=True),
        lax.psum_scatter(value_terms, "ctx", scatter_dimension=0, tiled=True),
    )
    key_low = key_grad.astype(jnp.bfloat16)
    value_low = value_grad.astype(jnp.bfloat16)
    joined_grad = jnp.concatenate([query_grad, key_low, value_low], axis=1)
    project_term = jnp.einsum("rd,re->de", inputs, joined_grad, preferred_element_type=jnp.float32)
    input_grad = (
        jnp.einsum("re,de->rd", joined_grad, w_project, preferred_element_type=jnp.float32)
        + grad_one
    )
    bias_terms = jnp.stack(
        [
            jnp.sum(query_grad.astype(jnp.float32), axis=0),
            jnp.sum(value_low.astype(jnp.float32), axis=0),
            jnp.sum(branch_grad.astype(jnp.float32), axis=0),
            jnp.sum(second_grad.astype(jnp.float32), axis=0),
        ]
    )
    widen_terms = jnp.sum(expand_grad.astype(jnp.float32), axis=0)
    norm_terms = jnp.stack(
        [
            jnp.sum(first_grad * normed_one, axis=0),
            jnp.sum(first_grad, axis=0),
            jnp.sum(grad_out * normed_two, axis=0),
            jnp.sum(grad_out, axis=0),
        ]
    )
    shares = (
        lax.psum_scatter(project_term, "fsdp", scatter_dimension=0, tiled=True),
        lax.psum_scatter(mixing_term, "fsdp", scatter_dimension=0, tiled=True),
        lax.psum_scatter(widen_term, "fsdp", scatter_dimension=0, tiled=True),
        lax.psum_scatter(narrow_term, "fsdp", scatter_dimension=0, tiled=True),
        lax.psum_scatter(bias_terms, "fsdp", scatter_dimension=1, tiled=True),
        lax.psum_scatter(widen_terms, "fsdp", scatter_dimension=0, tiled=True),
        lax.psum_scatter(norm_terms, "fsdp", scatter_dimension=1, tiled=True),
    )
    totals = lax.psum(
        (shares[0], shares[1], shares[2], shares[3], shares[4], shares[5], shares[6]), "ctx"
    )
    return (
        result.astype(jnp.bfloat16)[None],
        input_grad[None],
        totals[0],
        totals[1],
        totals[2],
        totals[3],
        totals[4],
        totals[5],
        totals[6],
    )


NT=(((1,),(1,)),((),()))
NN=(((1,),(0,)),((),()))
def dotf(a,b,dims): return lax.dot_general(a,b,dims,preferred_element_type=jnp.float32)

def cost(microseconds):
    return pl.CostEstimate(flops=int(microseconds * 5e7), bytes_accessed=2**12, transcendentals=0)


def attn_fwd_kernel(len_ref,q_ref,k_ref,v_ref,*refs):
    o_ref,lse_ref,vt_ref=refs[-3:]
    @pl.when(pl.program_id(1)==0)
    def _():
        vt_ref[...]=v_ref[...].T
    n=len_ref[0]
    q=q_ref[...]; k=k_ref[...]
    lanes=lax.broadcasted_iota(jnp.int32,q.shape,1)
    rows=lax.broadcasted_iota(jnp.int32,(k.shape[0],1),0)
    valid=rows<n
    outs = []
    for h in range(2):
        qh=jnp.where((lanes>=64)==(h==1),q*jnp.bfloat16(HEAD_DIM**-0.5),jnp.bfloat16(0))
        s=dotf(k,qh,NT)
        s=jnp.where(valid,s,-1e30)
        m=jnp.max(s,axis=0,keepdims=True)
        e=jnp.exp(s-m)
        l=jnp.sum(e,axis=0,keepdims=True)
        p=(e*(1.0/l)).astype(jnp.bfloat16)
        lse_ref[0,h:h+1,:]=m+jnp.log(l)
        outs.append(dotf(vt_ref[64*h:64*h+64,:],p,NN))
    o=jnp.concatenate(outs,axis=0)
    o_ref[...]=o.T.astype(jnp.bfloat16)

def attn_fwd(length, joined, before, QB=512):
    L = joined.shape[0]
    C = joined.shape[1] // 3
    pairs = C // 128
    QB = min(QB, L)
    return pl.pallas_call(
        attn_fwd_kernel,
        grid=(pairs, L // QB),
        in_specs=[
            pl.BlockSpec(memory_space=pltpu.SMEM),
            pl.BlockSpec((QB, 128), lambda p, i: (i, p)),
            pl.BlockSpec((L, 128), lambda p, i: (0, pairs + p)),
            pl.BlockSpec((L, 128), lambda p, i: (0, 2 * pairs + p)),
        ]
        + [pl.BlockSpec(memory_space=pl.ANY)] * len(before),
        out_specs=[
            pl.BlockSpec((QB, 128), lambda p, i: (i, p)),
            pl.BlockSpec((1, 2, QB), lambda p, i: (p, 0, i)),
        ],
        out_shape=[
            jax.ShapeDtypeStruct((L, C), jnp.bfloat16),
            jax.ShapeDtypeStruct((pairs, 2, L), jnp.float32),
        ],
        scratch_shapes=[pltpu.VMEM((128, L), jnp.bfloat16)],
        compiler_params=pltpu.CompilerParams(vmem_limit_bytes=20 * 2**20),
        cost_estimate=cost(14.5),
        name="attn_fwd",
    )(length, joined, joined, joined, *before)


def attn_bwd_kernel(core_ref, len_ref, q_ref, k_ref, v_ref, do_ref, do_other_ref, lse_ref, *refs):
    df_ref, sum_ref, kt_ref, dka_ref, dva_ref = refs[-5:]
    i = pl.program_id(1)

    @pl.when(i == 0)
    def _():
        kt_ref[...] = k_ref[...].T
        dka_ref[...] = jnp.zeros_like(dka_ref)
        dva_ref[...] = jnp.zeros_like(dva_ref)

    n = len_ref[0]
    scale = jnp.bfloat16(HEAD_DIM**-0.5)
    q = q_ref[...]
    k = k_ref[...]
    v = v_ref[...]
    do = jnp.where(i == core_ref[0], do_ref[...], do_other_ref[...])
    lanes = lax.broadcasted_iota(jnp.int32, q.shape, 1)
    valid = lax.broadcasted_iota(jnp.int32, (k.shape[0], 1), 0) < n
    outs = []
    for h in range(2):
        mine = (lanes >= HEAD_DIM) == (h == 1)
        qh = jnp.where(mine, q * scale, jnp.bfloat16(0))
        doh = jnp.where(mine, do, jnp.bfloat16(0))
        s = dotf(k, qh, NT)
        p = jnp.where(valid, jnp.exp(s - lse_ref[0, h : h + 1, :]), 0.0)
        dp = dotf(v, doh, NT)
        delta = jnp.sum(p * dp, axis=0, keepdims=True)
        ds = (p * (dp - delta)).astype(jnp.bfloat16)
        dva_ref[...] += dotf(p.astype(jnp.bfloat16), doh, NN)
        dka_ref[...] += dotf(ds, qh, NN)
        outs.append(dotf(kt_ref[HEAD_DIM * h : HEAD_DIM * (h + 1), :], ds, NN))
    dq = jnp.concatenate(outs, axis=0) * (HEAD_DIM**-0.5)
    df_ref[pl.ds(pl.multiple_of(i * q.shape[0], q.shape[0]), q.shape[0]), 0:128] = dq.T.astype(jnp.bfloat16)

    @pl.when(i == pl.num_programs(1) - 1)
    def _():
        df_ref[:, 128:256] = dka_ref[...].astype(jnp.bfloat16)
        df_ref[:, 256:384] = dva_ref[...].astype(jnp.bfloat16)
        sum_ref[0:1, :] = jnp.sum(df_ref[...].astype(jnp.float32), axis=0, keepdims=True)


def attn_bwd(core, length, joined, do, do_other, lse, before):
    L = joined.shape[0]
    pairs = joined.shape[1] // 384
    QB = L // 2
    block = lambda at: pl.BlockSpec((QB, 128), lambda p, i, c: (i, at * pairs + p))
    whole = lambda at: pl.BlockSpec((L, 128), lambda p, i, c: (0, at * pairs + p))
    return pl.pallas_call(
        attn_bwd_kernel,
        grid_spec=pltpu.PrefetchScalarGridSpec(
            num_scalar_prefetch=1,
            grid=(pairs, 2),
            in_specs=[
                pl.BlockSpec(memory_space=pltpu.SMEM),
                block(0),
                whole(1),
                whole(2),
                pl.BlockSpec((QB, 128), lambda p, i, c: (0, c[0] * pairs + p)),
                pl.BlockSpec((QB, 128), lambda p, i, c: (0, p)),
                pl.BlockSpec((1, 2, QB), lambda p, i, c: (p, 0, i)),
            ]
            + [pl.BlockSpec(memory_space=pl.ANY)] * len(before),
            out_specs=[
                pl.BlockSpec((L, 384), lambda p, i, c: (0, p)),
                pl.BlockSpec((8, 384), lambda p, i, c: (0, p)),
            ],
            scratch_shapes=[
                pltpu.VMEM((128, L), jnp.bfloat16),
                pltpu.VMEM((L, 128), jnp.float32),
                pltpu.VMEM((L, 128), jnp.float32),
            ],
        ),
        out_shape=[
            jax.ShapeDtypeStruct((L, pairs * 384), jnp.bfloat16),
            jax.ShapeDtypeStruct((8, pairs * 384), jnp.float32),
        ],
        compiler_params=pltpu.CompilerParams(vmem_limit_bytes=20 * 2**20),
        cost_estimate=cost(22.0),
        name="attn_bwd",
    )(core, length, joined, joined, joined, do, do_other, lse, *before)


TN = (((0,), (0,)), ((), ()))


def gelu_pair(z):
    cdf = 0.5 * (1.0 + lax.erf(z * (0.5**0.5)))
    pdf = jnp.exp(-0.5 * z * z) * ((0.5 / jnp.pi) ** 0.5)
    return z * cdf, cdf + z * pdf

def widen_kernel(core_ref, own_ref, other_ref, mix_own_ref, mix_other_ref, x_ref, rows_ref, w_ref, wb_ref,
                 low_ref, turned_ref, normed_ref, inverse_ref, g_ref, gp_ref, z_ref):
    @pl.when(pl.program_id(0) == 0)
    def _():
        width = x_ref.shape[1]
        branch = dotf(own_ref[...], mix_own_ref[...].reshape(width // 2, width), NN)
        branch += dotf(other_ref[...], mix_other_ref[...].reshape(width // 2, width), NN)
        hidden = x_ref[...].astype(jnp.float32) + (branch + rows_ref[2:3, :])
        centred = hidden - jnp.mean(hidden, axis=1, keepdims=True)
        inverse = lax.rsqrt(jnp.mean(centred * centred, axis=1, keepdims=True) + EPSILON)
        normed = centred * inverse
        normed_ref[...] = normed
        inverse_ref[...] = inverse
        low_ref[...] = (normed * rows_ref[4:5, :] + rows_ref[5:6, :]).astype(jnp.bfloat16)
        turned_ref[...] = low_ref[...].T

    widen_block(low_ref, w_ref, wb_ref, g_ref, gp_ref, z_ref)


def widen_block(low_ref, w_ref, wb_ref, g_ref, gp_ref, z_ref):
    rows = 64
    z_ref[...] = dotf(low_ref[...], w_ref[...].reshape(low_ref.shape[1], -1), NN)

    def step(i, carry):
        at = pl.ds(i * rows, rows)
        value, slope = gelu_pair(z_ref[at, :] + wb_ref[...])
        g_ref[at, :] = value.astype(jnp.bfloat16)
        gp_ref[at, :] = slope
        return carry

    lax.fori_loop(0, z_ref.shape[0] // rows, step, 0)


def widen(core, mixed_own, mixed_other, rest, narrow_rows, inputs, rows_float, widen_bias):
    rows, width = inputs.shape
    chips = rest.shape[0]
    shard = width // chips
    blocks = widen_bias.shape[1] // width
    half = width // 2
    start = narrow_rows // shard
    fixed = lambda shape: pl.BlockSpec(shape, lambda j, c: (0,) * len(shape))
    return pl.pallas_call(
        widen_kernel,
        grid_spec=pltpu.PrefetchScalarGridSpec(
            num_scalar_prefetch=1,
            grid=(blocks,),
            in_specs=[
                pl.BlockSpec((rows, half), lambda j, c: (c[0], 0)),
                pl.BlockSpec((rows, half), lambda j, c: (c[0], 0)),
                pl.BlockSpec((chips // 2, shard, width), lambda j, c: (c[0], start, 0)),
                pl.BlockSpec((chips // 2, shard, width), lambda j, c: (1 - c[0], start, 0)),
                fixed((rows, width)),
                fixed(rows_float.shape),
                pl.BlockSpec((chips, shard, width), lambda j, c: (0, start + 1 + j, 0)),
                pl.BlockSpec((1, width), lambda j, c: (0, j)),
            ],
            out_specs=[
                fixed((rows, width)),
                fixed((width, rows)),
                fixed((rows, width)),
                fixed((rows, 1)),
                pl.BlockSpec((rows, width), lambda j, c: (0, j)),
                pl.BlockSpec((rows, width), lambda j, c: (0, j)),
            ],
            scratch_shapes=[pltpu.VMEM((rows, width), jnp.float32)],
        ),
        out_shape=[
            jax.ShapeDtypeStruct((rows, width), jnp.bfloat16),
            jax.ShapeDtypeStruct((width, rows), jnp.bfloat16),
            jax.ShapeDtypeStruct((rows, width), jnp.float32),
            jax.ShapeDtypeStruct((rows, 1), jnp.float32),
            jax.ShapeDtypeStruct((rows, blocks * width), jnp.bfloat16),
            jax.ShapeDtypeStruct((rows, blocks * width), jnp.float32),
        ],
        compiler_params=pltpu.CompilerParams(vmem_limit_bytes=20 * 2**20),
        cost_estimate=cost(12.5),
        name="widen",
    )(core, mixed_own, mixed_other, rest, rest, inputs, rows_float, rest, widen_bias)


def back_kernel(core_ref, dm_ref, grad_two_ref, normed_ref, inverse_ref, rows_ref, narrow_ref, w_ref, gp_ref,
                mix_ref, *refs, spare):
    (dz_own_ref, dz_other_ref, columns_ref, one_ref, da_ref, da_other_ref, do_ref, do_other_ref, sums_ref,
     acc_ref) = refs[spare:]
    j = pl.program_id(0)
    rows, width = dm_ref.shape
    half = width // 2
    at_other = pl.ds(pl.multiple_of((1 - core_ref[0]) * half, half), half)
    dz = dotf(dm_ref[...], narrow_ref[...].reshape(width, width), NT) * gp_ref[...]
    dz = dz.astype(jnp.bfloat16)
    own_turn = j >= pl.num_programs(0) // 2

    @pl.when(own_turn)
    def _():
        dz_own_ref[...] = dz

    @pl.when(jnp.logical_not(own_turn))
    def _():
        dz_other_ref[...] = dz

    sums = jnp.broadcast_to(jnp.sum(dz.astype(jnp.float32), axis=0, keepdims=True), (128, width)).T
    shard = mix_ref.shape[1]
    chips = columns_ref.shape[0] // shard
    each = width // chips // shard
    lanes = lax.broadcasted_iota(jnp.int32, (shard, 128), 1)
    for chip in range(chips):
        total = jnp.zeros((shard, 128), jnp.float32)
        for k in range(each):
            at = (chip * each + k) * shard
            total = jnp.where(lanes == 8 + k, sums[at : at + shard, :], total)
        columns_ref[chip * shard : (chip + 1) * shard, :] = total
    part = dotf(dz, w_ref[...].reshape(width, -1), NT)

    @pl.when(j == 0)
    def _():
        acc_ref[...] = grad_two_ref[...] + part

    @pl.when(j > 0)
    def _():
        acc_ref[...] += part

    @pl.when(j == pl.num_programs(0) - 1)
    def _():
        first_grad = acc_ref[...]
        normed = normed_ref[...]
        inner = first_grad * rows_ref[4:5, :]
        one = inverse_ref[...] * (
            inner
            - jnp.mean(inner, axis=1, keepdims=True)
            - normed * jnp.mean(inner * normed, axis=1, keepdims=True)
        )
        one_ref[...] = one
        low = one.astype(jnp.bfloat16)
        da_ref[...] = low
        da_other_ref[...] = da_ref[:, at_other]
        do_ref[...] = dotf(low, mix_ref[...].reshape(width, width), NT).astype(jnp.bfloat16)
        do_other_ref[...] = do_ref[:, at_other]
        sums_ref[0:1, :] = jnp.sum(first_grad * normed, axis=0, keepdims=True)
        sums_ref[1:2, :] = jnp.sum(first_grad, axis=0, keepdims=True)
        sums_ref[2:3, :] = jnp.sum(low.astype(jnp.float32), axis=0, keepdims=True)


def back(core, dm, grad_two, normed, inverse, rows_float, rest, narrow_rows, gp, chips, before):
    rows, width = dm.shape
    shard = width // chips
    half = width // 2
    blocks = gp.shape[1] // width
    start = narrow_rows // shard
    at = lambda j, c: (j + (1 - c[0]) * (blocks // 2)) % blocks
    fixed = lambda shape: pl.BlockSpec(shape, lambda j, c: (0,) * len(shape))
    low = lambda shape: jax.ShapeDtypeStruct(shape, jnp.bfloat16)
    return pl.pallas_call(
        functools.partial(back_kernel, spare=len(before)),
        grid_spec=pltpu.PrefetchScalarGridSpec(
            num_scalar_prefetch=1,
            grid=(blocks,),
            in_specs=[
                fixed((rows, width)),
                fixed((rows, width)),
                fixed((rows, width)),
                fixed((rows, 1)),
                fixed(rows_float.shape),
                pl.BlockSpec((width // narrow_rows, narrow_rows, width), lambda j, c: (at(j, c), 0, 0)),
                pl.BlockSpec((chips, shard, width), lambda j, c: (0, start + 1 + at(j, c), 0)),
                pl.BlockSpec((rows, width), lambda j, c: (0, at(j, c))),
                pl.BlockSpec((chips, shard, width), lambda j, c: (0, start, 0)),
            ]
            + [pl.BlockSpec(memory_space=pl.ANY)] * len(before),
            out_specs=[
                pl.BlockSpec((rows, width), lambda j, c: (0, jnp.maximum(j - blocks // 2, 0))),
                pl.BlockSpec((rows, width), lambda j, c: (0, jnp.minimum(j, blocks // 2 - 1))),
                pl.BlockSpec((width // blocks, 128), lambda j, c: (at(j, c), 0)),
                fixed((rows, width)),
                fixed((rows, width)),
                fixed((rows, half)),
                fixed((rows, width)),
                fixed((rows, half)),
                fixed((8, width)),
            ],
            scratch_shapes=[pltpu.VMEM((rows, width), jnp.float32)],
        ),
        out_shape=[
            low((rows, blocks // 2 * width)),
            low((rows, blocks // 2 * width)),
            jax.ShapeDtypeStruct((width, 128), jnp.float32),
            jax.ShapeDtypeStruct((rows, width), jnp.float32),
            low((rows, width)),
            low((rows, half)),
            low((rows, width)),
            low((rows, half)),
            jax.ShapeDtypeStruct((8, width), jnp.float32),
        ],
        compiler_params=pltpu.CompilerParams(vmem_limit_bytes=56 * 2**20),
        cost_estimate=cost(13.8),
        name="back",
    )(core, dm, grad_two, normed, inverse, rows_float, rest, rest, gp, rest, *before)


def tokens_kernel(core_ref, grad_ref, w_ref, one_ref, *refs):
    own_ref, other_ref = refs[-2:]
    half = w_ref.shape[1] // 3

    def part():
        total = 0.0
        for pair in range(half // 128):
            for kind in range(3):
                at = kind * half + pair * 128
                start = pair * 384 + kind * 128
                total += dotf(grad_ref[:, start : start + 128], w_ref[:, at : at + 128], NT)
        return total

    @pl.when(pl.program_id(0) == 0)
    def _():
        other_ref[...] = part()

    @pl.when(pl.program_id(0) == 1)
    def _():
        own_ref[...] = part() + one_ref[...]


def tokens_grad(core, grad, w_own, grad_one, before):
    rows, width = grad_one.shape
    fixed = lambda shape: pl.BlockSpec(shape, lambda i, c: (0,) * len(shape))
    return pl.pallas_call(
        tokens_kernel,
        grid_spec=pltpu.PrefetchScalarGridSpec(
            num_scalar_prefetch=1,
            grid=(2,),
            in_specs=[
                pl.BlockSpec((rows, grad.shape[1]), lambda i, c: (jnp.where(i == 0, 1 - c[0], c[0]), 0)),
                fixed(w_own.shape),
                fixed((rows, width)),
            ]
            + [pl.BlockSpec(memory_space=pl.ANY)] * len(before),
            out_specs=[fixed((rows, width)), fixed((rows, width))],
        ),
        out_shape=[jax.ShapeDtypeStruct((rows, width), jnp.float32)] * 2,
        compiler_params=pltpu.CompilerParams(vmem_limit_bytes=20 * 2**20),
        cost_estimate=cost(100.0),
        name="tokens_grad",
    )(core, grad, w_own, grad_one, *before)


def widen_grad_kernel(own_ref, other_ref, grad_own_ref, grad_other_ref, left_ref, right_ref):
    term = dotf(own_ref[...], grad_own_ref[...], NN) + dotf(other_ref[...], grad_other_ref[...], NN)

    @pl.when(pl.program_id(0) == 0)
    def _():
        left_ref[...] = term.astype(jnp.bfloat16)

    @pl.when(pl.program_id(0) == 1)
    def _():
        right_ref[...] = term.astype(jnp.bfloat16)


def widen_grad(turned, turned_other, grad, grad_other):
    width, rows = turned.shape
    columns = grad.shape[1] // 2
    fixed = lambda shape: pl.BlockSpec(shape, lambda i: (0, 0))
    return pl.pallas_call(
        widen_grad_kernel,
        grid=(2,),
        in_specs=[fixed((width, rows))] * 2 + [pl.BlockSpec((rows, columns), lambda i: (0, i))] * 2,
        out_specs=[fixed((width, columns))] * 2,
        out_shape=[jax.ShapeDtypeStruct((width, columns), jnp.bfloat16)] * 2,
        compiler_params=pltpu.CompilerParams(vmem_limit_bytes=16 * 2**20),
        cost_estimate=cost(4.0),
        name="widen_grad",
    )(turned, turned_other, grad, grad_other)


def last_grad_kernel(core_ref, turned_ref, grad_ref, mixing_ref, grad_sums_ref, first_ref, second_ref, widen_ref,
                     left_ref, right_ref):
    half = mixing_ref.shape[1]
    pairs = grad_ref.shape[1] // 384
    left_ref[:, :half] = mixing_ref[...]
    for pair in range(pairs):
        term = dotf(turned_ref[...], grad_ref[:, pair * 384 : pair * 384 + 384], NN).astype(jnp.bfloat16)
        if pair == 0:
            left_ref[:, half:] = term
        else:
            right_ref[:, pair * 384 - 384 : pair * 384] = term

    def columns(rows):
        place = lax.broadcasted_iota(jnp.int32, (128, rows[0][1].shape[1]), 0)
        total = 0.0
        for at, row in rows:
            total = jnp.where(place == at, row, total)
        return total.T

    small = pl.ds(pairs * 384 - 384, 128)
    given = [(2, first_ref[2:3, :]), (3, second_ref[0:1, :]), (4, first_ref[0:1, :])]
    given += [(5, first_ref[1:2, :]), (6, second_ref[1:2, :]), (7, second_ref[2:3, :])]
    right_ref[:, small] = (columns(given) + widen_ref[...]).astype(jnp.bfloat16)
    sums = grad_sums_ref[0:1, :]
    queries = jnp.concatenate([sums[:, pair * 384 : pair * 384 + 128] for pair in range(pairs)], axis=1)
    values = jnp.concatenate([sums[:, pair * 384 + 256 : pair * 384 + 384] for pair in range(pairs)], axis=1)
    at = pl.ds(pl.multiple_of(core_ref[0] * half, half), half)
    right_ref[at, small] = right_ref[at, small] + columns([(0, queries), (1, values)]).astype(jnp.bfloat16)


def last_grad(core, turned, grad, mixing_term, grad_sums, first_sums, second_sums, widen_columns):
    width = turned.shape[0]
    columns = grad.shape[1]
    whole = pl.BlockSpec(memory_space=pltpu.VMEM)
    return pl.pallas_call(
        last_grad_kernel,
        in_specs=[pl.BlockSpec(memory_space=pltpu.SMEM)] + [whole] * 7,
        out_specs=[whole] * 2,
        out_shape=[
            jax.ShapeDtypeStruct((width, width // 2 + 384), jnp.bfloat16),
            jax.ShapeDtypeStruct((width, columns - 384 + 128), jnp.bfloat16),
        ],
        compiler_params=pltpu.CompilerParams(vmem_limit_bytes=16 * 2**20),
        cost_estimate=cost(4.0),
        name="last_grad",
    )(core, turned, grad, mixing_term, grad_sums, first_sums, second_sums, widen_columns)


def finish_kernel(core_ref, own_ref, other_ref, *refs, half):
    project_ref, mixing_ref, small_ref = refs[-3:]
    for ref, core in ((own_ref, core_ref[0]), (other_ref, 1 - core_ref[0])):
        mixing_ref[:, pl.ds(pl.multiple_of(core * half, half), half)] = ref[:, :half]
        for pair in range(half // 128):
            for kind in range(3):
                start = half + pair * 384 + kind * 128
                to = pl.multiple_of(core * half + (kind * 2 * half + pair * 128), 128)
                project_ref[:, pl.ds(to, 128)] = ref[:, start : start + 128]
    small = own_ref[:, 4 * half :] + other_ref[:, 4 * half :]
    small_ref[...] = small.T


def finish(core, share, other, half, before):
    rows = share.shape[0]
    whole = pl.BlockSpec(memory_space=pltpu.VMEM)
    return pl.pallas_call(
        functools.partial(finish_kernel, half=half),
        in_specs=[pl.BlockSpec(memory_space=pltpu.SMEM)] + [whole] * 2 + [pl.BlockSpec(memory_space=pl.ANY)] * len(before),
        out_specs=[whole] * 3,
        out_shape=[
            jax.ShapeDtypeStruct((rows, 6 * half), jnp.float32),
            jax.ShapeDtypeStruct((rows, 2 * half), jnp.float32),
            jax.ShapeDtypeStruct((128, rows), jnp.float32),
        ],
        compiler_params=pltpu.CompilerParams(vmem_limit_bytes=8 * 2**20),
        cost_estimate=cost(2.0),
        name="finish",
    )(core, share, other, *before)


def narrow_kernel(core_ref, g_ref, w_ref, normed_ref, rows_ref, cot_ref,
                  result_ref, two_ref, dm_ref, dm_own_ref, dm_other_ref, sums_ref, acc_ref):
    j = pl.program_id(0)
    width = w_ref.shape[2]
    half = width // 2
    at_own = pl.ds(pl.multiple_of(core_ref[0] * half, half), half)
    at_other = pl.ds(pl.multiple_of((1 - core_ref[0]) * half, half), half)

    @pl.when(j == 0)
    def _():
        acc_ref[...] = jnp.zeros_like(acc_ref)

    acc_ref[...] += dotf(g_ref[...], w_ref[...].reshape(width, width), NN)

    @pl.when(j == pl.num_programs(0) - 1)
    def _():
        hidden = normed_ref[...] * rows_ref[4:5, :] + rows_ref[5:6, :] + (acc_ref[...] + rows_ref[3:4, :])
        centred = hidden - jnp.mean(hidden, axis=1, keepdims=True)
        inverse = lax.rsqrt(jnp.mean(centred * centred, axis=1, keepdims=True) + EPSILON)
        normed = centred * inverse
        result_ref[...] = (normed * rows_ref[6:7, :] + rows_ref[7:8, :]).astype(jnp.bfloat16)
        cot = cot_ref[...].astype(jnp.float32)
        inner = cot * rows_ref[6:7, :]
        two = inverse * (
            inner
            - jnp.mean(inner, axis=1, keepdims=True)
            - normed * jnp.mean(inner * normed, axis=1, keepdims=True)
        )
        two_ref[...] = two
        dm = two.astype(jnp.bfloat16)
        dm_ref[...] = dm
        dm_own_ref[...] = dm_ref[:, at_own]
        dm_other_ref[...] = dm_ref[:, at_other]
        sums_ref[0:1, :] = jnp.sum(dm.astype(jnp.float32), axis=0, keepdims=True)
        sums_ref[1:2, :] = jnp.sum(cot * normed, axis=0, keepdims=True)
        sums_ref[2:3, :] = jnp.sum(cot, axis=0, keepdims=True)


def narrow(core, g, rest, narrow_rows, normed, rows_float, cotangent):
    rows, width = normed.shape
    half = width // 2
    fixed = lambda shape: pl.BlockSpec(shape, lambda j, c: (0,) * len(shape))
    return pl.pallas_call(
        narrow_kernel,
        grid_spec=pltpu.PrefetchScalarGridSpec(
            num_scalar_prefetch=1,
            grid=(g.shape[1] // width,),
            in_specs=[
                pl.BlockSpec((rows, width), lambda j, c: (0, j)),
                pl.BlockSpec((width // narrow_rows, narrow_rows, width), lambda j, c: (j, 0, 0)),
                fixed((rows, width)),
                fixed(rows_float.shape),
                fixed((rows, width)),
            ],
            out_specs=[
                fixed((rows, width)),
                fixed((rows, width)),
                fixed((rows, width)),
                fixed((rows, half)),
                fixed((rows, half)),
                fixed((8, width)),
            ],
            scratch_shapes=[pltpu.VMEM((rows, width), jnp.float32)],
        ),
        out_shape=[
            jax.ShapeDtypeStruct((rows, width), jnp.bfloat16),
            jax.ShapeDtypeStruct((rows, width), jnp.float32),
            jax.ShapeDtypeStruct((rows, width), jnp.bfloat16),
            jax.ShapeDtypeStruct((rows, half), jnp.bfloat16),
            jax.ShapeDtypeStruct((rows, half), jnp.bfloat16),
            jax.ShapeDtypeStruct((8, width), jnp.float32),
        ],
        compiler_params=pltpu.CompilerParams(vmem_limit_bytes=20 * 2**20),
        cost_estimate=cost(8.0),
        name="narrow",
    )(core, g, rest, normed, rows_float, cotangent)


def narrow_grad_kernel(own_ref, other_ref, dm_own_ref, dm_other_ref, out_ref):
    term = dotf(own_ref[...], dm_own_ref[...], TN) + dotf(other_ref[...], dm_other_ref[...], TN)
    out_ref[...] = term.reshape(out_ref.shape).astype(jnp.bfloat16)


def narrow_grad(g, g_other, dm_own, dm_other, chips):
    rows, hidden = g.shape
    half = dm_own.shape[1]
    lines = chips // 4
    size = hidden // lines
    fixed = lambda shape: pl.BlockSpec(shape, lambda j: (0, 0))
    return pl.pallas_call(
        narrow_grad_kernel,
        grid=(lines,),
        in_specs=[pl.BlockSpec((rows, size), lambda j: (0, j))] * 2 + [fixed((rows, half))] * 2,
        out_specs=pl.BlockSpec((4, 1, size // 4, half), lambda j: (0, j, 0, 0)),
        out_shape=jax.ShapeDtypeStruct((4, lines, size // 4, half), jnp.bfloat16),
        compiler_params=pltpu.CompilerParams(vmem_limit_bytes=12 * 2**20),
        cost_estimate=cost(4.5),
        name="narrow_grad",
    )(g, g_other, dm_own, dm_other)


def mixing_grad_kernel(core_ref, own_ref, other_ref, grad_ref, grad_other_ref, *refs):
    out_ref = refs[-1]
    rows, half = grad_other_ref.shape
    core = core_ref[0]
    here = pl.ds(pl.multiple_of(core * rows, rows), rows)
    there = pl.ds(pl.multiple_of((1 - core) * rows, rows), rows)
    at_own = pl.ds(pl.multiple_of(core * half, half), half)
    at_other = pl.ds(pl.multiple_of((1 - core) * half, half), half)
    grad = grad_ref[:, at_own]
    grad_other = grad_other_ref[...]
    for ref, at in ((own_ref, at_own), (other_ref, at_other)):
        term = dotf(ref[here, :], grad, TN) + dotf(ref[there, :], grad_other, TN)
        out_ref[at, :] = term.astype(jnp.bfloat16)


def mixing_grad(core, mixed_own, mixed_other, grad, grad_other):
    width = grad.shape[1]
    whole = pl.BlockSpec(memory_space=pltpu.VMEM)
    return pl.pallas_call(
        mixing_grad_kernel,
        in_specs=[pl.BlockSpec(memory_space=pltpu.SMEM)] + [whole] * 4,
        out_specs=whole,
        out_shape=jax.ShapeDtypeStruct((width, width // 2), jnp.bfloat16),
        compiler_params=pltpu.CompilerParams(vmem_limit_bytes=12 * 2**20),
        cost_estimate=cost(2.0),
        name="mixing_grad",
    )(core, mixed_own, mixed_other, grad, grad_other)


def qkv_kernel(place_ref, x_ref, left_ref, left_other_ref, right_ref, right_other_ref, joined_ref, w_ref, rows_ref,
               small_ref, *, small_at, far):
    core = place_ref[0]
    y = place_ref[far + 1]
    x = place_ref[far + 2]
    shard, cut = left_ref.shape[-2:]
    lines = left_ref.shape[0]
    for line in range(lines):
        for ref, bit in ((left_ref, y), (left_other_ref, 1 - y)):
            to = pl.multiple_of((line * 4 + bit * 2) * shard, 2 * shard)
            w_ref[pl.ds(to, 2 * shard), :cut] = ref[line].reshape(2 * shard, cut)
        for ref, bit in ((right_ref, x), (right_other_ref, 1 - x)):
            for row in range(2):
                to = pl.multiple_of((line * 4 + row * 2 + bit) * shard, shard)
                w_ref[pl.ds(to, shard), cut:] = ref[line, row, :, :small_at]
                small_ref[pl.ds(to, shard), :] = ref[line, row, :, small_at:].astype(jnp.float32)
    rows_ref[...] = small_ref[...].T[: rows_ref.shape[0]]
    half = w_ref.shape[1] // 3
    at = pl.ds(pl.multiple_of(core * half, half), half)
    product = dotf(x_ref[...], w_ref[...], NN)
    joined_ref[:, :half] = (product[:, :half] + rows_ref[0:1, at]).astype(jnp.bfloat16)
    joined_ref[:, half : 2 * half] = product[:, half : 2 * half].astype(jnp.bfloat16)
    joined_ref[:, 2 * half :] = (product[:, 2 * half :] + rows_ref[1:2, at]).astype(jnp.bfloat16)


def qkv(place, inputs, left, left_other, right, right_other, small_at):
    shard, cut = left.shape[-2:]
    length, width = inputs.shape
    far = left.ndim - 4
    lines = 2**far
    left, left_other = left.reshape(lines, 2, shard, cut), left_other.reshape(lines, 2, shard, cut)
    right, right_other = right.reshape(lines, 2, shard, cut), right_other.reshape(lines, 2, shard, cut)
    whole = pl.BlockSpec(memory_space=pltpu.VMEM)
    return pl.pallas_call(
        functools.partial(qkv_kernel, small_at=small_at, far=far),
        in_specs=[pl.BlockSpec(memory_space=pltpu.SMEM)] + [whole] * 5,
        out_specs=[whole] * 3,
        out_shape=[
            jax.ShapeDtypeStruct((length, cut + small_at), jnp.bfloat16),
            jax.ShapeDtypeStruct((width, cut + small_at), jnp.bfloat16),
            jax.ShapeDtypeStruct((16, width), jnp.float32),
        ],
        scratch_shapes=[pltpu.VMEM((width, 128), jnp.float32)],
        compiler_params=pltpu.CompilerParams(vmem_limit_bytes=56 * 2**20),
        cost_estimate=cost(4.0),
        name="qkv",
    )(place, inputs, left, left_other, right, right_other)


def pack_kernel(core_ref, narrow_ref, mixing_ref, widen_ref, project_ref, biases_ref, norms_ref, hidden_ref,
                rest_ref, packed_ref):
    core = core_ref[0]
    shard, width = mixing_ref.shape
    half = width // 2
    split = rest_ref.shape[0] - narrow_ref.shape[0]
    blocks = widen_ref.shape[1] // width

    @pl.when(core == 0)
    def _():
        rest_ref[: narrow_ref.shape[0]] = narrow_ref[...]
        rest_ref[narrow_ref.shape[0] :] = mixing_ref[:split]

    @pl.when(core == 1)
    def _():
        rest_ref[: shard - split] = mixing_ref[split:]
        for block in range(blocks):
            at = shard - split + block * shard
            rest_ref[at : at + shard] = widen_ref[:, block * width : (block + 1) * width]
        at = shard - split + blocks * shard
        if at < rest_ref.shape[0]:
            rest_ref[at:] = jnp.zeros((rest_ref.shape[0] - at, width), jnp.bfloat16)

    for kind in range(3):
        from_ = pl.ds(pl.multiple_of(core * half + kind * width, half), half)
        packed_ref[:, kind * half : (kind + 1) * half] = project_ref[:, from_]
    place = lax.broadcasted_iota(jnp.int32, (128, shard), 0)
    total = jnp.zeros((128, shard), jnp.float32)
    at = 0
    for ref in (biases_ref, norms_ref, hidden_ref):
        for row in range(ref.shape[0]):
            total = jnp.where(place == at, ref[row : row + 1, :].astype(jnp.float32), total)
            at += 1
    packed_ref[:, 3 * half :] = total.T.astype(jnp.bfloat16)


def pack(core, narrowing, mixing, widening, projection, biases, norms, hidden):
    shard, width = mixing.shape
    rows = narrowing.shape[0] + shard + widening.shape[1] // width * shard
    half_rows = -(-rows // 32) * 16
    whole = pl.BlockSpec(memory_space=pltpu.VMEM)
    return pl.pallas_call(
        pack_kernel,
        in_specs=[pl.BlockSpec(memory_space=pltpu.SMEM)] + [whole] * 7,
        out_specs=[whole] * 2,
        out_shape=[
            jax.ShapeDtypeStruct((half_rows, width), jnp.bfloat16),
            jax.ShapeDtypeStruct((shard, projection.shape[1] // 2 + 128), jnp.bfloat16),
        ],
        compiler_params=pltpu.CompilerParams(vmem_limit_bytes=60 * 2**20),
        cost_estimate=cost(2.0),
        name="pack",
    )(core, narrowing, mixing, widening, projection, biases, norms, hidden)


AXES = ("fsdp", "ctx")


def core_permute(value, chips):
    pairs = [(2 * f + c, 2 * f + 1 - c) for f in range(chips) for c in range(2)]
    return lax.ppermute(value, AXES, pairs)


def chip_permute(value, chips, mask):
    pairs = [(2 * f + c, 2 * (f ^ mask) + c) for f in range(chips) for c in range(2)]
    return lax.ppermute(value, AXES, pairs)


def chip_bit(mask):
    return (lax.axis_index("fsdp") // mask) % 2


def by_core(mine, other, axis):
    core = lax.axis_index("ctx")
    first = jnp.where(core == 0, mine, other)
    second = jnp.where(core == 0, other, mine)
    return jnp.concatenate([first, second], axis=axis)


def dims_of(chips):
    return [1 << b for b in reversed(range(chips.bit_length() - 1))]


def gather_step(value, chips, mask):
    axis = dims_of(chips).index(mask)
    other = chip_permute(value, chips, mask)
    bit = chip_bit(mask)
    first = jnp.where(bit == 0, value, other)
    second = jnp.where(bit == 0, other, value)
    return jnp.concatenate([first, second], axis=axis)


def bits_of(chips):
    return jnp.stack([chip_bit(mask) for mask in dims_of(chips)])


def first_send(value, chips, mask):
    shape = [chips // (2 * mask), 2, mask] + list(value.shape[1:])
    send = lax.dynamic_index_in_dim(value.reshape(shape), 1 - chip_bit(mask), 1, keepdims=False)
    return send.reshape(chips // 2, *value.shape[1:])


def block_at(step, left, free, fixed):
    index = 0
    for place, mask in enumerate(left):
        if mask in fixed:
            bit = fixed[mask]
        else:
            bit = (step // 2 ** (len(free) - 1 - free.index(mask))) % 2
        index = index + bit * 2 ** (len(left) - 1 - place)
    return index


def hop_kernel(bits_ref, *refs, parts, merged, spare):
    outs = refs[4 * parts + spare :]
    at = 0
    for part in range(parts):
        away, away_in, keep, keep_in = refs[4 * part : 4 * part + 4]
        columns = away.shape[2]
        send_ref, keep_ref = outs[:2] if merged else outs[2 * part : 2 * part + 2]
        where = pl.ds(at, columns)
        send_ref[:, :, where] = (away[...].astype(jnp.float32) + away_in[...].astype(jnp.float32)).astype(jnp.bfloat16)
        keep_ref[:, :, where] = keep[...].astype(jnp.float32) + keep_in[...].astype(jnp.float32)
        if merged:
            at += columns


def hop(parts, bits, chips, before, merged):
    masks = dims_of(chips)
    in_specs, operands, out_columns = [], [], []
    steps = 2 ** (len([mask for mask in parts[0][2] if mask != parts[0][3]]) - 1)
    for value, arrived, left, came, goes in parts:
        rows, columns = value.shape[1:]
        rest = [mask for mask in left if mask != came]
        free = [mask for mask in rest if mask != goes]
        block = (1, rows, columns)
        for flip in (1, 0):
            def at_value(i, b, left=left, free=free, came=came, goes=goes, flip=flip):
                mine = b[masks.index(goes)]
                side = 1 - mine if flip else mine
                return block_at(i, left, free, {came: b[masks.index(came)], goes: side}), 0, 0

            def at_arrived(i, b, rest=rest, free=free, goes=goes, flip=flip):
                mine = b[masks.index(goes)]
                return block_at(i, rest, free, {goes: 1 - mine if flip else mine}), 0, 0

            in_specs += [pl.BlockSpec(block, at_value), pl.BlockSpec(block, at_arrived)]
            operands += [value, arrived]
        out_columns.append(columns)
    if merged:
        out_columns = [sum(out_columns)]
    out_specs, out_shape = [], []
    for columns in out_columns:
        out_specs += [pl.BlockSpec((1, rows, columns), lambda i, b: (i, 0, 0))] * 2
        out_shape += [
            jax.ShapeDtypeStruct((steps, rows, columns), jnp.bfloat16),
            jax.ShapeDtypeStruct((steps, rows, columns), jnp.float32),
        ]
    outs = pl.pallas_call(
        functools.partial(hop_kernel, parts=len(parts), merged=merged, spare=len(before)),
        grid_spec=pltpu.PrefetchScalarGridSpec(
            num_scalar_prefetch=1,
            grid=(steps,),
            in_specs=in_specs + [pl.BlockSpec(memory_space=pl.ANY)] * len(before),
            out_specs=out_specs,
        ),
        out_shape=out_shape,
        compiler_params=pltpu.CompilerParams(vmem_limit_bytes=8 * 2**20),
        cost_estimate=cost(2.0),
        name="hop",
    )(bits, *operands, *before)
    return list(outs[0::2]), list(outs[1::2])


class Chain:
    def __init__(self, values, chips, bits):
        self.chips, self.bits, self.masks = chips, bits, dims_of(chips)
        self.far = self.masks[:-2]
        self.order = ([1, 2], [2, 1])
        self.kept = values
        self.sent = [first_send(part, chips, order[0]) for part, order in zip(self.kept, self.order)]

    def move(self, masks):
        self.arrived = [chip_permute(part, self.chips, mask) for part, mask in zip(self.sent, masks)]

    def first(self):
        self.move([1, 2])

    def second(self, before):
        self.sent, self.kept = hop(
            [
                (kept, arrived, self.masks, order[0], order[1])
                for kept, arrived, order in zip(self.kept, self.arrived, self.order)
            ],
            self.bits, self.chips, before, False,
        )
        self.move([2, 1])

    def third(self, before, others=()):
        parts = [
            (kept, arrived, self.far, order[1], self.far[-1])
            for chain in (self, *others)
            for kept, arrived, order in zip(chain.kept, chain.arrived, chain.order)
        ]
        self.sent, self.kept = hop(parts, self.bits, self.chips, before, True)
        self.move([self.far[-1]])

    def fourth(self, before):
        for at in range(len(self.far) - 1, 0, -1):
            part = (self.kept[0], self.arrived[0], self.far[:at], self.far[at], self.far[at - 1])
            self.sent, self.kept = hop([part], self.bits, self.chips, before, True)
            self.move([self.far[at - 1]])

    def last(self):
        return self.kept[0][0] + self.arrived[0][0].astype(jnp.float32)


def groups_of(chips):
    near = [list(range(at, at + 4)) for at in range(0, chips, 4)]
    far = [list(range(at, chips, 4)) for at in range(4)]
    return near, far


def core_half(value, axis, own):
    core = lax.axis_index("ctx")
    size = value.shape[axis] // 2
    which = core if own else 1 - core
    return lax.dynamic_slice_in_dim(value, which * size, size, axis)


def fast_body(
    tokens, lengths, cotangent, projection, mixing, widening, narrowing, biases, widen_bias, norms
):
    chips = lax.axis_size("fsdp")
    core = lax.axis_index("ctx")
    core_at = core.reshape(1)
    bits = dims_of(chips)
    far = bits[:-2]
    down_x = [1, 2] + far[::-1]
    down_y = [2, 1] + far[::-1]
    inputs = tokens[0]
    row_count, model_width = inputs.shape
    shard = projection.shape[0]
    half = model_width // 2
    swap = lambda value: core_permute(value, chips)

    hidden = widen_bias.shape[0] // shard
    rest, packed = pack(core_at, narrowing, mixing, widening, projection, biases, norms, widen_bias.reshape(hidden, shard))
    rest = lax.all_gather(rest, AXES, axis=0, tiled=True).reshape(chips, -1, model_width)
    packed = packed.reshape([1] * len(bits) + [shard, packed.shape[1]])
    cut = packed.shape[-1] // 2
    for mask in far:
        packed = gather_step(packed, chips, mask)
    left = gather_step(packed[..., :cut], chips, 1)
    right = gather_step(packed[..., cut:], chips, 2)
    left_other = chip_permute(left, chips, 2)
    right_other = chip_permute(right, chips, 1)

    narrow_rows = narrowing.shape[0]

    all_inputs = by_core(inputs, swap(inputs), 0)
    inputs_turned = all_inputs.T
    chip_bits = bits_of(chips)
    small_at = 3 * half - cut
    joined, w_own, rows_float = qkv(
        jnp.concatenate([core_at, chip_bits]), all_inputs, left, left_other, right, right_other, small_at
    )
    widen_float = rows_float[8 : 8 + hidden].reshape(hidden, chips, shard).transpose(1, 0, 2).reshape(1, -1)
    mixed_own, logsum = attn_fwd(lengths, joined, [inputs_turned])
    mixed_other = swap(mixed_own)
    first_low, first_turned, normed_one, inverse_one, active_low, slope = widen(
        core_at, mixed_own, mixed_other, rest, narrow_rows, inputs, rows_float, widen_float
    )
    first_other = swap(first_turned)
    active_other = swap(active_low)
    result, grad_two, second_grad, dm_own, dm_other, second_sums = narrow(
        core_at, active_low, rest, narrow_rows, normed_one, rows_float, cotangent[0]
    )

    near, line = groups_of(chips)
    narrow_term = narrow_grad(active_low, active_other, dm_own, swap(dm_other), chips)
    narrow_near = lax.psum_scatter(
        narrow_term, "fsdp", scatter_dimension=0, axis_index_groups=near, tiled=True
    ).reshape(chips // 4, narrow_rows, half)

    (
        expand_own, expand_other, widen_columns, grad_one, branch_grad, branch_other, mixed_grad, mixed_other_grad,
        first_sums,
    ) = back(
        core_at, second_grad, grad_two, normed_one, inverse_one, rows_float,
        rest, narrow_rows, slope, chips, [narrow_term],
    )
    mixed_grad_other = swap(mixed_other_grad)
    branch_other = swap(branch_other)
    widen_terms_two = widen_grad(first_turned, first_other, expand_own, swap(expand_other))
    widen_chain = Chain([term.reshape(chips, shard, -1) for term in widen_terms_two], chips, chip_bits)
    widen_chain.first()

    mixing_term = mixing_grad(core_at, mixed_own, mixed_other, branch_grad, branch_other)

    grad, grad_sums = attn_bwd(
        core_at, lengths, joined, mixed_grad, mixed_grad_other, logsum, widen_chain.sent + [mixing_term]
    )
    narrow_share = lax.psum_scatter(
        narrow_near, "fsdp", scatter_dimension=0, axis_index_groups=line, tiled=True
    )[0].astype(jnp.float32)
    last_terms = last_grad(
        core_at, inputs_turned, grad, mixing_term, grad_sums, first_sums, second_sums, widen_columns
    )
    last_chain = Chain([term.reshape(chips, shard, -1) for term in last_terms], chips, chip_bits)
    last_chain.first()
    widen_chain.second([grad, narrow_near] + last_chain.sent)
    own_part, other_part = tokens_grad(core_at, grad, w_own, grad_one, last_chain.sent + [narrow_share])
    last_chain.second(widen_chain.sent)
    widen_chain.third(last_chain.sent)
    last_chain.third(widen_chain.sent)
    input_grad = own_part + swap(other_part)
    widen_chain.fourth(last_chain.sent)
    last_chain.fourth(widen_chain.sent)
    join = lambda share: by_core(share, swap(share), 1)
    widen_share = join(widen_chain.last())
    narrow_share = join(narrow_share)
    last_share = last_chain.last()
    other_share = swap(last_share)

    grad_projection, grad_mixing, small_share = finish(
        core_at, last_share, other_share, half, [widen_share, narrow_share]
    )
    return (
        result.astype(jnp.bfloat16)[None],
        input_grad[None],
        grad_projection,
        grad_mixing,
        widen_share,
        narrow_share,
        small_share[:4],
        small_share[8 : 8 + hidden].reshape(-1),
        small_share[4:8],
    )


def solution(mesh):
    in_specs = (
        P("fsdp", "ctx", None),
        P("fsdp"),
        P("fsdp", "ctx", None),
        P("fsdp", None),
        P("fsdp", None),
        P("fsdp", None),
        P("fsdp", None),
        P(None, "fsdp"),
        P("fsdp"),
        P(None, "fsdp"),
    )
    out_specs = (
        P("fsdp", "ctx", None),
        P("fsdp", "ctx", None),
        P("fsdp", None),
        P("fsdp", None),
        P("fsdp", None),
        P("fsdp", None),
        P(None, "fsdp"),
        P("fsdp"),
        P(None, "fsdp"),
    )
    chips = mesh.shape["fsdp"]
    paired = mesh.shape["ctx"] == 2 and chips >= 4 and chips & (chips - 1) == 0
    body = fast_body if paired else general_body
    return jax.shard_map(body, mesh=mesh, in_specs=in_specs, out_specs=out_specs, check_vma=False)
```

```python
import functools

import jax
import jax.numpy as jnp
from jax import lax
from jax.experimental import pallas as pl
from jax.experimental.pallas import tpu as pltpu
from jax.sharding import PartitionSpec as P

HEADS = 12
HEAD_DIM = 64


EPSILON = 1e-12


def split_heads(matrix):
    return matrix.reshape(matrix.shape[0], HEADS, matrix.shape[1] // HEADS)


def pair_scores(left_rows, right_rows, factor):
    return (
        jnp.einsum(
            "ahd,bhd->hab",
            split_heads(left_rows),
            split_heads(right_rows),
            preferred_element_type=jnp.float32,
        )
        * factor
    )


def spread_rows(weights_hab, right_rows):
    out_rows = jnp.einsum(
        "hab,bhd->ahd", weights_hab, split_heads(right_rows), preferred_element_type=jnp.float32
    )
    return out_rows.reshape(out_rows.shape[0], -1)


def collect_rows(weights_hab, left_rows):
    out_rows = jnp.einsum(
        "hab,ahd->bhd", weights_hab, split_heads(left_rows), preferred_element_type=jnp.float32
    )
    return out_rows.reshape(out_rows.shape[0], -1)


def norm_forward(hidden, gain, shift):
    row_mean = jnp.mean(hidden, axis=-1, keepdims=True)
    centred = hidden - row_mean
    inverse = lax.rsqrt(jnp.mean(centred * centred, axis=-1, keepdims=True) + EPSILON)
    normed = centred * inverse
    return (normed * gain + shift, normed, inverse)


def norm_backward(upstream, normed, inverse, gain):
    inner = upstream * gain
    return inverse * (
        inner
        - jnp.mean(inner, axis=-1, keepdims=True)
        - normed * jnp.mean(inner * normed, axis=-1, keepdims=True)
    )


def gelu_exact(values_in):
    return jax.nn.gelu(values_in, approximate=False)


def general_body(
    tokens, lengths, cotangent, projection, mixing, widening, narrowing, biases, widen_bias, norms
):
    score_scale = HEAD_DIM ** (-0.5)
    gathered = (
        lax.all_gather(projection, "fsdp", axis=0, tiled=True),
        lax.all_gather(mixing, "fsdp", axis=0, tiled=True),
        lax.all_gather(widening, "fsdp", axis=0, tiled=True),
        lax.all_gather(narrowing, "fsdp", axis=0, tiled=True),
        lax.all_gather(biases, "fsdp", axis=1, tiled=True),
        lax.all_gather(widen_bias, "fsdp", axis=0, tiled=True),
        lax.all_gather(norms, "fsdp", axis=1, tiled=True),
    )
    w_project, w_mixing, w_widen, w_narrow, bias_rows, widen_all, norm_rows = gathered
    bias_float = bias_rows.astype(jnp.float32)
    widen_float = widen_all.astype(jnp.float32)
    norm_float = norm_rows.astype(jnp.float32)
    inputs = tokens[0]
    row_count, model_width = inputs.shape
    seq_length = lengths[0]
    joined_rows = jnp.dot(inputs, w_project, preferred_element_type=jnp.float32)
    queries = (joined_rows[:, :model_width] + bias_float[0]).astype(jnp.bfloat16)
    key_rows = joined_rows[:, model_width : 2 * model_width].astype(jnp.bfloat16)
    value_rows = (joined_rows[:, 2 * model_width :] + bias_float[1]).astype(jnp.bfloat16)
    all_keys, all_values = (
        lax.all_gather(key_rows, "ctx", axis=0, tiled=True),
        lax.all_gather(value_rows, "ctx", axis=0, tiled=True),
    )
    key_valid = jnp.arange(all_keys.shape[0], dtype=jnp.int32) < seq_length
    scores = jnp.where(key_valid[None, None, :], pair_scores(queries, all_keys, score_scale), -1e30)
    row_peak = jnp.max(scores, axis=-1, keepdims=True)
    exp_terms = jnp.exp(scores - row_peak)
    summed = jnp.sum(exp_terms, axis=-1, keepdims=True)
    prob_low = (exp_terms / summed).astype(jnp.bfloat16)
    logsum = row_peak + jnp.log(summed)
    mixed_low = spread_rows(prob_low, all_values).astype(jnp.bfloat16)
    branch = jnp.dot(mixed_low, w_mixing, preferred_element_type=jnp.float32) + bias_float[2]
    first_norm, normed_one, inverse_one = norm_forward(
        inputs.astype(jnp.float32) + branch, norm_float[0], norm_float[1]
    )
    first_low = first_norm.astype(jnp.bfloat16)
    expanded = jnp.dot(first_low, w_widen, preferred_element_type=jnp.float32) + widen_float
    activated, gelu_pull = jax.vjp(gelu_exact, expanded)
    active_low = activated.astype(jnp.bfloat16)
    second = jnp.dot(active_low, w_narrow, preferred_element_type=jnp.float32) + bias_float[3]
    result, normed_two, inverse_two = norm_forward(
        first_norm + second, norm_float[2], norm_float[3]
    )
    grad_out = cotangent[0].astype(jnp.float32)
    grad_two = norm_backward(grad_out, normed_two, inverse_two, norm_float[2])
    second_grad = grad_two.astype(jnp.bfloat16)
    narrow_term = jnp.einsum(
        "rf,rd->fd", active_low, second_grad, preferred_element_type=jnp.float32
    )
    active_grad = jnp.einsum("rd,fd->rf", second_grad, w_narrow, preferred_element_type=jnp.float32)
    expand_grad = gelu_pull(active_grad)[0].astype(jnp.bfloat16)
    widen_term = jnp.einsum("rd,rf->df", first_low, expand_grad, preferred_element_type=jnp.float32)
    first_grad = grad_two + jnp.einsum(
        "rf,df->rd", expand_grad, w_widen, preferred_element_type=jnp.float32
    )
    grad_one = norm_backward(first_grad, normed_one, inverse_one, norm_float[0])
    branch_grad = grad_one.astype(jnp.bfloat16)
    mixing_term = jnp.einsum(
        "rd,re->de", mixed_low, branch_grad, preferred_element_type=jnp.float32
    )
    mixed_grad = jnp.einsum(
        "re,de->rd", branch_grad, w_mixing, preferred_element_type=jnp.float32
    ).astype(jnp.bfloat16)
    scores = jnp.where(key_valid[None, None, :], pair_scores(queries, all_keys, score_scale), -1e30)
    prob_again = jnp.exp(scores - logsum)
    prob_grad = pair_scores(mixed_grad, all_values, 1.0)
    row_delta = jnp.sum(prob_again * prob_grad, axis=-1, keepdims=True)
    score_grad = (prob_again * (prob_grad - row_delta)).astype(jnp.bfloat16)
    query_grad = (spread_rows(score_grad, all_keys) * score_scale).astype(jnp.bfloat16)
    key_terms = collect_rows(score_grad, queries) * score_scale
    value_terms = collect_rows(prob_low, mixed_grad)
    key_grad, value_grad = (
        lax.psum_scatter(key_terms, "ctx", scatter_dimension=0, tiled=True),
        lax.psum_scatter(value_terms, "ctx", scatter_dimension=0, tiled=True),
    )
    key_low = key_grad.astype(jnp.bfloat16)
    value_low = value_grad.astype(jnp.bfloat16)
    joined_grad = jnp.concatenate([query_grad, key_low, value_low], axis=1)
    project_term = jnp.einsum("rd,re->de", inputs, joined_grad, preferred_element_type=jnp.float32)
    input_grad = (
        jnp.einsum("re,de->rd", joined_grad, w_project, preferred_element_type=jnp.float32)
        + grad_one
    )
    bias_terms = jnp.stack(
        [
            jnp.sum(query_grad.astype(jnp.float32), axis=0),
            jnp.sum(value_low.astype(jnp.float32), axis=0),
            jnp.sum(branch_grad.astype(jnp.float32), axis=0),
            jnp.sum(second_grad.astype(jnp.float32), axis=0),
        ]
    )
    widen_terms = jnp.sum(expand_grad.astype(jnp.float32), axis=0)
    norm_terms = jnp.stack(
        [
            jnp.sum(first_grad * normed_one, axis=0),
            jnp.sum(first_grad, axis=0),
            jnp.sum(grad_out * normed_two, axis=0),
            jnp.sum(grad_out, axis=0),
        ]
    )
    shares = (
        lax.psum_scatter(project_term, "fsdp", scatter_dimension=0, tiled=True),
        lax.psum_scatter(mixing_term, "fsdp", scatter_dimension=0, tiled=True),
        lax.psum_scatter(widen_term, "fsdp", scatter_dimension=0, tiled=True),
        lax.psum_scatter(narrow_term, "fsdp", scatter_dimension=0, tiled=True),
        lax.psum_scatter(bias_terms, "fsdp", scatter_dimension=1, tiled=True),
        lax.psum_scatter(widen_terms, "fsdp", scatter_dimension=0, tiled=True),
        lax.psum_scatter(norm_terms, "fsdp", scatter_dimension=1, tiled=True),
    )
    totals = lax.psum(
        (shares[0], shares[1], shares[2], shares[3], shares[4], shares[5], shares[6]), "ctx"
    )
    return (
        result.astype(jnp.bfloat16)[None],
        input_grad[None],
        totals[0],
        totals[1],
        totals[2],
        totals[3],
        totals[4],
        totals[5],
        totals[6],
    )


NT=(((1,),(1,)),((),()))
NN=(((1,),(0,)),((),()))
def dotf(a,b,dims): return lax.dot_general(a,b,dims,preferred_element_type=jnp.float32)

def cost(microseconds):
    return pl.CostEstimate(flops=int(microseconds * 5e7), bytes_accessed=2**12, transcendentals=0)


def attn_fwd_kernel(len_ref,q_ref,k_ref,v_ref,*refs):
    o_ref,lse_ref,vt_ref=refs[-3:]
    @pl.when(pl.program_id(1)==0)
    def _():
        vt_ref[...]=v_ref[...].T
    n=len_ref[0]
    q=q_ref[...]; k=k_ref[...]
    lanes=lax.broadcasted_iota(jnp.int32,q.shape,1)
    rows=lax.broadcasted_iota(jnp.int32,(k.shape[0],1),0)
    valid=rows<n
    outs = []
    for h in range(2):
        qh=jnp.where((lanes>=64)==(h==1),q*jnp.bfloat16(HEAD_DIM**-0.5),jnp.bfloat16(0))
        s=dotf(k,qh,NT)
        s=jnp.where(valid,s,-1e30)
        m=jnp.max(s,axis=0,keepdims=True)
        e=jnp.exp(s-m)
        l=jnp.sum(e,axis=0,keepdims=True)
        p=(e*(1.0/l)).astype(jnp.bfloat16)
        lse_ref[0,h:h+1,:]=m+jnp.log(l)
        outs.append(dotf(vt_ref[64*h:64*h+64,:],p,NN))
    o=jnp.concatenate(outs,axis=0)
    o_ref[...]=o.T.astype(jnp.bfloat16)

def attn_fwd(length, joined, before, QB=512):
    L = joined.shape[0]
    C = joined.shape[1] // 3
    pairs = C // 128
    QB = min(QB, L)
    return pl.pallas_call(
        attn_fwd_kernel,
        grid=(pairs, L // QB),
        in_specs=[
            pl.BlockSpec(memory_space=pltpu.SMEM),
            pl.BlockSpec((QB, 128), lambda p, i: (i, p)),
            pl.BlockSpec((L, 128), lambda p, i: (0, pairs + p)),
            pl.BlockSpec((L, 128), lambda p, i: (0, 2 * pairs + p)),
        ]
        + [pl.BlockSpec(memory_space=pl.ANY)] * len(before),
        out_specs=[
            pl.BlockSpec((QB, 128), lambda p, i: (i, p)),
            pl.BlockSpec((1, 2, QB), lambda p, i: (p, 0, i)),
        ],
        out_shape=[
            jax.ShapeDtypeStruct((L, C), jnp.bfloat16),
            jax.ShapeDtypeStruct((pairs, 2, L), jnp.float32),
        ],
        scratch_shapes=[pltpu.VMEM((128, L), jnp.bfloat16)],
        compiler_params=pltpu.CompilerParams(vmem_limit_bytes=20 * 2**20),
        cost_estimate=cost(14.5),
        name="attn_fwd",
    )(length, joined, joined, joined, *before)


def attn_bwd_kernel(core_ref, len_ref, q_ref, k_ref, v_ref, do_ref, do_other_ref, lse_ref, *refs):
    df_ref, sum_ref, kt_ref, dka_ref, dva_ref = refs[-5:]
    i = pl.program_id(1)

    @pl.when(i == 0)
    def _():
        kt_ref[...] = k_ref[...].T
        dka_ref[...] = jnp.zeros_like(dka_ref)
        dva_ref[...] = jnp.zeros_like(dva_ref)

    n = len_ref[0]
    scale = jnp.bfloat16(HEAD_DIM**-0.5)
    q = q_ref[...]
    k = k_ref[...]
    v = v_ref[...]
    do = jnp.where(i == core_ref[0], do_ref[...], do_other_ref[...])
    lanes = lax.broadcasted_iota(jnp.int32, q.shape, 1)
    valid = lax.broadcasted_iota(jnp.int32, (k.shape[0], 1), 0) < n
    outs = []
    for h in range(2):
        mine = (lanes >= HEAD_DIM) == (h == 1)
        qh = jnp.where(mine, q * scale, jnp.bfloat16(0))
        doh = jnp.where(mine, do, jnp.bfloat16(0))
        s = dotf(k, qh, NT)
        p = jnp.where(valid, jnp.exp(s - lse_ref[0, h : h + 1, :]), 0.0)
        dp = dotf(v, doh, NT)
        delta = jnp.sum(p * dp, axis=0, keepdims=True)
        ds = (p * (dp - delta)).astype(jnp.bfloat16)
        dva_ref[...] += dotf(p.astype(jnp.bfloat16), doh, NN)
        dka_ref[...] += dotf(ds, qh, NN)
        outs.append(dotf(kt_ref[HEAD_DIM * h : HEAD_DIM * (h + 1), :], ds, NN))
    dq = jnp.concatenate(outs, axis=0) * (HEAD_DIM**-0.5)
    df_ref[pl.ds(pl.multiple_of(i * q.shape[0], q.shape[0]), q.shape[0]), 0:128] = dq.T.astype(jnp.bfloat16)

    @pl.when(i == pl.num_programs(1) - 1)
    def _():
        df_ref[:, 128:256] = dka_ref[...].astype(jnp.bfloat16)
        df_ref[:, 256:384] = dva_ref[...].astype(jnp.bfloat16)
        sum_ref[0:1, :] = jnp.sum(df_ref[...].astype(jnp.float32), axis=0, keepdims=True)


def attn_bwd(core, length, joined, do, do_other, lse, before):
    L = joined.shape[0]
    pairs = joined.shape[1] // 384
    QB = L // 2
    block = lambda at: pl.BlockSpec((QB, 128), lambda p, i, c: (i, at * pairs + p))
    whole = lambda at: pl.BlockSpec((L, 128), lambda p, i, c: (0, at * pairs + p))
    return pl.pallas_call(
        attn_bwd_kernel,
        grid_spec=pltpu.PrefetchScalarGridSpec(
            num_scalar_prefetch=1,
            grid=(pairs, 2),
            in_specs=[
                pl.BlockSpec(memory_space=pltpu.SMEM),
                block(0),
                whole(1),
                whole(2),
                pl.BlockSpec((QB, 128), lambda p, i, c: (0, c[0] * pairs + p)),
                pl.BlockSpec((QB, 128), lambda p, i, c: (0, p)),
                pl.BlockSpec((1, 2, QB), lambda p, i, c: (p, 0, i)),
            ]
            + [pl.BlockSpec(memory_space=pl.ANY)] * len(before),
            out_specs=[
                pl.BlockSpec((L, 384), lambda p, i, c: (0, p)),
                pl.BlockSpec((8, 384), lambda p, i, c: (0, p)),
            ],
            scratch_shapes=[
                pltpu.VMEM((128, L), jnp.bfloat16),
                pltpu.VMEM((L, 128), jnp.float32),
                pltpu.VMEM((L, 128), jnp.float32),
            ],
        ),
        out_shape=[
            jax.ShapeDtypeStruct((L, pairs * 384), jnp.bfloat16),
            jax.ShapeDtypeStruct((8, pairs * 384), jnp.float32),
        ],
        compiler_params=pltpu.CompilerParams(vmem_limit_bytes=20 * 2**20),
        cost_estimate=cost(22.0),
        name="attn_bwd",
    )(core, length, joined, joined, joined, do, do_other, lse, *before)


TN = (((0,), (0,)), ((), ()))


def gelu_pair(z):
    cdf = 0.5 * (1.0 + lax.erf(z * (0.5**0.5)))
    pdf = jnp.exp(-0.5 * z * z) * ((0.5 / jnp.pi) ** 0.5)
    return z * cdf, cdf + z * pdf

def widen_kernel(core_ref, own_ref, other_ref, mix_own_ref, mix_other_ref, x_ref, rows_ref, w_ref, wb_ref,
                 low_ref, turned_ref, normed_ref, inverse_ref, g_ref, gp_ref, z_ref):
    @pl.when(pl.program_id(0) == 0)
    def _():
        width = x_ref.shape[1]
        branch = dotf(own_ref[...], mix_own_ref[...].reshape(width // 2, width), NN)
        branch += dotf(other_ref[...], mix_other_ref[...].reshape(width // 2, width), NN)
        hidden = x_ref[...].astype(jnp.float32) + (branch + rows_ref[2:3, :])
        centred = hidden - jnp.mean(hidden, axis=1, keepdims=True)
        inverse = lax.rsqrt(jnp.mean(centred * centred, axis=1, keepdims=True) + EPSILON)
        normed = centred * inverse
        normed_ref[...] = normed
        inverse_ref[...] = inverse
        low_ref[...] = (normed * rows_ref[4:5, :] + rows_ref[5:6, :]).astype(jnp.bfloat16)
        turned_ref[...] = low_ref[...].T

    widen_block(low_ref, w_ref, wb_ref, g_ref, gp_ref, z_ref)


def widen_block(low_ref, w_ref, wb_ref, g_ref, gp_ref, z_ref):
    rows = 64
    z_ref[...] = dotf(low_ref[...], w_ref[...].reshape(low_ref.shape[1], -1), NN)

    def step(i, carry):
        at = pl.ds(i * rows, rows)
        value, slope = gelu_pair(z_ref[at, :] + wb_ref[...])
        g_ref[at, :] = value.astype(jnp.bfloat16)
        gp_ref[at, :] = slope
        return carry

    lax.fori_loop(0, z_ref.shape[0] // rows, step, 0)


def widen(core, mixed_own, mixed_other, rest, narrow_rows, inputs, rows_float, widen_bias):
    rows, width = inputs.shape
    chips = rest.shape[0]
    shard = width // chips
    blocks = widen_bias.shape[1] // width
    half = width // 2
    start = narrow_rows // shard
    fixed = lambda shape: pl.BlockSpec(shape, lambda j, c: (0,) * len(shape))
    return pl.pallas_call(
        widen_kernel,
        grid_spec=pltpu.PrefetchScalarGridSpec(
            num_scalar_prefetch=1,
            grid=(blocks,),
            in_specs=[
                pl.BlockSpec((rows, half), lambda j, c: (c[0], 0)),
                pl.BlockSpec((rows, half), lambda j, c: (c[0], 0)),
                pl.BlockSpec((chips // 2, shard, width), lambda j, c: (c[0], start, 0)),
                pl.BlockSpec((chips // 2, shard, width), lambda j, c: (1 - c[0], start, 0)),
                fixed((rows, width)),
                fixed(rows_float.shape),
                pl.BlockSpec((chips, shard, width), lambda j, c: (0, start + 1 + j, 0)),
                pl.BlockSpec((1, width), lambda j, c: (0, j)),
            ],
            out_specs=[
                fixed((rows, width)),
                fixed((width, rows)),
                fixed((rows, width)),
                fixed((rows, 1)),
                pl.BlockSpec((rows, width), lambda j, c: (0, j)),
                pl.BlockSpec((rows, width), lambda j, c: (0, j)),
            ],
            scratch_shapes=[pltpu.VMEM((rows, width), jnp.float32)],
        ),
        out_shape=[
            jax.ShapeDtypeStruct((rows, width), jnp.bfloat16),
            jax.ShapeDtypeStruct((width, rows), jnp.bfloat16),
            jax.ShapeDtypeStruct((rows, width), jnp.float32),
            jax.ShapeDtypeStruct((rows, 1), jnp.float32),
            jax.ShapeDtypeStruct((rows, blocks * width), jnp.bfloat16),
            jax.ShapeDtypeStruct((rows, blocks * width), jnp.float32),
        ],
        compiler_params=pltpu.CompilerParams(vmem_limit_bytes=20 * 2**20),
        cost_estimate=cost(12.5),
        name="widen",
    )(core, mixed_own, mixed_other, rest, rest, inputs, rows_float, rest, widen_bias)


def back_kernel(core_ref, dm_ref, grad_two_ref, normed_ref, inverse_ref, rows_ref, narrow_ref, w_ref, gp_ref,
                mix_ref, *refs, spare):
    (dz_own_ref, dz_other_ref, columns_ref, one_ref, da_ref, da_other_ref, do_ref, do_other_ref, sums_ref,
     acc_ref) = refs[spare:]
    j = pl.program_id(0)
    rows, width = dm_ref.shape
    half = width // 2
    at_other = pl.ds(pl.multiple_of((1 - core_ref[0]) * half, half), half)
    dz = dotf(dm_ref[...], narrow_ref[...].reshape(width, width), NT) * gp_ref[...]
    dz = dz.astype(jnp.bfloat16)
    own_turn = j >= pl.num_programs(0) // 2

    @pl.when(own_turn)
    def _():
        dz_own_ref[...] = dz

    @pl.when(jnp.logical_not(own_turn))
    def _():
        dz_other_ref[...] = dz

    sums = jnp.broadcast_to(jnp.sum(dz.astype(jnp.float32), axis=0, keepdims=True), (128, width)).T
    shard = mix_ref.shape[1]
    chips = columns_ref.shape[0] // shard
    each = width // chips // shard
    lanes = lax.broadcasted_iota(jnp.int32, (shard, 128), 1)
    for chip in range(chips):
        total = jnp.zeros((shard, 128), jnp.float32)
        for k in range(each):
            at = (chip * each + k) * shard
            total = jnp.where(lanes == 8 + k, sums[at : at + shard, :], total)
        columns_ref[chip * shard : (chip + 1) * shard, :] = total
    part = dotf(dz, w_ref[...].reshape(width, -1), NT)

    @pl.when(j == 0)
    def _():
        acc_ref[...] = grad_two_ref[...] + part

    @pl.when(j > 0)
    def _():
        acc_ref[...] += part

    @pl.when(j == pl.num_programs(0) - 1)
    def _():
        first_grad = acc_ref[...]
        normed = normed_ref[...]
        inner = first_grad * rows_ref[4:5, :]
        one = inverse_ref[...] * (
            inner
            - jnp.mean(inner, axis=1, keepdims=True)
            - normed * jnp.mean(inner * normed, axis=1, keepdims=True)
        )
        one_ref[...] = one
        low = one.astype(jnp.bfloat16)
        da_ref[...] = low
        da_other_ref[...] = da_ref[:, at_other]
        do_ref[...] = dotf(low, mix_ref[...].reshape(width, width), NT).astype(jnp.bfloat16)
        do_other_ref[...] = do_ref[:, at_other]
        sums_ref[0:1, :] = jnp.sum(first_grad * normed, axis=0, keepdims=True)
        sums_ref[1:2, :] = jnp.sum(first_grad, axis=0, keepdims=True)
        sums_ref[2:3, :] = jnp.sum(low.astype(jnp.float32), axis=0, keepdims=True)


def back(core, dm, grad_two, normed, inverse, rows_float, rest, narrow_rows, gp, chips, before):
    rows, width = dm.shape
    shard = width // chips
    half = width // 2
    blocks = gp.shape[1] // width
    start = narrow_rows // shard
    at = lambda j, c: (j + (1 - c[0]) * (blocks // 2)) % blocks
    fixed = lambda shape: pl.BlockSpec(shape, lambda j, c: (0,) * len(shape))
    low = lambda shape: jax.ShapeDtypeStruct(shape, jnp.bfloat16)
    return pl.pallas_call(
        functools.partial(back_kernel, spare=len(before)),
        grid_spec=pltpu.PrefetchScalarGridSpec(
            num_scalar_prefetch=1,
            grid=(blocks,),
            in_specs=[
                fixed((rows, width)),
                fixed((rows, width)),
                fixed((rows, width)),
                fixed((rows, 1)),
                fixed(rows_float.shape),
                pl.BlockSpec((width // narrow_rows, narrow_rows, width), lambda j, c: (at(j, c), 0, 0)),
                pl.BlockSpec((chips, shard, width), lambda j, c: (0, start + 1 + at(j, c), 0)),
                pl.BlockSpec((rows, width), lambda j, c: (0, at(j, c))),
                pl.BlockSpec((chips, shard, width), lambda j, c: (0, start, 0)),
            ]
            + [pl.BlockSpec(memory_space=pl.ANY)] * len(before),
            out_specs=[
                pl.BlockSpec((rows, width), lambda j, c: (0, jnp.maximum(j - blocks // 2, 0))),
                pl.BlockSpec((rows, width), lambda j, c: (0, jnp.minimum(j, blocks // 2 - 1))),
                pl.BlockSpec((width // blocks, 128), lambda j, c: (at(j, c), 0)),
                fixed((rows, width)),
                fixed((rows, width)),
                fixed((rows, half)),
                fixed((rows, width)),
                fixed((rows, half)),
                fixed((8, width)),
            ],
            scratch_shapes=[pltpu.VMEM((rows, width), jnp.float32)],
        ),
        out_shape=[
            low((rows, blocks // 2 * width)),
            low((rows, blocks // 2 * width)),
            jax.ShapeDtypeStruct((width, 128), jnp.float32),
            jax.ShapeDtypeStruct((rows, width), jnp.float32),
            low((rows, width)),
            low((rows, half)),
            low((rows, width)),
            low((rows, half)),
            jax.ShapeDtypeStruct((8, width), jnp.float32),
        ],
        compiler_params=pltpu.CompilerParams(vmem_limit_bytes=56 * 2**20),
        cost_estimate=cost(13.8),
        name="back",
    )(core, dm, grad_two, normed, inverse, rows_float, rest, rest, gp, rest, *before)


def tokens_kernel(core_ref, grad_ref, w_ref, one_ref, *refs):
    own_ref, other_ref = refs[-2:]
    half = w_ref.shape[1] // 3

    def part():
        total = 0.0
        for pair in range(half // 128):
            for kind in range(3):
                at = kind * half + pair * 128
                start = pair * 384 + kind * 128
                total += dotf(grad_ref[:, start : start + 128], w_ref[:, at : at + 128], NT)
        return total

    @pl.when(pl.program_id(0) == 0)
    def _():
        other_ref[...] = part()

    @pl.when(pl.program_id(0) == 1)
    def _():
        own_ref[...] = part() + one_ref[...]


def tokens_grad(core, grad, w_own, grad_one, before):
    rows, width = grad_one.shape
    fixed = lambda shape: pl.BlockSpec(shape, lambda i, c: (0,) * len(shape))
    return pl.pallas_call(
        tokens_kernel,
        grid_spec=pltpu.PrefetchScalarGridSpec(
            num_scalar_prefetch=1,
            grid=(2,),
            in_specs=[
                pl.BlockSpec((rows, grad.shape[1]), lambda i, c: (jnp.where(i == 0, 1 - c[0], c[0]), 0)),
                fixed(w_own.shape),
                fixed((rows, width)),
            ]
            + [pl.BlockSpec(memory_space=pl.ANY)] * len(before),
            out_specs=[fixed((rows, width)), fixed((rows, width))],
        ),
        out_shape=[jax.ShapeDtypeStruct((rows, width), jnp.float32)] * 2,
        compiler_params=pltpu.CompilerParams(vmem_limit_bytes=20 * 2**20),
        cost_estimate=cost(100.0),
        name="tokens_grad",
    )(core, grad, w_own, grad_one, *before)


def widen_grad_kernel(own_ref, other_ref, grad_own_ref, grad_other_ref, left_ref, right_ref):
    term = dotf(own_ref[...], grad_own_ref[...], NN) + dotf(other_ref[...], grad_other_ref[...], NN)

    @pl.when(pl.program_id(0) == 0)
    def _():
        left_ref[...] = term.astype(jnp.bfloat16)

    @pl.when(pl.program_id(0) == 1)
    def _():
        right_ref[...] = term.astype(jnp.bfloat16)


def widen_grad(turned, turned_other, grad, grad_other):
    width, rows = turned.shape
    columns = grad.shape[1] // 2
    fixed = lambda shape: pl.BlockSpec(shape, lambda i: (0, 0))
    return pl.pallas_call(
        widen_grad_kernel,
        grid=(2,),
        in_specs=[fixed((width, rows))] * 2 + [pl.BlockSpec((rows, columns), lambda i: (0, i))] * 2,
        out_specs=[fixed((width, columns))] * 2,
        out_shape=[jax.ShapeDtypeStruct((width, columns), jnp.bfloat16)] * 2,
        compiler_params=pltpu.CompilerParams(vmem_limit_bytes=16 * 2**20),
        cost_estimate=cost(4.0),
        name="widen_grad",
    )(turned, turned_other, grad, grad_other)


def last_grad_kernel(core_ref, turned_ref, grad_ref, mixing_ref, grad_sums_ref, first_ref, second_ref, widen_ref,
                     left_ref, right_ref):
    half = mixing_ref.shape[1]
    pairs = grad_ref.shape[1] // 384
    left_ref[:, :half] = mixing_ref[...]
    for pair in range(pairs):
        term = dotf(turned_ref[...], grad_ref[:, pair * 384 : pair * 384 + 384], NN).astype(jnp.bfloat16)
        if pair == 0:
            left_ref[:, half:] = term
        else:
            right_ref[:, pair * 384 - 384 : pair * 384] = term

    def columns(rows):
        place = lax.broadcasted_iota(jnp.int32, (128, rows[0][1].shape[1]), 0)
        total = 0.0
        for at, row in rows:
            total = jnp.where(place == at, row, total)
        return total.T

    small = pl.ds(pairs * 384 - 384, 128)
    given = [(2, first_ref[2:3, :]), (3, second_ref[0:1, :]), (4, first_ref[0:1, :])]
    given += [(5, first_ref[1:2, :]), (6, second_ref[1:2, :]), (7, second_ref[2:3, :])]
    right_ref[:, small] = (columns(given) + widen_ref[...]).astype(jnp.bfloat16)
    sums = grad_sums_ref[0:1, :]
    queries = jnp.concatenate([sums[:, pair * 384 : pair * 384 + 128] for pair in range(pairs)], axis=1)
    values = jnp.concatenate([sums[:, pair * 384 + 256 : pair * 384 + 384] for pair in range(pairs)], axis=1)
    at = pl.ds(pl.multiple_of(core_ref[0] * half, half), half)
    right_ref[at, small] = right_ref[at, small] + columns([(0, queries), (1, values)]).astype(jnp.bfloat16)


def last_grad(core, turned, grad, mixing_term, grad_sums, first_sums, second_sums, widen_columns):
    width = turned.shape[0]
    columns = grad.shape[1]
    whole = pl.BlockSpec(memory_space=pltpu.VMEM)
    return pl.pallas_call(
        last_grad_kernel,
        in_specs=[pl.BlockSpec(memory_space=pltpu.SMEM)] + [whole] * 7,
        out_specs=[whole] * 2,
        out_shape=[
            jax.ShapeDtypeStruct((width, width // 2 + 384), jnp.bfloat16),
            jax.ShapeDtypeStruct((width, columns - 384 + 128), jnp.bfloat16),
        ],
        compiler_params=pltpu.CompilerParams(vmem_limit_bytes=16 * 2**20),
        cost_estimate=cost(4.0),
        name="last_grad",
    )(core, turned, grad, mixing_term, grad_sums, first_sums, second_sums, widen_columns)


def finish_kernel(core_ref, own_ref, other_ref, *refs, half):
    project_ref, mixing_ref, small_ref = refs[-3:]
    for ref, core in ((own_ref, core_ref[0]), (other_ref, 1 - core_ref[0])):
        mixing_ref[:, pl.ds(pl.multiple_of(core * half, half), half)] = ref[:, :half]
        for pair in range(half // 128):
            for kind in range(3):
                start = half + pair * 384 + kind * 128
                to = pl.multiple_of(core * half + (kind * 2 * half + pair * 128), 128)
                project_ref[:, pl.ds(to, 128)] = ref[:, start : start + 128]
    small = own_ref[:, 4 * half :] + other_ref[:, 4 * half :]
    small_ref[...] = small.T


def finish(core, share, other, half, before):
    rows = share.shape[0]
    whole = pl.BlockSpec(memory_space=pltpu.VMEM)
    return pl.pallas_call(
        functools.partial(finish_kernel, half=half),
        in_specs=[pl.BlockSpec(memory_space=pltpu.SMEM)] + [whole] * 2 + [pl.BlockSpec(memory_space=pl.ANY)] * len(before),
        out_specs=[whole] * 3,
        out_shape=[
            jax.ShapeDtypeStruct((rows, 6 * half), jnp.float32),
            jax.ShapeDtypeStruct((rows, 2 * half), jnp.float32),
            jax.ShapeDtypeStruct((128, rows), jnp.float32),
        ],
        compiler_params=pltpu.CompilerParams(vmem_limit_bytes=8 * 2**20),
        cost_estimate=cost(2.0),
        name="finish",
    )(core, share, other, *before)


def narrow_kernel(core_ref, g_ref, w_ref, normed_ref, rows_ref, cot_ref,
                  result_ref, two_ref, dm_ref, dm_own_ref, dm_other_ref, sums_ref, acc_ref):
    j = pl.program_id(0)
    width = w_ref.shape[2]
    half = width // 2
    at_own = pl.ds(pl.multiple_of(core_ref[0] * half, half), half)
    at_other = pl.ds(pl.multiple_of((1 - core_ref[0]) * half, half), half)

    @pl.when(j == 0)
    def _():
        acc_ref[...] = jnp.zeros_like(acc_ref)

    acc_ref[...] += dotf(g_ref[...], w_ref[...].reshape(width, width), NN)

    @pl.when(j == pl.num_programs(0) - 1)
    def _():
        hidden = normed_ref[...] * rows_ref[4:5, :] + rows_ref[5:6, :] + (acc_ref[...] + rows_ref[3:4, :])
        centred = hidden - jnp.mean(hidden, axis=1, keepdims=True)
        inverse = lax.rsqrt(jnp.mean(centred * centred, axis=1, keepdims=True) + EPSILON)
        normed = centred * inverse
        result_ref[...] = (normed * rows_ref[6:7, :] + rows_ref[7:8, :]).astype(jnp.bfloat16)
        cot = cot_ref[...].astype(jnp.float32)
        inner = cot * rows_ref[6:7, :]
        two = inverse * (
            inner
            - jnp.mean(inner, axis=1, keepdims=True)
            - normed * jnp.mean(inner * normed, axis=1, keepdims=True)
        )
        two_ref[...] = two
        dm = two.astype(jnp.bfloat16)
        dm_ref[...] = dm
        dm_own_ref[...] = dm_ref[:, at_own]
        dm_other_ref[...] = dm_ref[:, at_other]
        sums_ref[0:1, :] = jnp.sum(dm.astype(jnp.float32), axis=0, keepdims=True)
        sums_ref[1:2, :] = jnp.sum(cot * normed, axis=0, keepdims=True)
        sums_ref[2:3, :] = jnp.sum(cot, axis=0, keepdims=True)


def narrow(core, g, rest, narrow_rows, normed, rows_float, cotangent):
    rows, width = normed.shape
    half = width // 2
    fixed = lambda shape: pl.BlockSpec(shape, lambda j, c: (0,) * len(shape))
    return pl.pallas_call(
        narrow_kernel,
        grid_spec=pltpu.PrefetchScalarGridSpec(
            num_scalar_prefetch=1,
            grid=(g.shape[1] // width,),
            in_specs=[
                pl.BlockSpec((rows, width), lambda j, c: (0, j)),
                pl.BlockSpec((width // narrow_rows, narrow_rows, width), lambda j, c: (j, 0, 0)),
                fixed((rows, width)),
                fixed(rows_float.shape),
                fixed((rows, width)),
            ],
            out_specs=[
                fixed((rows, width)),
                fixed((rows, width)),
                fixed((rows, width)),
                fixed((rows, half)),
                fixed((rows, half)),
                fixed((8, width)),
            ],
            scratch_shapes=[pltpu.VMEM((rows, width), jnp.float32)],
        ),
        out_shape=[
            jax.ShapeDtypeStruct((rows, width), jnp.bfloat16),
            jax.ShapeDtypeStruct((rows, width), jnp.float32),
            jax.ShapeDtypeStruct((rows, width), jnp.bfloat16),
            jax.ShapeDtypeStruct((rows, half), jnp.bfloat16),
            jax.ShapeDtypeStruct((rows, half), jnp.bfloat16),
            jax.ShapeDtypeStruct((8, width), jnp.float32),
        ],
        compiler_params=pltpu.CompilerParams(vmem_limit_bytes=20 * 2**20),
        cost_estimate=cost(8.0),
        name="narrow",
    )(core, g, rest, normed, rows_float, cotangent)


def narrow_grad_kernel(own_ref, other_ref, dm_own_ref, dm_other_ref, out_ref):
    term = dotf(own_ref[...], dm_own_ref[...], TN) + dotf(other_ref[...], dm_other_ref[...], TN)
    out_ref[...] = term.reshape(out_ref.shape).astype(jnp.bfloat16)


def narrow_grad(g, g_other, dm_own, dm_other, chips):
    rows, hidden = g.shape
    half = dm_own.shape[1]
    lines = chips // 4
    size = hidden // lines
    fixed = lambda shape: pl.BlockSpec(shape, lambda j: (0, 0))
    return pl.pallas_call(
        narrow_grad_kernel,
        grid=(lines,),
        in_specs=[pl.BlockSpec((rows, size), lambda j: (0, j))] * 2 + [fixed((rows, half))] * 2,
        out_specs=pl.BlockSpec((4, 1, size // 4, half), lambda j: (0, j, 0, 0)),
        out_shape=jax.ShapeDtypeStruct((4, lines, size // 4, half), jnp.bfloat16),
        compiler_params=pltpu.CompilerParams(vmem_limit_bytes=12 * 2**20),
        cost_estimate=cost(4.5),
        name="narrow_grad",
    )(g, g_other, dm_own, dm_other)


def mixing_grad_kernel(core_ref, own_ref, other_ref, grad_ref, grad_other_ref, *refs):
    out_ref = refs[-1]
    rows, half = grad_other_ref.shape
    core = core_ref[0]
    here = pl.ds(pl.multiple_of(core * rows, rows), rows)
    there = pl.ds(pl.multiple_of((1 - core) * rows, rows), rows)
    at_own = pl.ds(pl.multiple_of(core * half, half), half)
    at_other = pl.ds(pl.multiple_of((1 - core) * half, half), half)
    grad = grad_ref[:, at_own]
    grad_other = grad_other_ref[...]
    for ref, at in ((own_ref, at_own), (other_ref, at_other)):
        term = dotf(ref[here, :], grad, TN) + dotf(ref[there, :], grad_other, TN)
        out_ref[at, :] = term.astype(jnp.bfloat16)


def mixing_grad(core, mixed_own, mixed_other, grad, grad_other):
    width = grad.shape[1]
    whole = pl.BlockSpec(memory_space=pltpu.VMEM)
    return pl.pallas_call(
        mixing_grad_kernel,
        in_specs=[pl.BlockSpec(memory_space=pltpu.SMEM)] + [whole] * 4,
        out_specs=whole,
        out_shape=jax.ShapeDtypeStruct((width, width // 2), jnp.bfloat16),
        compiler_params=pltpu.CompilerParams(vmem_limit_bytes=12 * 2**20),
        cost_estimate=cost(2.0),
        name="mixing_grad",
    )(core, mixed_own, mixed_other, grad, grad_other)


def qkv_kernel(place_ref, x_ref, left_ref, left_other_ref, right_ref, right_other_ref, joined_ref, w_ref, rows_ref,
               small_ref, *, small_at, far):
    core = place_ref[0]
    y = place_ref[far + 1]
    x = place_ref[far + 2]
    shard, cut = left_ref.shape[-2:]
    lines = left_ref.shape[0]
    for line in range(lines):
        for ref, bit in ((left_ref, y), (left_other_ref, 1 - y)):
            to = pl.multiple_of((line * 4 + bit * 2) * shard, 2 * shard)
            w_ref[pl.ds(to, 2 * shard), :cut] = ref[line].reshape(2 * shard, cut)
        for ref, bit in ((right_ref, x), (right_other_ref, 1 - x)):
            for row in range(2):
                to = pl.multiple_of((line * 4 + row * 2 + bit) * shard, shard)
                w_ref[pl.ds(to, shard), cut:] = ref[line, row, :, :small_at]
                small_ref[pl.ds(to, shard), :] = ref[line, row, :, small_at:].astype(jnp.float32)
    rows_ref[...] = small_ref[...].T[: rows_ref.shape[0]]
    half = w_ref.shape[1] // 3
    at = pl.ds(pl.multiple_of(core * half, half), half)
    product = dotf(x_ref[...], w_ref[...], NN)
    joined_ref[:, :half] = (product[:, :half] + rows_ref[0:1, at]).astype(jnp.bfloat16)
    joined_ref[:, half : 2 * half] = product[:, half : 2 * half].astype(jnp.bfloat16)
    joined_ref[:, 2 * half :] = (product[:, 2 * half :] + rows_ref[1:2, at]).astype(jnp.bfloat16)


def qkv(place, inputs, left, left_other, right, right_other, small_at):
    shard, cut = left.shape[-2:]
    length, width = inputs.shape
    far = left.ndim - 4
    lines = 2**far
    left, left_other = left.reshape(lines, 2, shard, cut), left_other.reshape(lines, 2, shard, cut)
    right, right_other = right.reshape(lines, 2, shard, cut), right_other.reshape(lines, 2, shard, cut)
    whole = pl.BlockSpec(memory_space=pltpu.VMEM)
    return pl.pallas_call(
        functools.partial(qkv_kernel, small_at=small_at, far=far),
        in_specs=[pl.BlockSpec(memory_space=pltpu.SMEM)] + [whole] * 5,
        out_specs=[whole] * 3,
        out_shape=[
            jax.ShapeDtypeStruct((length, cut + small_at), jnp.bfloat16),
            jax.ShapeDtypeStruct((width, cut + small_at), jnp.bfloat16),
            jax.ShapeDtypeStruct((16, width), jnp.float32),
        ],
        scratch_shapes=[pltpu.VMEM((width, 128), jnp.float32)],
        compiler_params=pltpu.CompilerParams(vmem_limit_bytes=16 * 2**20),
        cost_estimate=cost(4.0),
        name="qkv",
    )(place, inputs, left, left_other, right, right_other)


def pack_kernel(core_ref, narrow_ref, mixing_ref, widen_ref, project_ref, biases_ref, norms_ref, hidden_ref,
                rest_ref, packed_ref):
    core = core_ref[0]
    shard, width = mixing_ref.shape
    half = width // 2
    split = rest_ref.shape[0] - narrow_ref.shape[0]
    blocks = widen_ref.shape[1] // width

    @pl.when(core == 0)
    def _():
        rest_ref[: narrow_ref.shape[0]] = narrow_ref[...]
        rest_ref[narrow_ref.shape[0] :] = mixing_ref[:split]

    @pl.when(core == 1)
    def _():
        rest_ref[: shard - split] = mixing_ref[split:]
        for block in range(blocks):
            at = shard - split + block * shard
            rest_ref[at : at + shard] = widen_ref[:, block * width : (block + 1) * width]
        at = shard - split + blocks * shard
        if at < rest_ref.shape[0]:
            rest_ref[at:] = jnp.zeros((rest_ref.shape[0] - at, width), jnp.bfloat16)

    for kind in range(3):
        from_ = pl.ds(pl.multiple_of(core * half + kind * width, half), half)
        packed_ref[:, kind * half : (kind + 1) * half] = project_ref[:, from_]
    place = lax.broadcasted_iota(jnp.int32, (128, shard), 0)
    total = jnp.zeros((128, shard), jnp.float32)
    at = 0
    for ref in (biases_ref, norms_ref, hidden_ref):
        for row in range(ref.shape[0]):
            total = jnp.where(place == at, ref[row : row + 1, :].astype(jnp.float32), total)
            at += 1
    packed_ref[:, 3 * half :] = total.T.astype(jnp.bfloat16)


def pack(core, narrowing, mixing, widening, projection, biases, norms, hidden):
    shard, width = mixing.shape
    rows = narrowing.shape[0] + shard + widening.shape[1] // width * shard
    half_rows = -(-rows // 32) * 16
    whole = pl.BlockSpec(memory_space=pltpu.VMEM)
    return pl.pallas_call(
        pack_kernel,
        in_specs=[pl.BlockSpec(memory_space=pltpu.SMEM)] + [whole] * 7,
        out_specs=[whole] * 2,
        out_shape=[
            jax.ShapeDtypeStruct((half_rows, width), jnp.bfloat16),
            jax.ShapeDtypeStruct((shard, projection.shape[1] // 2 + 128), jnp.bfloat16),
        ],
        compiler_params=pltpu.CompilerParams(vmem_limit_bytes=60 * 2**20),
        cost_estimate=cost(2.0),
        name="pack",
    )(core, narrowing, mixing, widening, projection, biases, norms, hidden)


AXES = ("fsdp", "ctx")


def core_permute(value, chips):
    pairs = [(2 * f + c, 2 * f + 1 - c) for f in range(chips) for c in range(2)]
    return lax.ppermute(value, AXES, pairs)


def chip_permute(value, chips, mask):
    pairs = [(2 * f + c, 2 * (f ^ mask) + c) for f in range(chips) for c in range(2)]
    return lax.ppermute(value, AXES, pairs)


def chip_bit(mask):
    return (lax.axis_index("fsdp") // mask) % 2


def by_core(mine, other, axis):
    core = lax.axis_index("ctx")
    first = jnp.where(core == 0, mine, other)
    second = jnp.where(core == 0, other, mine)
    return jnp.concatenate([first, second], axis=axis)


def dims_of(chips):
    return [1 << b for b in reversed(range(chips.bit_length() - 1))]


def gather_step(value, chips, mask):
    axis = dims_of(chips).index(mask)
    other = chip_permute(value, chips, mask)
    bit = chip_bit(mask)
    first = jnp.where(bit == 0, value, other)
    second = jnp.where(bit == 0, other, value)
    return jnp.concatenate([first, second], axis=axis)


def bits_of(chips):
    return jnp.stack([chip_bit(mask) for mask in dims_of(chips)])


def first_send(value, chips, mask):
    shape = [chips // (2 * mask), 2, mask] + list(value.shape[1:])
    send = lax.dynamic_index_in_dim(value.reshape(shape), 1 - chip_bit(mask), 1, keepdims=False)
    return send.reshape(chips // 2, *value.shape[1:])


def block_at(step, left, free, fixed):
    index = 0
    for place, mask in enumerate(left):
        if mask in fixed:
            bit = fixed[mask]
        else:
            bit = (step // 2 ** (len(free) - 1 - free.index(mask))) % 2
        index = index + bit * 2 ** (len(left) - 1 - place)
    return index


def hop_kernel(bits_ref, *refs, parts, merged, spare):
    outs = refs[4 * parts + spare :]
    at = 0
    for part in range(parts):
        away, away_in, keep, keep_in = refs[4 * part : 4 * part + 4]
        columns = away.shape[2]
        send_ref, keep_ref = outs[:2] if merged else outs[2 * part : 2 * part + 2]
        where = pl.ds(at, columns)
        send_ref[:, :, where] = (away[...].astype(jnp.float32) + away_in[...].astype(jnp.float32)).astype(jnp.bfloat16)
        keep_ref[:, :, where] = keep[...].astype(jnp.float32) + keep_in[...].astype(jnp.float32)
        if merged:
            at += columns


def hop(parts, bits, chips, before, merged):
    masks = dims_of(chips)
    in_specs, operands, out_columns = [], [], []
    steps = 2 ** (len([mask for mask in parts[0][2] if mask != parts[0][3]]) - 1)
    for value, arrived, left, came, goes in parts:
        rows, columns = value.shape[1:]
        rest = [mask for mask in left if mask != came]
        free = [mask for mask in rest if mask != goes]
        block = (1, rows, columns)
        for flip in (1, 0):
            def at_value(i, b, left=left, free=free, came=came, goes=goes, flip=flip):
                mine = b[masks.index(goes)]
                side = 1 - mine if flip else mine
                return block_at(i, left, free, {came: b[masks.index(came)], goes: side}), 0, 0

            def at_arrived(i, b, rest=rest, free=free, goes=goes, flip=flip):
                mine = b[masks.index(goes)]
                return block_at(i, rest, free, {goes: 1 - mine if flip else mine}), 0, 0

            in_specs += [pl.BlockSpec(block, at_value), pl.BlockSpec(block, at_arrived)]
            operands += [value, arrived]
        out_columns.append(columns)
    if merged:
        out_columns = [sum(out_columns)]
    out_specs, out_shape = [], []
    for columns in out_columns:
        out_specs += [pl.BlockSpec((1, rows, columns), lambda i, b: (i, 0, 0))] * 2
        out_shape += [
            jax.ShapeDtypeStruct((steps, rows, columns), jnp.bfloat16),
            jax.ShapeDtypeStruct((steps, rows, columns), jnp.float32),
        ]
    outs = pl.pallas_call(
        functools.partial(hop_kernel, parts=len(parts), merged=merged, spare=len(before)),
        grid_spec=pltpu.PrefetchScalarGridSpec(
            num_scalar_prefetch=1,
            grid=(steps,),
            in_specs=in_specs + [pl.BlockSpec(memory_space=pl.ANY)] * len(before),
            out_specs=out_specs,
        ),
        out_shape=out_shape,
        compiler_params=pltpu.CompilerParams(vmem_limit_bytes=8 * 2**20),
        cost_estimate=cost(2.0),
        name="hop",
    )(bits, *operands, *before)
    return list(outs[0::2]), list(outs[1::2])


class Chain:
    def __init__(self, values, chips, bits):
        self.chips, self.bits, self.masks = chips, bits, dims_of(chips)
        self.far = self.masks[:-2]
        self.order = ([1, 2], [2, 1])
        self.kept = values
        self.sent = [first_send(part, chips, order[0]) for part, order in zip(self.kept, self.order)]

    def move(self, masks):
        self.arrived = [chip_permute(part, self.chips, mask) for part, mask in zip(self.sent, masks)]

    def first(self):
        self.move([1, 2])

    def second(self, before):
        self.sent, self.kept = hop(
            [
                (kept, arrived, self.masks, order[0], order[1])
                for kept, arrived, order in zip(self.kept, self.arrived, self.order)
            ],
            self.bits, self.chips, before, False,
        )
        self.move([2, 1])

    def third(self, before, others=()):
        parts = [
            (kept, arrived, self.far, order[1], self.far[-1])
            for chain in (self, *others)
            for kept, arrived, order in zip(chain.kept, chain.arrived, chain.order)
        ]
        self.sent, self.kept = hop(parts, self.bits, self.chips, before, True)
        self.move([self.far[-1]])

    def fourth(self, before):
        for at in range(len(self.far) - 1, 0, -1):
            part = (self.kept[0], self.arrived[0], self.far[:at], self.far[at], self.far[at - 1])
            self.sent, self.kept = hop([part], self.bits, self.chips, before, True)
            self.move([self.far[at - 1]])

    def last(self):
        return self.kept[0][0] + self.arrived[0][0].astype(jnp.float32)


def groups_of(chips):
    near = [list(range(at, at + 4)) for at in range(0, chips, 4)]
    far = [list(range(at, chips, 4)) for at in range(4)]
    return near, far


def core_half(value, axis, own):
    core = lax.axis_index("ctx")
    size = value.shape[axis] // 2
    which = core if own else 1 - core
    return lax.dynamic_slice_in_dim(value, which * size, size, axis)


def fast_body(
    tokens, lengths, cotangent, projection, mixing, widening, narrowing, biases, widen_bias, norms
):
    chips = lax.axis_size("fsdp")
    core = lax.axis_index("ctx")
    core_at = core.reshape(1)
    bits = dims_of(chips)
    far = bits[:-2]
    down_x = [1, 2] + far[::-1]
    down_y = [2, 1] + far[::-1]
    inputs = tokens[0]
    row_count, model_width = inputs.shape
    shard = projection.shape[0]
    half = model_width // 2
    swap = lambda value: core_permute(value, chips)

    hidden = widen_bias.shape[0] // shard
    rest, packed = pack(core_at, narrowing, mixing, widening, projection, biases, norms, widen_bias.reshape(hidden, shard))
    rest = lax.all_gather(rest, AXES, axis=0, tiled=True).reshape(chips, -1, model_width)
    packed = packed.reshape([1] * len(bits) + [shard, packed.shape[1]])
    cut = packed.shape[-1] // 2
    for mask in far:
        packed = gather_step(packed, chips, mask)
    left = gather_step(packed[..., :cut], chips, 1)
    right = gather_step(packed[..., cut:], chips, 2)
    left_other = chip_permute(left, chips, 2)
    right_other = chip_permute(right, chips, 1)

    narrow_rows = narrowing.shape[0]

    all_inputs = by_core(inputs, swap(inputs), 0)
    inputs_turned = all_inputs.T
    chip_bits = bits_of(chips)
    small_at = 3 * half - cut
    joined, w_own, rows_float = qkv(
        jnp.concatenate([core_at, chip_bits]), all_inputs, left, left_other, right, right_other, small_at
    )
    widen_float = rows_float[8 : 8 + hidden].reshape(hidden, chips, shard).transpose(1, 0, 2).reshape(1, -1)
    mixed_own, logsum = attn_fwd(lengths, joined, [inputs_turned])
    mixed_other = swap(mixed_own)
    first_low, first_turned, normed_one, inverse_one, active_low, slope = widen(
        core_at, mixed_own, mixed_other, rest, narrow_rows, inputs, rows_float, widen_float
    )
    first_other = swap(first_turned)
    active_other = swap(active_low)
    result, grad_two, second_grad, dm_own, dm_other, second_sums = narrow(
        core_at, active_low, rest, narrow_rows, normed_one, rows_float, cotangent[0]
    )

    near, line = groups_of(chips)
    narrow_term = narrow_grad(active_low, active_other, dm_own, swap(dm_other), chips)
    narrow_near = lax.psum_scatter(
        narrow_term, "fsdp", scatter_dimension=0, axis_index_groups=near, tiled=True
    ).reshape(chips // 4, narrow_rows, half)

    (
        expand_own, expand_other, widen_columns, grad_one, branch_grad, branch_other, mixed_grad, mixed_other_grad,
        first_sums,
    ) = back(
        core_at, second_grad, grad_two, normed_one, inverse_one, rows_float,
        rest, narrow_rows, slope, chips, [narrow_term],
    )
    mixed_grad_other = swap(mixed_other_grad)
    branch_other = swap(branch_other)
    widen_terms_two = widen_grad(first_turned, first_other, expand_own, swap(expand_other))
    widen_chain = Chain([term.reshape(chips, shard, -1) for term in widen_terms_two], chips, chip_bits)
    widen_chain.first()

    mixing_term = mixing_grad(core_at, mixed_own, mixed_other, branch_grad, branch_other)

    grad, grad_sums = attn_bwd(
        core_at, lengths, joined, mixed_grad, mixed_grad_other, logsum, widen_chain.sent + [mixing_term]
    )
    narrow_share = lax.psum_scatter(
        narrow_near, "fsdp", scatter_dimension=0, axis_index_groups=line, tiled=True
    )[0].astype(jnp.float32)
    last_terms = last_grad(
        core_at, inputs_turned, grad, mixing_term, grad_sums, first_sums, second_sums, widen_columns
    )
    last_chain = Chain([term.reshape(chips, shard, -1) for term in last_terms], chips, chip_bits)
    last_chain.first()
    widen_chain.second([grad, narrow_near] + last_chain.sent)
    own_part, other_part = tokens_grad(core_at, grad, w_own, grad_one, last_chain.sent + [narrow_share])
    last_chain.second(widen_chain.sent)
    widen_chain.third(last_chain.sent)
    last_chain.third(widen_chain.sent)
    input_grad = own_part + swap(other_part)
    widen_chain.fourth(last_chain.sent)
    last_chain.fourth(widen_chain.sent)
    join = lambda share: by_core(share, swap(share), 1)
    widen_share = join(widen_chain.last())
    narrow_share = join(narrow_share)
    last_share = last_chain.last()
    other_share = swap(last_share)

    grad_projection, grad_mixing, small_share = finish(
        core_at, last_share, other_share, half, [widen_share, narrow_share]
    )
    return (
        result.astype(jnp.bfloat16)[None],
        input_grad[None],
        grad_projection,
        grad_mixing,
        widen_share,
        narrow_share,
        small_share[:4],
        small_share[8 : 8 + hidden].reshape(-1),
        small_share[4:8],
    )


def solution(mesh):
    in_specs = (
        P("fsdp", "ctx", None),
        P("fsdp"),
        P("fsdp", "ctx", None),
        P("fsdp", None),
        P("fsdp", None),
        P("fsdp", None),
        P("fsdp", None),
        P(None, "fsdp"),
        P("fsdp"),
        P(None, "fsdp"),
    )
    out_specs = (
        P("fsdp", "ctx", None),
        P("fsdp", "ctx", None),
        P("fsdp", None),
        P("fsdp", None),
        P("fsdp", None),
        P("fsdp", None),
        P(None, "fsdp"),
        P("fsdp"),
        P(None, "fsdp"),
    )
    chips = mesh.shape["fsdp"]
    paired = mesh.shape["ctx"] == 2 and chips >= 4 and chips & (chips - 1) == 0
    body = fast_body if paired else general_body
    return jax.shard_map(body, mesh=mesh, in_specs=in_specs, out_specs=out_specs, check_vma=False)
```

```python
import functools

import jax
import jax.numpy as jnp
from jax import lax
from jax.experimental import pallas as pl
from jax.experimental.pallas import tpu as pltpu
from jax.sharding import PartitionSpec as P

HEADS = 12
HEAD_DIM = 64


EPSILON = 1e-12


def split_heads(matrix):
    return matrix.reshape(matrix.shape[0], HEADS, matrix.shape[1] // HEADS)


def pair_scores(left_rows, right_rows, factor):
    return (
        jnp.einsum(
            "ahd,bhd->hab",
            split_heads(left_rows),
            split_heads(right_rows),
            preferred_element_type=jnp.float32,
        )
        * factor
    )


def spread_rows(weights_hab, right_rows):
    out_rows = jnp.einsum(
        "hab,bhd->ahd", weights_hab, split_heads(right_rows), preferred_element_type=jnp.float32
    )
    return out_rows.reshape(out_rows.shape[0], -1)


def collect_rows(weights_hab, left_rows):
    out_rows = jnp.einsum(
        "hab,ahd->bhd", weights_hab, split_heads(left_rows), preferred_element_type=jnp.float32
    )
    return out_rows.reshape(out_rows.shape[0], -1)


def norm_forward(hidden, gain, shift):
    row_mean = jnp.mean(hidden, axis=-1, keepdims=True)
    centred = hidden - row_mean
    inverse = lax.rsqrt(jnp.mean(centred * centred, axis=-1, keepdims=True) + EPSILON)
    normed = centred * inverse
    return (normed * gain + shift, normed, inverse)


def norm_backward(upstream, normed, inverse, gain):
    inner = upstream * gain
    return inverse * (
        inner
        - jnp.mean(inner, axis=-1, keepdims=True)
        - normed * jnp.mean(inner * normed, axis=-1, keepdims=True)
    )


def gelu_exact(values_in):
    return jax.nn.gelu(values_in, approximate=False)


def general_body(
    tokens, lengths, cotangent, projection, mixing, widening, narrowing, biases, widen_bias, norms
):
    score_scale = HEAD_DIM ** (-0.5)
    gathered = (
        lax.all_gather(projection, "fsdp", axis=0, tiled=True),
        lax.all_gather(mixing, "fsdp", axis=0, tiled=True),
        lax.all_gather(widening, "fsdp", axis=0, tiled=True),
        lax.all_gather(narrowing, "fsdp", axis=0, tiled=True),
        lax.all_gather(biases, "fsdp", axis=1, tiled=True),
        lax.all_gather(widen_bias, "fsdp", axis=0, tiled=True),
        lax.all_gather(norms, "fsdp", axis=1, tiled=True),
    )
    w_project, w_mixing, w_widen, w_narrow, bias_rows, widen_all, norm_rows = gathered
    bias_float = bias_rows.astype(jnp.float32)
    widen_float = widen_all.astype(jnp.float32)
    norm_float = norm_rows.astype(jnp.float32)
    inputs = tokens[0]
    row_count, model_width = inputs.shape
    seq_length = lengths[0]
    joined_rows = jnp.dot(inputs, w_project, preferred_element_type=jnp.float32)
    queries = (joined_rows[:, :model_width] + bias_float[0]).astype(jnp.bfloat16)
    key_rows = joined_rows[:, model_width : 2 * model_width].astype(jnp.bfloat16)
    value_rows = (joined_rows[:, 2 * model_width :] + bias_float[1]).astype(jnp.bfloat16)
    all_keys, all_values = (
        lax.all_gather(key_rows, "ctx", axis=0, tiled=True),
        lax.all_gather(value_rows, "ctx", axis=0, tiled=True),
    )
    key_valid = jnp.arange(all_keys.shape[0], dtype=jnp.int32) < seq_length
    scores = jnp.where(key_valid[None, None, :], pair_scores(queries, all_keys, score_scale), -1e30)
    row_peak = jnp.max(scores, axis=-1, keepdims=True)
    exp_terms = jnp.exp(scores - row_peak)
    summed = jnp.sum(exp_terms, axis=-1, keepdims=True)
    prob_low = (exp_terms / summed).astype(jnp.bfloat16)
    logsum = row_peak + jnp.log(summed)
    mixed_low = spread_rows(prob_low, all_values).astype(jnp.bfloat16)
    branch = jnp.dot(mixed_low, w_mixing, preferred_element_type=jnp.float32) + bias_float[2]
    first_norm, normed_one, inverse_one = norm_forward(
        inputs.astype(jnp.float32) + branch, norm_float[0], norm_float[1]
    )
    first_low = first_norm.astype(jnp.bfloat16)
    expanded = jnp.dot(first_low, w_widen, preferred_element_type=jnp.float32) + widen_float
    activated, gelu_pull = jax.vjp(gelu_exact, expanded)
    active_low = activated.astype(jnp.bfloat16)
    second = jnp.dot(active_low, w_narrow, preferred_element_type=jnp.float32) + bias_float[3]
    result, normed_two, inverse_two = norm_forward(
        first_norm + second, norm_float[2], norm_float[3]
    )
    grad_out = cotangent[0].astype(jnp.float32)
    grad_two = norm_backward(grad_out, normed_two, inverse_two, norm_float[2])
    second_grad = grad_two.astype(jnp.bfloat16)
    narrow_term = jnp.einsum(
        "rf,rd->fd", active_low, second_grad, preferred_element_type=jnp.float32
    )
    active_grad = jnp.einsum("rd,fd->rf", second_grad, w_narrow, preferred_element_type=jnp.float32)
    expand_grad = gelu_pull(active_grad)[0].astype(jnp.bfloat16)
    widen_term = jnp.einsum("rd,rf->df", first_low, expand_grad, preferred_element_type=jnp.float32)
    first_grad = grad_two + jnp.einsum(
        "rf,df->rd", expand_grad, w_widen, preferred_element_type=jnp.float32
    )
    grad_one = norm_backward(first_grad, normed_one, inverse_one, norm_float[0])
    branch_grad = grad_one.astype(jnp.bfloat16)
    mixing_term = jnp.einsum(
        "rd,re->de", mixed_low, branch_grad, preferred_element_type=jnp.float32
    )
    mixed_grad = jnp.einsum(
        "re,de->rd", branch_grad, w_mixing, preferred_element_type=jnp.float32
    ).astype(jnp.bfloat16)
    scores = jnp.where(key_valid[None, None, :], pair_scores(queries, all_keys, score_scale), -1e30)
    prob_again = jnp.exp(scores - logsum)
    prob_grad = pair_scores(mixed_grad, all_values, 1.0)
    row_delta = jnp.sum(prob_again * prob_grad, axis=-1, keepdims=True)
    score_grad = (prob_again * (prob_grad - row_delta)).astype(jnp.bfloat16)
    query_grad = (spread_rows(score_grad, all_keys) * score_scale).astype(jnp.bfloat16)
    key_terms = collect_rows(score_grad, queries) * score_scale
    value_terms = collect_rows(prob_low, mixed_grad)
    key_grad, value_grad = (
        lax.psum_scatter(key_terms, "ctx", scatter_dimension=0, tiled=True),
        lax.psum_scatter(value_terms, "ctx", scatter_dimension=0, tiled=True),
    )
    key_low = key_grad.astype(jnp.bfloat16)
    value_low = value_grad.astype(jnp.bfloat16)
    joined_grad = jnp.concatenate([query_grad, key_low, value_low], axis=1)
    project_term = jnp.einsum("rd,re->de", inputs, joined_grad, preferred_element_type=jnp.float32)
    input_grad = (
        jnp.einsum("re,de->rd", joined_grad, w_project, preferred_element_type=jnp.float32)
        + grad_one
    )
    bias_terms = jnp.stack(
        [
            jnp.sum(query_grad.astype(jnp.float32), axis=0),
            jnp.sum(value_low.astype(jnp.float32), axis=0),
            jnp.sum(branch_grad.astype(jnp.float32), axis=0),
            jnp.sum(second_grad.astype(jnp.float32), axis=0),
        ]
    )
    widen_terms = jnp.sum(expand_grad.astype(jnp.float32), axis=0)
    norm_terms = jnp.stack(
        [
            jnp.sum(first_grad * normed_one, axis=0),
            jnp.sum(first_grad, axis=0),
            jnp.sum(grad_out * normed_two, axis=0),
            jnp.sum(grad_out, axis=0),
        ]
    )
    shares = (
        lax.psum_scatter(project_term, "fsdp", scatter_dimension=0, tiled=True),
        lax.psum_scatter(mixing_term, "fsdp", scatter_dimension=0, tiled=True),
        lax.psum_scatter(widen_term, "fsdp", scatter_dimension=0, tiled=True),
        lax.psum_scatter(narrow_term, "fsdp", scatter_dimension=0, tiled=True),
        lax.psum_scatter(bias_terms, "fsdp", scatter_dimension=1, tiled=True),
        lax.psum_scatter(widen_terms, "fsdp", scatter_dimension=0, tiled=True),
        lax.psum_scatter(norm_terms, "fsdp", scatter_dimension=1, tiled=True),
    )
    totals = lax.psum(
        (shares[0], shares[1], shares[2], shares[3], shares[4], shares[5], shares[6]), "ctx"
    )
    return (
        result.astype(jnp.bfloat16)[None],
        input_grad[None],
        totals[0],
        totals[1],
        totals[2],
        totals[3],
        totals[4],
        totals[5],
        totals[6],
    )


NT=(((1,),(1,)),((),()))
NN=(((1,),(0,)),((),()))
def dotf(a,b,dims): return lax.dot_general(a,b,dims,preferred_element_type=jnp.float32)

def cost(microseconds):
    return pl.CostEstimate(flops=int(microseconds * 5e7), bytes_accessed=2**12, transcendentals=0)


def attn_fwd_kernel(len_ref,q_ref,k_ref,v_ref,*refs):
    o_ref,lse_ref,vt_ref=refs[-3:]
    @pl.when(pl.program_id(1)==0)
    def _():
        vt_ref[...]=v_ref[...].T
    n=len_ref[0]
    q=q_ref[...]; k=k_ref[...]
    lanes=lax.broadcasted_iota(jnp.int32,q.shape,1)
    rows=lax.broadcasted_iota(jnp.int32,(k.shape[0],1),0)
    valid=rows<n
    outs = []
    for h in range(2):
        qh=jnp.where((lanes>=64)==(h==1),q*jnp.bfloat16(HEAD_DIM**-0.5),jnp.bfloat16(0))
        s=dotf(k,qh,NT)
        s=jnp.where(valid,s,-1e30)
        m=jnp.max(s,axis=0,keepdims=True)
        e=jnp.exp(s-m)
        l=jnp.sum(e,axis=0,keepdims=True)
        p=(e*(1.0/l)).astype(jnp.bfloat16)
        lse_ref[0,h:h+1,:]=m+jnp.log(l)
        outs.append(dotf(vt_ref[64*h:64*h+64,:],p,NN))
    o=jnp.concatenate(outs,axis=0)
    o_ref[...]=o.T.astype(jnp.bfloat16)

def attn_fwd(length, joined, before, QB=512):
    L = joined.shape[0]
    C = joined.shape[1] // 3
    pairs = C // 128
    QB = min(QB, L)
    return pl.pallas_call(
        attn_fwd_kernel,
        grid=(pairs, L // QB),
        in_specs=[
            pl.BlockSpec(memory_space=pltpu.SMEM),
            pl.BlockSpec((QB, 128), lambda p, i: (i, p)),
            pl.BlockSpec((L, 128), lambda p, i: (0, pairs + p)),
            pl.BlockSpec((L, 128), lambda p, i: (0, 2 * pairs + p)),
        ]
        + [pl.BlockSpec(memory_space=pl.ANY)] * len(before),
        out_specs=[
            pl.BlockSpec((QB, 128), lambda p, i: (i, p)),
            pl.BlockSpec((1, 2, QB), lambda p, i: (p, 0, i)),
        ],
        out_shape=[
            jax.ShapeDtypeStruct((L, C), jnp.bfloat16),
            jax.ShapeDtypeStruct((pairs, 2, L), jnp.float32),
        ],
        scratch_shapes=[pltpu.VMEM((128, L), jnp.bfloat16)],
        compiler_params=pltpu.CompilerParams(vmem_limit_bytes=20 * 2**20),
        cost_estimate=cost(14.5),
        name="attn_fwd",
    )(length, joined, joined, joined, *before)


def attn_bwd_kernel(core_ref, len_ref, q_ref, k_ref, v_ref, do_ref, do_other_ref, lse_ref, *refs):
    df_ref, sum_ref, kt_ref, dka_ref, dva_ref = refs[-5:]
    i = pl.program_id(1)

    @pl.when(i == 0)
    def _():
        kt_ref[...] = k_ref[...].T
        dka_ref[...] = jnp.zeros_like(dka_ref)
        dva_ref[...] = jnp.zeros_like(dva_ref)

    n = len_ref[0]
    scale = jnp.bfloat16(HEAD_DIM**-0.5)
    q = q_ref[...]
    k = k_ref[...]
    v = v_ref[...]
    do = jnp.where(i == core_ref[0], do_ref[...], do_other_ref[...])
    lanes = lax.broadcasted_iota(jnp.int32, q.shape, 1)
    valid = lax.broadcasted_iota(jnp.int32, (k.shape[0], 1), 0) < n
    outs = []
    for h in range(2):
        mine = (lanes >= HEAD_DIM) == (h == 1)
        qh = jnp.where(mine, q * scale, jnp.bfloat16(0))
        doh = jnp.where(mine, do, jnp.bfloat16(0))
        s = dotf(k, qh, NT)
        p = jnp.where(valid, jnp.exp(s - lse_ref[0, h : h + 1, :]), 0.0)
        dp = dotf(v, doh, NT)
        delta = jnp.sum(p * dp, axis=0, keepdims=True)
        ds = (p * (dp - delta)).astype(jnp.bfloat16)
        dva_ref[...] += dotf(p.astype(jnp.bfloat16), doh, NN)
        dka_ref[...] += dotf(ds, qh, NN)
        outs.append(dotf(kt_ref[HEAD_DIM * h : HEAD_DIM * (h + 1), :], ds, NN))
    dq = jnp.concatenate(outs, axis=0) * (HEAD_DIM**-0.5)
    df_ref[pl.ds(pl.multiple_of(i * q.shape[0], q.shape[0]), q.shape[0]), 0:128] = dq.T.astype(jnp.bfloat16)

    @pl.when(i == pl.num_programs(1) - 1)
    def _():
        df_ref[:, 128:256] = dka_ref[...].astype(jnp.bfloat16)
        df_ref[:, 256:384] = dva_ref[...].astype(jnp.bfloat16)
        sum_ref[0:1, :] = jnp.sum(df_ref[...].astype(jnp.float32), axis=0, keepdims=True)


def attn_bwd(core, length, joined, do, do_other, lse, before):
    L = joined.shape[0]
    pairs = joined.shape[1] // 384
    QB = L // 2
    block = lambda at: pl.BlockSpec((QB, 128), lambda p, i, c: (i, at * pairs + p))
    whole = lambda at: pl.BlockSpec((L, 128), lambda p, i, c: (0, at * pairs + p))
    return pl.pallas_call(
        attn_bwd_kernel,
        grid_spec=pltpu.PrefetchScalarGridSpec(
            num_scalar_prefetch=1,
            grid=(pairs, 2),
            in_specs=[
                pl.BlockSpec(memory_space=pltpu.SMEM),
                block(0),
                whole(1),
                whole(2),
                pl.BlockSpec((QB, 128), lambda p, i, c: (0, c[0] * pairs + p)),
                pl.BlockSpec((QB, 128), lambda p, i, c: (0, p)),
                pl.BlockSpec((1, 2, QB), lambda p, i, c: (p, 0, i)),
            ]
            + [pl.BlockSpec(memory_space=pl.ANY)] * len(before),
            out_specs=[
                pl.BlockSpec((L, 384), lambda p, i, c: (0, p)),
                pl.BlockSpec((8, 384), lambda p, i, c: (0, p)),
            ],
            scratch_shapes=[
                pltpu.VMEM((128, L), jnp.bfloat16),
                pltpu.VMEM((L, 128), jnp.float32),
                pltpu.VMEM((L, 128), jnp.float32),
            ],
        ),
        out_shape=[
            jax.ShapeDtypeStruct((L, pairs * 384), jnp.bfloat16),
            jax.ShapeDtypeStruct((8, pairs * 384), jnp.float32),
        ],
        compiler_params=pltpu.CompilerParams(vmem_limit_bytes=20 * 2**20),
        cost_estimate=cost(22.0),
        name="attn_bwd",
    )(core, length, joined, joined, joined, do, do_other, lse, *before)


TN = (((0,), (0,)), ((), ()))


def gelu_pair(z):
    cdf = 0.5 * (1.0 + lax.erf(z * (0.5**0.5)))
    pdf = jnp.exp(-0.5 * z * z) * ((0.5 / jnp.pi) ** 0.5)
    return z * cdf, cdf + z * pdf

def widen_kernel(core_ref, own_ref, other_ref, mix_own_ref, mix_other_ref, x_ref, rows_ref, w_ref, wb_ref,
                 low_ref, turned_ref, normed_ref, inverse_ref, g_ref, gp_ref, z_ref):
    @pl.when(pl.program_id(0) == 0)
    def _():
        width = x_ref.shape[1]
        branch = dotf(own_ref[...], mix_own_ref[...].reshape(width // 2, width), NN)
        branch += dotf(other_ref[...], mix_other_ref[...].reshape(width // 2, width), NN)
        hidden = x_ref[...].astype(jnp.float32) + (branch + rows_ref[2:3, :])
        centred = hidden - jnp.mean(hidden, axis=1, keepdims=True)
        inverse = lax.rsqrt(jnp.mean(centred * centred, axis=1, keepdims=True) + EPSILON)
        normed = centred * inverse
        normed_ref[...] = normed
        inverse_ref[...] = inverse
        low_ref[...] = (normed * rows_ref[4:5, :] + rows_ref[5:6, :]).astype(jnp.bfloat16)
        turned_ref[...] = low_ref[...].T

    widen_block(low_ref, w_ref, wb_ref, g_ref, gp_ref, z_ref)


def widen_block(low_ref, w_ref, wb_ref, g_ref, gp_ref, z_ref):
    rows = 64
    z_ref[...] = dotf(low_ref[...], w_ref[...].reshape(low_ref.shape[1], -1), NN)

    def step(i, carry):
        at = pl.ds(i * rows, rows)
        value, slope = gelu_pair(z_ref[at, :] + wb_ref[...])
        g_ref[at, :] = value.astype(jnp.bfloat16)
        gp_ref[at, :] = slope
        return carry

    lax.fori_loop(0, z_ref.shape[0] // rows, step, 0)


def widen(core, mixed_own, mixed_other, rest, narrow_rows, inputs, rows_float, widen_bias):
    rows, width = inputs.shape
    chips = rest.shape[0]
    shard = width // chips
    blocks = widen_bias.shape[1] // width
    half = width // 2
    start = narrow_rows // shard
    fixed = lambda shape: pl.BlockSpec(shape, lambda j, c: (0,) * len(shape))
    return pl.pallas_call(
        widen_kernel,
        grid_spec=pltpu.PrefetchScalarGridSpec(
            num_scalar_prefetch=1,
            grid=(blocks,),
            in_specs=[
                pl.BlockSpec((rows, half), lambda j, c: (c[0], 0)),
                pl.BlockSpec((rows, half), lambda j, c: (c[0], 0)),
                pl.BlockSpec((chips // 2, shard, width), lambda j, c: (c[0], start, 0)),
                pl.BlockSpec((chips // 2, shard, width), lambda j, c: (1 - c[0], start, 0)),
                fixed((rows, width)),
                fixed(rows_float.shape),
                pl.BlockSpec((chips, shard, width), lambda j, c: (0, start + 1 + j, 0)),
                pl.BlockSpec((1, width), lambda j, c: (0, j)),
            ],
            out_specs=[
                fixed((rows, width)),
                fixed((width, rows)),
                fixed((rows, width)),
                fixed((rows, 1)),
                pl.BlockSpec((rows, width), lambda j, c: (0, j)),
                pl.BlockSpec((rows, width), lambda j, c: (0, j)),
            ],
            scratch_shapes=[pltpu.VMEM((rows, width), jnp.float32)],
        ),
        out_shape=[
            jax.ShapeDtypeStruct((rows, width), jnp.bfloat16),
            jax.ShapeDtypeStruct((width, rows), jnp.bfloat16),
            jax.ShapeDtypeStruct((rows, width), jnp.float32),
            jax.ShapeDtypeStruct((rows, 1), jnp.float32),
            jax.ShapeDtypeStruct((rows, blocks * width), jnp.bfloat16),
            jax.ShapeDtypeStruct((rows, blocks * width), jnp.float32),
        ],
        compiler_params=pltpu.CompilerParams(vmem_limit_bytes=20 * 2**20),
        cost_estimate=cost(12.5),
        name="widen",
    )(core, mixed_own, mixed_other, rest, rest, inputs, rows_float, rest, widen_bias)


def back_kernel(core_ref, dm_ref, grad_two_ref, normed_ref, inverse_ref, rows_ref, narrow_ref, w_ref, gp_ref,
                mix_ref, *refs, spare):
    (dz_own_ref, dz_other_ref, columns_ref, one_ref, da_ref, da_other_ref, do_ref, do_other_ref, sums_ref,
     acc_ref) = refs[spare:]
    j = pl.program_id(0)
    rows, width = dm_ref.shape
    half = width // 2
    at_other = pl.ds(pl.multiple_of((1 - core_ref[0]) * half, half), half)
    dz = dotf(dm_ref[...], narrow_ref[...].reshape(width, width), NT) * gp_ref[...]
    dz = dz.astype(jnp.bfloat16)
    own_turn = j >= pl.num_programs(0) // 2

    @pl.when(own_turn)
    def _():
        dz_own_ref[...] = dz

    @pl.when(jnp.logical_not(own_turn))
    def _():
        dz_other_ref[...] = dz

    sums = jnp.broadcast_to(jnp.sum(dz.astype(jnp.float32), axis=0, keepdims=True), (128, width)).T
    shard = mix_ref.shape[1]
    chips = columns_ref.shape[0] // shard
    each = width // chips // shard
    lanes = lax.broadcasted_iota(jnp.int32, (shard, 128), 1)
    for chip in range(chips):
        total = jnp.zeros((shard, 128), jnp.float32)
        for k in range(each):
            at = (chip * each + k) * shard
            total = jnp.where(lanes == 8 + k, sums[at : at + shard, :], total)
        columns_ref[chip * shard : (chip + 1) * shard, :] = total
    part = dotf(dz, w_ref[...].reshape(width, -1), NT)

    @pl.when(j == 0)
    def _():
        acc_ref[...] = grad_two_ref[...] + part

    @pl.when(j > 0)
    def _():
        acc_ref[...] += part

    @pl.when(j == pl.num_programs(0) - 1)
    def _():
        first_grad = acc_ref[...]
        normed = normed_ref[...]
        inner = first_grad * rows_ref[4:5, :]
        one = inverse_ref[...] * (
            inner
            - jnp.mean(inner, axis=1, keepdims=True)
            - normed * jnp.mean(inner * normed, axis=1, keepdims=True)
        )
        one_ref[...] = one
        low = one.astype(jnp.bfloat16)
        da_ref[...] = low
        da_other_ref[...] = da_ref[:, at_other]
        do_ref[...] = dotf(low, mix_ref[...].reshape(width, width), NT).astype(jnp.bfloat16)
        do_other_ref[...] = do_ref[:, at_other]
        sums_ref[0:1, :] = jnp.sum(first_grad * normed, axis=0, keepdims=True)
        sums_ref[1:2, :] = jnp.sum(first_grad, axis=0, keepdims=True)
        sums_ref[2:3, :] = jnp.sum(low.astype(jnp.float32), axis=0, keepdims=True)


def back(core, dm, grad_two, normed, inverse, rows_float, rest, narrow_rows, gp, chips, before):
    rows, width = dm.shape
    shard = width // chips
    half = width // 2
    blocks = gp.shape[1] // width
    start = narrow_rows // shard
    at = lambda j, c: (j + (1 - c[0]) * (blocks // 2)) % blocks
    fixed = lambda shape: pl.BlockSpec(shape, lambda j, c: (0,) * len(shape))
    low = lambda shape: jax.ShapeDtypeStruct(shape, jnp.bfloat16)
    return pl.pallas_call(
        functools.partial(back_kernel, spare=len(before)),
        grid_spec=pltpu.PrefetchScalarGridSpec(
            num_scalar_prefetch=1,
            grid=(blocks,),
            in_specs=[
                fixed((rows, width)),
                fixed((rows, width)),
                fixed((rows, width)),
                fixed((rows, 1)),
                fixed(rows_float.shape),
                pl.BlockSpec((width // narrow_rows, narrow_rows, width), lambda j, c: (at(j, c), 0, 0)),
                pl.BlockSpec((chips, shard, width), lambda j, c: (0, start + 1 + at(j, c), 0)),
                pl.BlockSpec((rows, width), lambda j, c: (0, at(j, c))),
                pl.BlockSpec((chips, shard, width), lambda j, c: (0, start, 0)),
            ]
            + [pl.BlockSpec(memory_space=pl.ANY)] * len(before),
            out_specs=[
                pl.BlockSpec((rows, width), lambda j, c: (0, jnp.maximum(j - blocks // 2, 0))),
                pl.BlockSpec((rows, width), lambda j, c: (0, jnp.minimum(j, blocks // 2 - 1))),
                pl.BlockSpec((width // blocks, 128), lambda j, c: (at(j, c), 0)),
                fixed((rows, width)),
                fixed((rows, width)),
                fixed((rows, half)),
                fixed((rows, width)),
                fixed((rows, half)),
                fixed((8, width)),
            ],
            scratch_shapes=[pltpu.VMEM((rows, width), jnp.float32)],
        ),
        out_shape=[
            low((rows, blocks // 2 * width)),
            low((rows, blocks // 2 * width)),
            jax.ShapeDtypeStruct((width, 128), jnp.float32),
            jax.ShapeDtypeStruct((rows, width), jnp.float32),
            low((rows, width)),
            low((rows, half)),
            low((rows, width)),
            low((rows, half)),
            jax.ShapeDtypeStruct((8, width), jnp.float32),
        ],
        compiler_params=pltpu.CompilerParams(vmem_limit_bytes=56 * 2**20),
        cost_estimate=cost(13.8),
        name="back",
    )(core, dm, grad_two, normed, inverse, rows_float, rest, rest, gp, rest, *before)


def tokens_kernel(core_ref, grad_ref, w_ref, one_ref, *refs):
    own_ref, other_ref = refs[-2:]
    half = w_ref.shape[1] // 3

    def part():
        total = 0.0
        for pair in range(half // 128):
            for kind in range(3):
                at = kind * half + pair * 128
                start = pair * 384 + kind * 128
                total += dotf(grad_ref[:, start : start + 128], w_ref[:, at : at + 128], NT)
        return total

    @pl.when(pl.program_id(0) == 0)
    def _():
        other_ref[...] = part()

    @pl.when(pl.program_id(0) == 1)
    def _():
        own_ref[...] = part() + one_ref[...]


def tokens_grad(core, grad, w_own, grad_one, before):
    rows, width = grad_one.shape
    fixed = lambda shape: pl.BlockSpec(shape, lambda i, c: (0,) * len(shape))
    return pl.pallas_call(
        tokens_kernel,
        grid_spec=pltpu.PrefetchScalarGridSpec(
            num_scalar_prefetch=1,
            grid=(2,),
            in_specs=[
                pl.BlockSpec((rows, grad.shape[1]), lambda i, c: (jnp.where(i == 0, 1 - c[0], c[0]), 0)),
                fixed(w_own.shape),
                fixed((rows, width)),
            ]
            + [pl.BlockSpec(memory_space=pl.ANY)] * len(before),
            out_specs=[fixed((rows, width)), fixed((rows, width))],
        ),
        out_shape=[jax.ShapeDtypeStruct((rows, width), jnp.float32)] * 2,
        compiler_params=pltpu.CompilerParams(vmem_limit_bytes=20 * 2**20),
        cost_estimate=cost(100.0),
        name="tokens_grad",
    )(core, grad, w_own, grad_one, *before)


def widen_grad_kernel(own_ref, other_ref, grad_own_ref, grad_other_ref, left_ref, right_ref):
    term = dotf(own_ref[...], grad_own_ref[...], NN) + dotf(other_ref[...], grad_other_ref[...], NN)

    @pl.when(pl.program_id(0) == 0)
    def _():
        left_ref[...] = term.astype(jnp.bfloat16)

    @pl.when(pl.program_id(0) == 1)
    def _():
        right_ref[...] = term.astype(jnp.bfloat16)


def widen_grad(turned, turned_other, grad, grad_other):
    width, rows = turned.shape
    columns = grad.shape[1] // 2
    fixed = lambda shape: pl.BlockSpec(shape, lambda i: (0, 0))
    return pl.pallas_call(
        widen_grad_kernel,
        grid=(2,),
        in_specs=[fixed((width, rows))] * 2 + [pl.BlockSpec((rows, columns), lambda i: (0, i))] * 2,
        out_specs=[fixed((width, columns))] * 2,
        out_shape=[jax.ShapeDtypeStruct((width, columns), jnp.bfloat16)] * 2,
        compiler_params=pltpu.CompilerParams(vmem_limit_bytes=16 * 2**20),
        cost_estimate=cost(4.0),
        name="widen_grad",
    )(turned, turned_other, grad, grad_other)


def last_grad_kernel(core_ref, turned_ref, grad_ref, mixing_ref, grad_sums_ref, first_ref, second_ref, widen_ref,
                     left_ref, right_ref):
    half = mixing_ref.shape[1]
    pairs = grad_ref.shape[1] // 384
    left_ref[:, :half] = mixing_ref[...]
    for pair in range(pairs):
        term = dotf(turned_ref[...], grad_ref[:, pair * 384 : pair * 384 + 384], NN).astype(jnp.bfloat16)
        if pair == 0:
            left_ref[:, half:] = term
        else:
            right_ref[:, pair * 384 - 384 : pair * 384] = term

    def columns(rows):
        place = lax.broadcasted_iota(jnp.int32, (128, rows[0][1].shape[1]), 0)
        total = 0.0
        for at, row in rows:
            total = jnp.where(place == at, row, total)
        return total.T

    small = pl.ds(pairs * 384 - 384, 128)
    given = [(2, first_ref[2:3, :]), (3, second_ref[0:1, :]), (4, first_ref[0:1, :])]
    given += [(5, first_ref[1:2, :]), (6, second_ref[1:2, :]), (7, second_ref[2:3, :])]
    right_ref[:, small] = (columns(given) + widen_ref[...]).astype(jnp.bfloat16)
    sums = grad_sums_ref[0:1, :]
    queries = jnp.concatenate([sums[:, pair * 384 : pair * 384 + 128] for pair in range(pairs)], axis=1)
    values = jnp.concatenate([sums[:, pair * 384 + 256 : pair * 384 + 384] for pair in range(pairs)], axis=1)
    at = pl.ds(pl.multiple_of(core_ref[0] * half, half), half)
    right_ref[at, small] = right_ref[at, small] + columns([(0, queries), (1, values)]).astype(jnp.bfloat16)


def last_grad(core, turned, grad, mixing_term, grad_sums, first_sums, second_sums, widen_columns):
    width = turned.shape[0]
    columns = grad.shape[1]
    whole = pl.BlockSpec(memory_space=pltpu.VMEM)
    return pl.pallas_call(
        last_grad_kernel,
        in_specs=[pl.BlockSpec(memory_space=pltpu.SMEM)] + [whole] * 7,
        out_specs=[whole] * 2,
        out_shape=[
            jax.ShapeDtypeStruct((width, width // 2 + 384), jnp.bfloat16),
            jax.ShapeDtypeStruct((width, columns - 384 + 128), jnp.bfloat16),
        ],
        compiler_params=pltpu.CompilerParams(vmem_limit_bytes=16 * 2**20),
        cost_estimate=cost(4.0),
        name="last_grad",
    )(core, turned, grad, mixing_term, grad_sums, first_sums, second_sums, widen_columns)


def finish_kernel(core_ref, own_ref, other_ref, *refs, half):
    project_ref, mixing_ref, small_ref = refs[-3:]
    for ref, core in ((own_ref, core_ref[0]), (other_ref, 1 - core_ref[0])):
        mixing_ref[:, pl.ds(pl.multiple_of(core * half, half), half)] = ref[:, :half]
        for pair in range(half // 128):
            for kind in range(3):
                start = half + pair * 384 + kind * 128
                to = pl.multiple_of(core * half + (kind * 2 * half + pair * 128), 128)
                project_ref[:, pl.ds(to, 128)] = ref[:, start : start + 128]
    small = own_ref[:, 4 * half :] + other_ref[:, 4 * half :]
    small_ref[...] = small.T


def finish(core, share, other, half, before):
    rows = share.shape[0]
    whole = pl.BlockSpec(memory_space=pltpu.VMEM)
    return pl.pallas_call(
        functools.partial(finish_kernel, half=half),
        in_specs=[pl.BlockSpec(memory_space=pltpu.SMEM)] + [whole] * 2 + [pl.BlockSpec(memory_space=pl.ANY)] * len(before),
        out_specs=[whole] * 3,
        out_shape=[
            jax.ShapeDtypeStruct((rows, 6 * half), jnp.float32),
            jax.ShapeDtypeStruct((rows, 2 * half), jnp.float32),
            jax.ShapeDtypeStruct((128, rows), jnp.float32),
        ],
        compiler_params=pltpu.CompilerParams(vmem_limit_bytes=8 * 2**20),
        cost_estimate=cost(2.0),
        name="finish",
    )(core, share, other, *before)


def narrow_kernel(core_ref, g_ref, w_ref, normed_ref, rows_ref, cot_ref,
                  result_ref, two_ref, dm_ref, dm_own_ref, dm_other_ref, sums_ref, acc_ref):
    j = pl.program_id(0)
    width = w_ref.shape[2]
    half = width // 2
    at_own = pl.ds(pl.multiple_of(core_ref[0] * half, half), half)
    at_other = pl.ds(pl.multiple_of((1 - core_ref[0]) * half, half), half)

    @pl.when(j == 0)
    def _():
        acc_ref[...] = jnp.zeros_like(acc_ref)

    acc_ref[...] += dotf(g_ref[...], w_ref[...].reshape(width, width), NN)

    @pl.when(j == pl.num_programs(0) - 1)
    def _():
        hidden = normed_ref[...] * rows_ref[4:5, :] + rows_ref[5:6, :] + (acc_ref[...] + rows_ref[3:4, :])
        centred = hidden - jnp.mean(hidden, axis=1, keepdims=True)
        inverse = lax.rsqrt(jnp.mean(centred * centred, axis=1, keepdims=True) + EPSILON)
        normed = centred * inverse
        result_ref[...] = (normed * rows_ref[6:7, :] + rows_ref[7:8, :]).astype(jnp.bfloat16)
        cot = cot_ref[...].astype(jnp.float32)
        inner = cot * rows_ref[6:7, :]
        two = inverse * (
            inner
            - jnp.mean(inner, axis=1, keepdims=True)
            - normed * jnp.mean(inner * normed, axis=1, keepdims=True)
        )
        two_ref[...] = two
        dm = two.astype(jnp.bfloat16)
        dm_ref[...] = dm
        dm_own_ref[...] = dm_ref[:, at_own]
        dm_other_ref[...] = dm_ref[:, at_other]
        sums_ref[0:1, :] = jnp.sum(dm.astype(jnp.float32), axis=0, keepdims=True)
        sums_ref[1:2, :] = jnp.sum(cot * normed, axis=0, keepdims=True)
        sums_ref[2:3, :] = jnp.sum(cot, axis=0, keepdims=True)


def narrow(core, g, rest, narrow_rows, normed, rows_float, cotangent):
    rows, width = normed.shape
    half = width // 2
    fixed = lambda shape: pl.BlockSpec(shape, lambda j, c: (0,) * len(shape))
    return pl.pallas_call(
        narrow_kernel,
        grid_spec=pltpu.PrefetchScalarGridSpec(
            num_scalar_prefetch=1,
            grid=(g.shape[1] // width,),
            in_specs=[
                pl.BlockSpec((rows, width), lambda j, c: (0, j)),
                pl.BlockSpec((width // narrow_rows, narrow_rows, width), lambda j, c: (j, 0, 0)),
                fixed((rows, width)),
                fixed(rows_float.shape),
                fixed((rows, width)),
            ],
            out_specs=[
                fixed((rows, width)),
                fixed((rows, width)),
                fixed((rows, width)),
                fixed((rows, half)),
                fixed((rows, half)),
                fixed((8, width)),
            ],
            scratch_shapes=[pltpu.VMEM((rows, width), jnp.float32)],
        ),
        out_shape=[
            jax.ShapeDtypeStruct((rows, width), jnp.bfloat16),
            jax.ShapeDtypeStruct((rows, width), jnp.float32),
            jax.ShapeDtypeStruct((rows, width), jnp.bfloat16),
            jax.ShapeDtypeStruct((rows, half), jnp.bfloat16),
            jax.ShapeDtypeStruct((rows, half), jnp.bfloat16),
            jax.ShapeDtypeStruct((8, width), jnp.float32),
        ],
        compiler_params=pltpu.CompilerParams(vmem_limit_bytes=20 * 2**20),
        cost_estimate=cost(8.0),
        name="narrow",
    )(core, g, rest, normed, rows_float, cotangent)


def narrow_grad_kernel(own_ref, other_ref, dm_own_ref, dm_other_ref, out_ref):
    term = dotf(own_ref[...], dm_own_ref[...], TN) + dotf(other_ref[...], dm_other_ref[...], TN)
    out_ref[...] = term.reshape(out_ref.shape).astype(jnp.bfloat16)


def narrow_grad(g, g_other, dm_own, dm_other, chips):
    rows, hidden = g.shape
    half = dm_own.shape[1]
    lines = chips // 4
    size = hidden // lines
    fixed = lambda shape: pl.BlockSpec(shape, lambda j: (0, 0))
    return pl.pallas_call(
        narrow_grad_kernel,
        grid=(lines,),
        in_specs=[pl.BlockSpec((rows, size), lambda j: (0, j))] * 2 + [fixed((rows, half))] * 2,
        out_specs=pl.BlockSpec((4, 1, size // 4, half), lambda j: (0, j, 0, 0)),
        out_shape=jax.ShapeDtypeStruct((4, lines, size // 4, half), jnp.bfloat16),
        compiler_params=pltpu.CompilerParams(vmem_limit_bytes=12 * 2**20),
        cost_estimate=cost(4.5),
        name="narrow_grad",
    )(g, g_other, dm_own, dm_other)


def mixing_grad_kernel(core_ref, own_ref, other_ref, grad_ref, grad_other_ref, *refs):
    out_ref = refs[-1]
    rows, half = grad_other_ref.shape
    core = core_ref[0]
    here = pl.ds(pl.multiple_of(core * rows, rows), rows)
    there = pl.ds(pl.multiple_of((1 - core) * rows, rows), rows)
    at_own = pl.ds(pl.multiple_of(core * half, half), half)
    at_other = pl.ds(pl.multiple_of((1 - core) * half, half), half)
    grad = grad_ref[:, at_own]
    grad_other = grad_other_ref[...]
    for ref, at in ((own_ref, at_own), (other_ref, at_other)):
        term = dotf(ref[here, :], grad, TN) + dotf(ref[there, :], grad_other, TN)
        out_ref[at, :] = term.astype(jnp.bfloat16)


def mixing_grad(core, mixed_own, mixed_other, grad, grad_other):
    width = grad.shape[1]
    whole = pl.BlockSpec(memory_space=pltpu.VMEM)
    return pl.pallas_call(
        mixing_grad_kernel,
        in_specs=[pl.BlockSpec(memory_space=pltpu.SMEM)] + [whole] * 4,
        out_specs=whole,
        out_shape=jax.ShapeDtypeStruct((width, width // 2), jnp.bfloat16),
        compiler_params=pltpu.CompilerParams(vmem_limit_bytes=12 * 2**20),
        cost_estimate=cost(2.0),
        name="mixing_grad",
    )(core, mixed_own, mixed_other, grad, grad_other)


def qkv_kernel(place_ref, x_ref, left_ref, left_other_ref, right_ref, right_other_ref, joined_ref, w_ref, rows_ref,
               small_ref, *, small_at, far):
    core = place_ref[0]
    y = place_ref[far + 1]
    x = place_ref[far + 2]
    shard, cut = left_ref.shape[-2:]
    lines = left_ref.shape[0]
    for line in range(lines):
        for ref, bit in ((left_ref, y), (left_other_ref, 1 - y)):
            to = pl.multiple_of((line * 4 + bit * 2) * shard, 2 * shard)
            w_ref[pl.ds(to, 2 * shard), :cut] = ref[line].reshape(2 * shard, cut)
        for ref, bit in ((right_ref, x), (right_other_ref, 1 - x)):
            for row in range(2):
                to = pl.multiple_of((line * 4 + row * 2 + bit) * shard, shard)
                w_ref[pl.ds(to, shard), cut:] = ref[line, row, :, :small_at]
                small_ref[pl.ds(to, shard), :] = ref[line, row, :, small_at:].astype(jnp.float32)
    rows_ref[...] = small_ref[...].T[: rows_ref.shape[0]]
    half = w_ref.shape[1] // 3
    at = pl.ds(pl.multiple_of(core * half, half), half)
    product = dotf(x_ref[...], w_ref[...], NN)
    joined_ref[:, :half] = (product[:, :half] + rows_ref[0:1, at]).astype(jnp.bfloat16)
    joined_ref[:, half : 2 * half] = product[:, half : 2 * half].astype(jnp.bfloat16)
    joined_ref[:, 2 * half :] = (product[:, 2 * half :] + rows_ref[1:2, at]).astype(jnp.bfloat16)


def qkv(place, inputs, left, left_other, right, right_other, small_at):
    shard, cut = left.shape[-2:]
    length, width = inputs.shape
    far = left.ndim - 4
    lines = 2**far
    left, left_other = left.reshape(lines, 2, shard, cut), left_other.reshape(lines, 2, shard, cut)
    right, right_other = right.reshape(lines, 2, shard, cut), right_other.reshape(lines, 2, shard, cut)
    whole = pl.BlockSpec(memory_space=pltpu.VMEM)
    return pl.pallas_call(
        functools.partial(qkv_kernel, small_at=small_at, far=far),
        in_specs=[pl.BlockSpec(memory_space=pltpu.SMEM)] + [whole] * 5,
        out_specs=[whole] * 3,
        out_shape=[
            jax.ShapeDtypeStruct((length, cut + small_at), jnp.bfloat16),
            jax.ShapeDtypeStruct((width, cut + small_at), jnp.bfloat16),
            jax.ShapeDtypeStruct((16, width), jnp.float32),
        ],
        scratch_shapes=[pltpu.VMEM((width, 128), jnp.float32)],
        compiler_params=pltpu.CompilerParams(vmem_limit_bytes=16 * 2**20),
        cost_estimate=cost(4.0),
        name="qkv",
    )(place, inputs, left, left_other, right, right_other)


def pack_rest_kernel(core_ref, narrow_ref, mixing_ref, widen_ref, rest_ref):
    core = core_ref[0]
    shard, width = mixing_ref.shape
    split = rest_ref.shape[0] - narrow_ref.shape[0]
    blocks = widen_ref.shape[1] // width

    @pl.when(core == 0)
    def _():
        rest_ref[: narrow_ref.shape[0]] = narrow_ref[...]
        rest_ref[narrow_ref.shape[0] :] = mixing_ref[:split]

    @pl.when(core == 1)
    def _():
        rest_ref[: shard - split] = mixing_ref[split:]
        for block in range(blocks):
            at = shard - split + block * shard
            rest_ref[at : at + shard] = widen_ref[:, block * width : (block + 1) * width]
        at = shard - split + blocks * shard
        if at < rest_ref.shape[0]:
            rest_ref[at:] = jnp.zeros((rest_ref.shape[0] - at, width), jnp.bfloat16)


def pack_rest(core, narrowing, mixing, widening):
    shard, width = mixing.shape
    rows = narrowing.shape[0] + shard + widening.shape[1] // width * shard
    half_rows = -(-rows // 32) * 16
    whole = pl.BlockSpec(memory_space=pltpu.VMEM)
    return pl.pallas_call(
        pack_rest_kernel,
        in_specs=[pl.BlockSpec(memory_space=pltpu.SMEM)] + [whole] * 3,
        out_specs=whole,
        out_shape=jax.ShapeDtypeStruct((half_rows, width), jnp.bfloat16),
        compiler_params=pltpu.CompilerParams(vmem_limit_bytes=60 * 2**20),
        cost_estimate=cost(2.0),
        name="pack_rest",
    )(core, narrowing, mixing, widening)


def pack_kernel(core_ref, project_ref, biases_ref, norms_ref, hidden_ref, packed_ref):
    core = core_ref[0]
    shard = packed_ref.shape[0]
    half = project_ref.shape[1] // 6
    for kind in range(3):
        from_ = pl.ds(pl.multiple_of(core * half + kind * 2 * half, half), half)
        packed_ref[:, kind * half : (kind + 1) * half] = project_ref[:, from_]
    place = lax.broadcasted_iota(jnp.int32, (128, shard), 0)
    total = jnp.zeros((128, shard), jnp.float32)
    at = 0
    for ref in (biases_ref, norms_ref, hidden_ref):
        for row in range(ref.shape[0]):
            total = jnp.where(place == at, ref[row : row + 1, :].astype(jnp.float32), total)
            at += 1
    packed_ref[:, 3 * half :] = total.T.astype(jnp.bfloat16)


def pack(core, projection, biases, norms, hidden):
    shard = projection.shape[0]
    whole = pl.BlockSpec(memory_space=pltpu.VMEM)
    return pl.pallas_call(
        pack_kernel,
        in_specs=[pl.BlockSpec(memory_space=pltpu.SMEM)] + [whole] * 4,
        out_specs=whole,
        out_shape=jax.ShapeDtypeStruct((shard, projection.shape[1] // 2 + 128), jnp.bfloat16),
        compiler_params=pltpu.CompilerParams(vmem_limit_bytes=60 * 2**20),
        cost_estimate=cost(2.0),
        name="pack",
    )(core, projection, biases, norms, hidden)


AXES = ("fsdp", "ctx")


def core_permute(value, chips):
    pairs = [(2 * f + c, 2 * f + 1 - c) for f in range(chips) for c in range(2)]
    return lax.ppermute(value, AXES, pairs)


def chip_permute(value, chips, mask):
    pairs = [(2 * f + c, 2 * (f ^ mask) + c) for f in range(chips) for c in range(2)]
    return lax.ppermute(value, AXES, pairs)


def chip_bit(mask):
    return (lax.axis_index("fsdp") // mask) % 2


def by_core(mine, other, axis):
    core = lax.axis_index("ctx")
    first = jnp.where(core == 0, mine, other)
    second = jnp.where(core == 0, other, mine)
    return jnp.concatenate([first, second], axis=axis)


def dims_of(chips):
    return [1 << b for b in reversed(range(chips.bit_length() - 1))]


def gather_step(value, chips, mask):
    axis = dims_of(chips).index(mask)
    other = chip_permute(value, chips, mask)
    bit = chip_bit(mask)
    first = jnp.where(bit == 0, value, other)
    second = jnp.where(bit == 0, other, value)
    return jnp.concatenate([first, second], axis=axis)


def bits_of(chips):
    return jnp.stack([chip_bit(mask) for mask in dims_of(chips)])


def first_send(value, chips, mask):
    shape = [chips // (2 * mask), 2, mask] + list(value.shape[1:])
    send = lax.dynamic_index_in_dim(value.reshape(shape), 1 - chip_bit(mask), 1, keepdims=False)
    return send.reshape(chips // 2, *value.shape[1:])


def block_at(step, left, free, fixed):
    index = 0
    for place, mask in enumerate(left):
        if mask in fixed:
            bit = fixed[mask]
        else:
            bit = (step // 2 ** (len(free) - 1 - free.index(mask))) % 2
        index = index + bit * 2 ** (len(left) - 1 - place)
    return index


def hop_kernel(bits_ref, *refs, parts, merged, spare):
    outs = refs[4 * parts + spare :]
    at = 0
    for part in range(parts):
        away, away_in, keep, keep_in = refs[4 * part : 4 * part + 4]
        columns = away.shape[2]
        send_ref, keep_ref = outs[:2] if merged else outs[2 * part : 2 * part + 2]
        where = pl.ds(at, columns)
        send_ref[:, :, where] = (away[...].astype(jnp.float32) + away_in[...].astype(jnp.float32)).astype(jnp.bfloat16)
        keep_ref[:, :, where] = keep[...].astype(jnp.float32) + keep_in[...].astype(jnp.float32)
        if merged:
            at += columns


def hop(parts, bits, chips, before, merged):
    masks = dims_of(chips)
    in_specs, operands, out_columns = [], [], []
    steps = 2 ** (len([mask for mask in parts[0][2] if mask != parts[0][3]]) - 1)
    for value, arrived, left, came, goes in parts:
        rows, columns = value.shape[1:]
        rest = [mask for mask in left if mask != came]
        free = [mask for mask in rest if mask != goes]
        block = (1, rows, columns)
        for flip in (1, 0):
            def at_value(i, b, left=left, free=free, came=came, goes=goes, flip=flip):
                mine = b[masks.index(goes)]
                side = 1 - mine if flip else mine
                return block_at(i, left, free, {came: b[masks.index(came)], goes: side}), 0, 0

            def at_arrived(i, b, rest=rest, free=free, goes=goes, flip=flip):
                mine = b[masks.index(goes)]
                return block_at(i, rest, free, {goes: 1 - mine if flip else mine}), 0, 0

            in_specs += [pl.BlockSpec(block, at_value), pl.BlockSpec(block, at_arrived)]
            operands += [value, arrived]
        out_columns.append(columns)
    if merged:
        out_columns = [sum(out_columns)]
    out_specs, out_shape = [], []
    for columns in out_columns:
        out_specs += [pl.BlockSpec((1, rows, columns), lambda i, b: (i, 0, 0))] * 2
        out_shape += [
            jax.ShapeDtypeStruct((steps, rows, columns), jnp.bfloat16),
            jax.ShapeDtypeStruct((steps, rows, columns), jnp.float32),
        ]
    outs = pl.pallas_call(
        functools.partial(hop_kernel, parts=len(parts), merged=merged, spare=len(before)),
        grid_spec=pltpu.PrefetchScalarGridSpec(
            num_scalar_prefetch=1,
            grid=(steps,),
            in_specs=in_specs + [pl.BlockSpec(memory_space=pl.ANY)] * len(before),
            out_specs=out_specs,
        ),
        out_shape=out_shape,
        compiler_params=pltpu.CompilerParams(vmem_limit_bytes=8 * 2**20),
        cost_estimate=cost(2.0),
        name="hop",
    )(bits, *operands, *before)
    return list(outs[0::2]), list(outs[1::2])


class Chain:
    def __init__(self, values, chips, bits):
        self.chips, self.bits, self.masks = chips, bits, dims_of(chips)
        self.far = self.masks[:-2]
        self.order = ([1, 2], [2, 1])
        self.kept = values
        self.sent = [first_send(part, chips, order[0]) for part, order in zip(self.kept, self.order)]

    def move(self, masks):
        self.arrived = [chip_permute(part, self.chips, mask) for part, mask in zip(self.sent, masks)]

    def first(self):
        self.move([1, 2])

    def second(self, before):
        self.sent, self.kept = hop(
            [
                (kept, arrived, self.masks, order[0], order[1])
                for kept, arrived, order in zip(self.kept, self.arrived, self.order)
            ],
            self.bits, self.chips, before, False,
        )
        self.move([2, 1])

    def third(self, before, others=()):
        parts = [
            (kept, arrived, self.far, order[1], self.far[-1])
            for chain in (self, *others)
            for kept, arrived, order in zip(chain.kept, chain.arrived, chain.order)
        ]
        self.sent, self.kept = hop(parts, self.bits, self.chips, before, True)
        self.move([self.far[-1]])

    def fourth(self, before):
        for at in range(len(self.far) - 1, 0, -1):
            part = (self.kept[0], self.arrived[0], self.far[:at], self.far[at], self.far[at - 1])
            self.sent, self.kept = hop([part], self.bits, self.chips, before, True)
            self.move([self.far[at - 1]])

    def last(self):
        return self.kept[0][0] + self.arrived[0][0].astype(jnp.float32)


def groups_of(chips):
    near = [list(range(at, at + 4)) for at in range(0, chips, 4)]
    far = [list(range(at, chips, 4)) for at in range(4)]
    return near, far


def core_half(value, axis, own):
    core = lax.axis_index("ctx")
    size = value.shape[axis] // 2
    which = core if own else 1 - core
    return lax.dynamic_slice_in_dim(value, which * size, size, axis)


def fast_body(
    tokens, lengths, cotangent, projection, mixing, widening, narrowing, biases, widen_bias, norms
):
    chips = lax.axis_size("fsdp")
    core = lax.axis_index("ctx")
    core_at = core.reshape(1)
    bits = dims_of(chips)
    far = bits[:-2]
    down_x = [1, 2] + far[::-1]
    down_y = [2, 1] + far[::-1]
    inputs = tokens[0]
    row_count, model_width = inputs.shape
    shard = projection.shape[0]
    half = model_width // 2
    swap = lambda value: core_permute(value, chips)

    hidden = widen_bias.shape[0] // shard
    rest = pack_rest(core_at, narrowing, mixing, widening)
    packed = pack(core_at, projection, biases, norms, widen_bias.reshape(hidden, shard))
    rest = lax.all_gather(rest, AXES, axis=0, tiled=True).reshape(chips, -1, model_width)
    packed = packed.reshape([1] * len(bits) + [shard, packed.shape[1]])
    cut = packed.shape[-1] // 2
    for mask in far:
        packed = gather_step(packed, chips, mask)
    left = gather_step(packed[..., :cut], chips, 1)
    right = gather_step(packed[..., cut:], chips, 2)
    left_other = chip_permute(left, chips, 2)
    right_other = chip_permute(right, chips, 1)

    narrow_rows = narrowing.shape[0]

    all_inputs = by_core(inputs, swap(inputs), 0)
    inputs_turned = all_inputs.T
    chip_bits = bits_of(chips)
    small_at = 3 * half - cut
    joined, w_own, rows_float = qkv(
        jnp.concatenate([core_at, chip_bits]), all_inputs, left, left_other, right, right_other, small_at
    )
    widen_float = rows_float[8 : 8 + hidden].reshape(hidden, chips, shard).transpose(1, 0, 2).reshape(1, -1)
    mixed_own, logsum = attn_fwd(lengths, joined, [inputs_turned])
    mixed_other = swap(mixed_own)
    first_low, first_turned, normed_one, inverse_one, active_low, slope = widen(
        core_at, mixed_own, mixed_other, rest, narrow_rows, inputs, rows_float, widen_float
    )
    first_other = swap(first_turned)
    active_other = swap(active_low)
    result, grad_two, second_grad, dm_own, dm_other, second_sums = narrow(
        core_at, active_low, rest, narrow_rows, normed_one, rows_float, cotangent[0]
    )

    near, line = groups_of(chips)
    narrow_term = narrow_grad(active_low, active_other, dm_own, swap(dm_other), chips)
    narrow_near = lax.psum_scatter(
        narrow_term, "fsdp", scatter_dimension=0, axis_index_groups=near, tiled=True
    ).reshape(chips // 4, narrow_rows, half)

    (
        expand_own, expand_other, widen_columns, grad_one, branch_grad, branch_other, mixed_grad, mixed_other_grad,
        first_sums,
    ) = back(
        core_at, second_grad, grad_two, normed_one, inverse_one, rows_float,
        rest, narrow_rows, slope, chips, [narrow_term],
    )
    mixed_grad_other = swap(mixed_other_grad)
    branch_other = swap(branch_other)
    widen_terms_two = widen_grad(first_turned, first_other, expand_own, swap(expand_other))
    widen_chain = Chain([term.reshape(chips, shard, -1) for term in widen_terms_two], chips, chip_bits)
    widen_chain.first()

    mixing_term = mixing_grad(core_at, mixed_own, mixed_other, branch_grad, branch_other)

    grad, grad_sums = attn_bwd(
        core_at, lengths, joined, mixed_grad, mixed_grad_other, logsum, widen_chain.sent + [mixing_term]
    )
    narrow_share = lax.psum_scatter(
        narrow_near, "fsdp", scatter_dimension=0, axis_index_groups=line, tiled=True
    )[0].astype(jnp.float32)
    last_terms = last_grad(
        core_at, inputs_turned, grad, mixing_term, grad_sums, first_sums, second_sums, widen_columns
    )
    last_chain = Chain([term.reshape(chips, shard, -1) for term in last_terms], chips, chip_bits)
    last_chain.first()
    widen_chain.second([grad, narrow_near] + last_chain.sent)
    own_part, other_part = tokens_grad(core_at, grad, w_own, grad_one, last_chain.sent + [narrow_share])
    last_chain.second(widen_chain.sent)
    widen_chain.third(last_chain.sent)
    last_chain.third(widen_chain.sent)
    input_grad = own_part + swap(other_part)
    widen_chain.fourth(last_chain.sent)
    last_chain.fourth(widen_chain.sent)
    join = lambda share: by_core(share, swap(share), 1)
    widen_share = join(widen_chain.last())
    narrow_share = join(narrow_share)
    last_share = last_chain.last()
    other_share = swap(last_share)

    grad_projection, grad_mixing, small_share = finish(
        core_at, last_share, other_share, half, [widen_share, narrow_share, input_grad]
    )
    return (
        result.astype(jnp.bfloat16)[None],
        input_grad[None],
        grad_projection,
        grad_mixing,
        widen_share,
        narrow_share,
        small_share[:4],
        small_share[8 : 8 + hidden].reshape(-1),
        small_share[4:8],
    )


def solution(mesh):
    in_specs = (
        P("fsdp", "ctx", None),
        P("fsdp"),
        P("fsdp", "ctx", None),
        P("fsdp", None),
        P("fsdp", None),
        P("fsdp", None),
        P("fsdp", None),
        P(None, "fsdp"),
        P("fsdp"),
        P(None, "fsdp"),
    )
    out_specs = (
        P("fsdp", "ctx", None),
        P("fsdp", "ctx", None),
        P("fsdp", None),
        P("fsdp", None),
        P("fsdp", None),
        P("fsdp", None),
        P(None, "fsdp"),
        P("fsdp"),
        P(None, "fsdp"),
    )
    chips = mesh.shape["fsdp"]
    paired = mesh.shape["ctx"] == 2 and chips >= 4 and chips & (chips - 1) == 0
    body = fast_body if paired else general_body
    return jax.shard_map(body, mesh=mesh, in_specs=in_specs, out_specs=out_specs, check_vma=False)
```
